32 devices in a mesh: ctx: 8 (over z, x), head: 4 (over y, core).
Axes of the slice: x: 2, y: 2, z: 4, core: 2. Of those that a mesh axis runs over, the one named last changes fastest.
Arguments:
- queries: bfloat16 [16384, 4096], P('ctx', 'head'), may hold values from -28 to 28
- keys: bfloat16 [16384, 1024], P('ctx', 'head'), may hold values from -13 to 13
- values: bfloat16 [16384, 1024], P('ctx', 'head'), may hold values from -6 to 6
- vertical: int32 [8, 16], P('head'), may hold values from 0 to 255, as said below
- slash: int32 [8, 8], P('head'), may hold values from 0 to 63, as said below
Outputs:
- attention: bfloat16 [16384, 4096], P(('ctx', 'head'))
The draws below stay inside these ranges and needn't reach their ends.
Inputs may be any that keep to these rules, and one draw needn't show every extreme that they name: `vertical`: each row lists 16 different blocks; at most 4 of one row lie within one index of ctx (2048 tokens), and exactly 4 do in some index. `slash`: each row lists 8 different offsets, 0 and 2 * 32 - 1 among them.
All inputs are finite; a program needn't handle non-finite values.
Results may differ from the reference program's by a relative error of at most 0.0043.
Values may be sent and summed in bfloat16 or wider, within the bound.
No kernel may reach another device: no remote copies, remote signals or barrier semaphores. Data moves between devices by JAX's collectives and lax.ppermute only.
A program may use at most 64 MiB of HBM per device.

```python
import math
import jax
import jax.numpy as jnp
from jax import lax

HD = 128
KVH = 8
QH = 32
BLK = 64
TOK_DEV = 2048
NV = 16
NS = 8
MOWN = 4
LOOK = 2
HQ = 4
TOKENS = 16384
N_CTX = 8


def shared_draw(key):
    query_draw = jnp.clip(jax.random.normal(jax.random.fold_in(key, 101), (TOKENS, KVH, HQ, HD), jnp.float32), -5.0, 5.0)
    key_draw = jnp.clip(jax.random.normal(jax.random.fold_in(key, 102), (TOKENS, KVH, HD), jnp.float32), -5.0, 5.0)
    return (query_draw.reshape(TOKENS, KVH * HQ * HD), key_draw.reshape(TOKENS, KVH * HD))


def draw_queries(key, part):
    return shared_draw(key)[0].astype(jnp.bfloat16)


def draw_keys(key, part):
    return shared_draw(key)[1].astype(jnp.bfloat16)


def draw_vertical(key, part):
    blocks_dev = TOK_DEV // BLK
    heavy = jax.random.randint(jax.random.fold_in(key, 11), (KVH,), 0, N_CTX)

    def one_head(head_key, heavy_shard):
        heavy_local = jax.random.permutation(jax.random.fold_in(head_key, 1), blocks_dev)[:MOWN]
        heavy_blocks = heavy_shard * blocks_dev + heavy_local
        others = jax.random.permutation(jax.random.fold_in(head_key, 2), N_CTX - 1)
        spread = jax.random.permutation(jax.random.fold_in(head_key, 3), blocks_dev)
        positions = jnp.arange(NV - MOWN)
        shard_ids = (heavy_shard + 1 + others[positions % (N_CTX - 1)]) % N_CTX
        local_ids = spread[positions // (N_CTX - 1)]
        light_blocks = shard_ids * blocks_dev + local_ids
        listed = jnp.concatenate([heavy_blocks, light_blocks])
        return listed[jax.random.permutation(jax.random.fold_in(head_key, 4), NV)]
    head_keys = jax.random.split(jax.random.fold_in(key, 12), KVH)
    return jax.vmap(one_head)(head_keys, heavy).astype(jnp.int32)


def draw_slash(key, part):
    span_blocks = LOOK * (TOK_DEV // BLK)

    def one_head(head_key):
        middle = jax.random.permutation(head_key, span_blocks - 2)[:NS - 2] + 1
        return jnp.concatenate([jnp.zeros((1,), jnp.int32), jnp.full((1,), span_blocks - 1, jnp.int32), middle.astype(jnp.int32)])
    head_keys = jax.random.split(jax.random.fold_in(key, 21), KVH)
    return jax.vmap(one_head)(head_keys).astype(jnp.int32)


def levels(stream_key, shape, pieces, low, largest):
    def one(axis_at, parts):
        draws = jax.random.uniform(jax.random.fold_in(jax.random.fold_in(stream_key, 6), axis_at), (parts,), jnp.float32, low / len(pieces), largest / len(pieces))
        return jnp.repeat(jnp.exp(draws), shape[axis_at] // parts).reshape((-1,) + (1,) * (len(shape) - axis_at - 1))

    loudness = one(*pieces[0])
    for cut in pieces[1:]:
        loudness = loudness * one(*cut)
    return loudness


def normal_values(key, dims, scale, limit, pieces=(), kind=jnp.bfloat16):
    values = jax.random.normal(key, dims, jnp.float32) * scale
    if len(pieces) > 0:
        values = levels(key, dims, pieces, -0.22, 0.18) * values
    return jnp.clip(values, min=-limit, max=limit).astype(kind)


def setup_inputs(seed: int = 0) -> dict:
    key_of = jax.random.split(jax.random.key(seed), 6)
    return {
        "queries": draw_queries(jax.random.fold_in(key_of[5], 71), 0),
        "keys": draw_keys(jax.random.fold_in(key_of[5], 71), 0),
        "values": normal_values(key_of[2], (TOKENS, KVH * HD), 1.0, 6.0, ((0, 8), (1, 4))),
        "vertical": draw_vertical(jax.random.fold_in(key_of[5], 71), 0),
        "slash": draw_slash(jax.random.fold_in(key_of[5], 71), 0),
    }


def reference(queries, keys, values, vertical, slash):
    block_count = TOKENS // BLK
    group_heads = QH // KVH
    score_scale = 1.0 / math.sqrt(HD)
    query_blocks = queries.reshape(block_count, BLK, KVH, group_heads, HD)
    key_blocks = keys.reshape(block_count, BLK, KVH, HD)
    value_blocks = values.reshape(block_count, BLK, KVH, HD)
    offsets = jnp.arange(BLK).astype(jnp.int32)

    def attend_head(head_index):
        head_keys = jnp.take(key_blocks, head_index, axis=2)
        head_values = jnp.take(value_blocks, head_index, axis=2)
        head_queries = jnp.take(query_blocks, head_index, axis=2)
        vert_blocks = jnp.take(vertical, head_index, axis=0)
        slash_offsets = jnp.take(slash, head_index, axis=0)
        vert_keys = jnp.take(head_keys, vert_blocks, axis=0).reshape(NV * BLK, HD)
        vert_values = jnp.take(head_values, vert_blocks, axis=0).reshape(NV * BLK, HD)
        vert_pos = (vert_blocks[:, None] * BLK + offsets[None, :]).reshape(NV * BLK)

        def attend_block(block_index):
            query_rows = jnp.take(head_queries, block_index, axis=0)
            query_pos = block_index * BLK + offsets
            slash_blocks = block_index - slash_offsets
            safe_blocks = jnp.maximum(slash_blocks, 0)
            slash_keys = jnp.take(head_keys, safe_blocks, axis=0).reshape(NS * BLK, HD)
            slash_values = jnp.take(head_values, safe_blocks, axis=0).reshape(NS * BLK, HD)
            in_vertical = jnp.any(slash_blocks[:, None] == vert_blocks[None, :], axis=1)
            slash_valid = (slash_blocks >= 0) & jnp.logical_not(in_vertical)
            slash_pos = (slash_blocks[:, None] * BLK + offsets[None, :]).reshape(NS * BLK)
            key_valid = jnp.concatenate([jnp.ones((NV * BLK,), jnp.bool_), jnp.repeat(slash_valid, BLK)])
            key_pos = jnp.concatenate([vert_pos, slash_pos])
            allowed = key_valid[None, :] & (key_pos[None, :] <= query_pos[:, None])
            all_keys = jnp.concatenate([vert_keys, slash_keys]).astype(jnp.float32)
            all_values = jnp.concatenate([vert_values, slash_values]).astype(jnp.float32)
            scores = jnp.einsum('rhd,kd->hrk', query_rows.astype(jnp.float32), all_keys) * score_scale
            scores = jnp.where(allowed[None], scores, -1e+30)
            row_max = lax.optimization_barrier(jnp.max(scores, axis=2, keepdims=True))
            weights = jnp.exp(scores - row_max)
            denominator = lax.optimization_barrier(jnp.sum(weights, axis=2))
            rounded = lax.optimization_barrier(weights.astype(jnp.bfloat16)).astype(jnp.float32)
            weighted = jnp.einsum('hrk,kd->rhd', rounded, all_values)
            return (weighted / denominator.T[:, :, None]).astype(jnp.bfloat16)
        return lax.map(attend_block, jnp.arange(block_count).astype(jnp.int32))
    heads_out = lax.map(attend_head, jnp.arange(KVH).astype(jnp.int32))
    return jnp.transpose(heads_out, (1, 2, 0, 3, 4)).reshape(TOKENS, KVH * group_heads * HD)
```

```python
import functools
import math

import jax
import jax.numpy as jnp
from jax import lax
from jax.experimental import pallas as pl
from jax.experimental.pallas import tpu as pltpu
from jax.sharding import PartitionSpec as P

HD = 128
BLK = 64
NV = 16
NS = 8
MOWN = 4
LOOK = 2
NEG = -1e30
STEP_BLOCKS = 2
CHUNKS = 2


def slots_kernel(local_ref, keys_ref, values_ref, out_ref, sem):
    copies = []
    for head in range(out_ref.shape[0]):
        for slot in range(MOWN):
            rows = pl.ds(pl.multiple_of(local_ref[head, slot] * BLK, BLK), BLK)
            for side, source in enumerate((keys_ref, values_ref)):
                copies.append(
                    pltpu.make_async_copy(
                        source.at[rows, pl.ds(head * HD, HD)],
                        out_ref.at[head, pl.ds(slot * BLK, BLK), pl.ds(side * HD, HD)],
                        sem.at[len(copies)],
                    )
                )
    for copy in copies:
        copy.start()
    for copy in copies:
        copy.wait()


def owned_slots(local_block, keys, values):
    heads = local_block.shape[0]
    return pl.pallas_call(
        slots_kernel,
        out_shape=jax.ShapeDtypeStruct((heads, MOWN * BLK, 2 * HD), keys.dtype),
        in_specs=[
            pl.BlockSpec(memory_space=pltpu.SMEM),
            pl.BlockSpec(memory_space=pl.ANY),
            pl.BlockSpec(memory_space=pl.ANY),
        ],
        out_specs=pl.BlockSpec(memory_space=pl.ANY),
        scratch_shapes=[pltpu.SemaphoreType.DMA((heads * MOWN * 2,))],
        compiler_params=pltpu.CompilerParams(vmem_limit_bytes=1 << 20),
        cost_estimate=pl.CostEstimate(
            flops=0, bytes_accessed=4 * heads * MOWN * BLK * 2 * HD, transcendentals=0
        ),
    )(local_block, keys, values)


def attend_kernel(
    head,
    steps,
    group_heads,
    chunk_blocks,
    part_ref,
    parity_ref,
    slot_ref,
    slash_ref,
    query_ref,
    bias_ref,
    own_ref,
    *rest,
):
    two_back = rest[:CHUNKS]
    even_back = rest[CHUNKS : 2 * CHUNKS]
    odd_back, gathered_ref, out_ref, vert, slash, vert_sem, slash_sem = rest[2 * CHUNKS :]
    blocks_dev = own_ref.shape[0] // BLK
    step = pl.program_id(0)
    part = part_ref[0]
    parity = parity_ref[0]

    def block_index(at_step, at):
        return (part * steps + at_step) * STEP_BLOCKS + at

    def fetch(at_step):
        buffer = lax.rem(at_step, 2)
        for at in range(STEP_BLOCKS):
            for entry in range(NS):
                source = block_index(at_step, at) - slash_ref[head, entry]
                target = slash.at[buffer, at, pl.ds(entry * BLK, BLK)]
                sem = slash_sem.at[buffer]

                def rows(first):
                    return pl.ds(pl.multiple_of(first * BLK, BLK), BLK)

                @pl.when(source >= 0)
                def _():
                    pltpu.make_async_copy(own_ref.at[rows(source)], target, sem).start()

                @pl.when((source < 0) & (source >= -blocks_dev) & (parity == 1))
                def _():
                    pltpu.make_async_copy(
                        odd_back.at[rows(source + blocks_dev)], target, sem
                    ).start()

                for chunk in range(CHUNKS):
                    low = chunk * chunk_blocks
                    first = source + blocks_dev - low

                    @pl.when((first >= 0) & (first < chunk_blocks) & (source < 0) & (parity == 0))
                    def _():
                        pltpu.make_async_copy(
                            even_back[chunk].at[rows(first)], target, sem
                        ).start()

                    second = source + 2 * blocks_dev - low

                    @pl.when((second >= 0) & (second < chunk_blocks))
                    def _():
                        pltpu.make_async_copy(
                            two_back[chunk].at[rows(second)], target, sem
                        ).start()

    @pl.when(step == 0)
    def _():
        fetch(0)
        for entry in range(NV):
            pltpu.make_async_copy(
                gathered_ref.at[
                    slot_ref[head, entry] // MOWN,
                    head,
                    pl.ds(pl.multiple_of(lax.rem(slot_ref[head, entry], MOWN) * BLK, BLK), BLK),
                ],
                vert.at[pl.ds(entry * BLK, BLK)],
                vert_sem,
            ).start()
        pltpu.make_async_copy(vert, vert, vert_sem).wait()

    @pl.when(step + 1 < steps)
    def _():
        fetch(step + 1)

    buffer = lax.rem(step, 2)
    here = slash.at[buffer]
    pltpu.make_async_copy(here, here, slash_sem.at[buffer]).wait()

    rate = math.log2(math.e) / math.sqrt(HD)
    rows = group_heads * BLK
    row_token = lax.broadcasted_iota(jnp.int32, (rows, 2 * BLK), 0) % BLK
    column = lax.broadcasted_iota(jnp.int32, (rows, 2 * BLK), 1)
    diagonal = jnp.where((column < BLK) & (column > row_token), NEG, 0.0).astype(jnp.float32)
    ones_vert = jnp.ones((NV * BLK, HD), jnp.bfloat16)
    ones_slash = jnp.ones((NS * BLK, HD), jnp.bfloat16)
    contract = (((1,), (1,)), ((), ()))
    for at in range(STEP_BLOCKS):
        query = jnp.concatenate(
            [
                query_ref[at * BLK : (at + 1) * BLK, h * HD : (h + 1) * HD]
                for h in range(group_heads)
            ],
            axis=0,
        )
        bias = bias_ref[pl.ds(block_index(step, at), 1), :]
        vert_scores = lax.dot_general(
            query, vert[:, :HD], contract, preferred_element_type=jnp.float32
        )
        slash_scores = lax.dot_general(
            query, slash[buffer, at, :, :HD], contract, preferred_element_type=jnp.float32
        )
        vert_scores = vert_scores + bias[:, : NV * BLK]
        slash_scores = slash_scores + bias[:, NV * BLK :]
        slash_scores = jnp.concatenate(
            [slash_scores[:, : 2 * BLK] + diagonal, slash_scores[:, 2 * BLK :]], axis=1
        )
        row_max = jnp.maximum(
            jnp.max(vert_scores, axis=1, keepdims=True),
            jnp.max(slash_scores, axis=1, keepdims=True),
        )
        vert_weights = jnp.exp2((vert_scores - row_max) * rate).astype(jnp.bfloat16)
        slash_weights = jnp.exp2((slash_scores - row_max) * rate).astype(jnp.bfloat16)
        total = jnp.dot(
            vert_weights,
            jnp.concatenate([vert[:, HD:], ones_vert], axis=1),
            preferred_element_type=jnp.float32,
        ) + jnp.dot(
            slash_weights,
            jnp.concatenate([slash[buffer, at, :, HD:], ones_slash], axis=1),
            preferred_element_type=jnp.float32,
        )
        result = (total[:, :HD] / total[:, HD:]).astype(jnp.bfloat16)
        for h in range(group_heads):
            out_ref[at * BLK : (at + 1) * BLK, h * HD : (h + 1) * HD] = result[
                h * BLK : (h + 1) * BLK
            ]


def attend(head, part, parity, slot_index, slash, queries, bias, own, two_back, even_back, odd_back,
           gathered, part_rows):
    group_cols = queries.shape[1] // slash.shape[0]
    group_heads = group_cols // HD
    step_rows = STEP_BLOCKS * BLK
    steps = part_rows // step_rows
    any_spec = pl.BlockSpec(memory_space=pl.ANY)
    keys_seen = (NV + NS) * BLK
    return pl.pallas_call(
        functools.partial(
            attend_kernel, head, steps, group_heads, two_back[0].shape[0] // BLK
        ),
        out_shape=jax.ShapeDtypeStruct((part_rows, group_cols), jnp.bfloat16),
        grid_spec=pltpu.PrefetchScalarGridSpec(
            num_scalar_prefetch=4,
            grid=(steps,),
            in_specs=[
                pl.BlockSpec(
                    (step_rows, group_cols), lambda s, part, *_: (part[0] * steps + s, head)
                ),
                pl.BlockSpec(bias.shape, lambda s, *_: (0, 0)),
            ]
            + [any_spec] * (3 + 2 * CHUNKS),
            out_specs=pl.BlockSpec((step_rows, group_cols), lambda s, *_: (s, 0)),
            scratch_shapes=[
                pltpu.VMEM((NV * BLK, 2 * HD), jnp.bfloat16),
                pltpu.VMEM((2, STEP_BLOCKS, NS * BLK, 2 * HD), jnp.bfloat16),
                pltpu.SemaphoreType.DMA,
                pltpu.SemaphoreType.DMA((2,)),
            ],
        ),
        compiler_params=pltpu.CompilerParams(
            dimension_semantics=("arbitrary",), vmem_limit_bytes=32 << 20
        ),
        cost_estimate=pl.CostEstimate(
            flops=4 * part_rows * group_heads * keys_seen * HD,
            bytes_accessed=4 * part_rows * group_cols + 16 * keys_seen * HD,
            transcendentals=part_rows * group_heads * keys_seen,
        ),
    )(part, parity, slot_index, slash, queries, bias, own, *two_back, *even_back, odd_back, gathered)


def local(queries, keys, values, vertical, slash):
    shard_count = lax.axis_size("ctx")
    shard_index = lax.axis_index("ctx")
    head_count = lax.axis_size("head")
    head_index = lax.axis_index("head")
    tok_rows = queries.shape[0]
    kv_local = keys.shape[1] // HD
    group_cols = queries.shape[1] // kv_local
    blocks_dev = tok_rows // BLK
    part_rows = tok_rows // head_count

    owners = vertical // blocks_dev
    order = jnp.arange(NV, dtype=jnp.int32)
    same_owner = owners[:, :, None] == owners[:, None, :]
    earlier = order[None, :] < order[:, None]
    slot_rank = jnp.sum((same_owner & earlier[None]).astype(jnp.int32), axis=2)
    slot_index = owners * MOWN + slot_rank
    in_slot = (owners == shard_index)[:, :, None] & (
        slot_rank[:, :, None] == jnp.arange(MOWN, dtype=jnp.int32)
    )
    local_block = jnp.sum(in_slot * (vertical % blocks_dev)[:, :, None], axis=1)
    gathered = lax.all_gather(owned_slots(local_block, keys, values), "ctx")

    slash_rank = jnp.sum((slash[:, None, :] < slash[:, :, None]).astype(jnp.int32), axis=2)
    place = slash_rank[:, :, None] == jnp.arange(NS, dtype=jnp.int32)
    slash = jnp.sum(place * slash[:, :, None], axis=1)

    global_blocks = shard_index * blocks_dev + jnp.arange(blocks_dev, dtype=jnp.int32)
    vert_valid = vertical[:, None, :] < global_blocks[None, :, None]
    slash_blocks = global_blocks[None, :, None] - slash[:, None, :]
    in_vertical = jnp.any(slash_blocks[:, :, :, None] == vertical[:, None, None, :], axis=3)
    slash_valid = (slash[:, None, :] == 0) | ((slash_blocks >= 0) & jnp.logical_not(in_vertical))
    valid = jnp.concatenate([vert_valid, slash_valid], axis=2)
    bias = jnp.repeat(jnp.where(valid, 0.0, NEG).astype(jnp.float32), BLK, axis=2)

    two_pairs = [(i, i + 2) for i in range(shard_count - 2)]
    even_to_odd = [(i, i + 1) for i in range(0, shard_count - 1, 2)]
    odd_to_even = [(i, i - 1) for i in range(1, shard_count, 2)]
    chunk_rows = tok_rows // CHUNKS
    windows = []
    for head in range(kv_local):
        columns = slice(head * HD, (head + 1) * HD)
        own = jnp.concatenate([keys[:, columns], values[:, columns]], axis=1)
        two_back = [
            lax.ppermute(own[c * chunk_rows : (c + 1) * chunk_rows], "ctx", two_pairs)
            for c in range(CHUNKS)
        ]
        odd_back = lax.ppermute(own, "ctx", even_to_odd)
        even_back = [lax.ppermute(piece, "ctx", odd_to_even) for piece in two_back]
        windows.append((own, two_back, even_back, odd_back))

    parity = (shard_index % 2).reshape(1).astype(jnp.int32)
    out = jnp.zeros((part_rows, head_count * kv_local * group_cols), jnp.bfloat16)
    for head in range(kv_local):
        own, two_back, even_back, odd_back = windows[head]
        for flip in range(head_count - 1, -1, -1):
            other = head_index ^ flip
            piece = attend(
                head, other.reshape(1).astype(jnp.int32), parity, slot_index, slash, queries,
                bias[head], own, two_back, even_back, odd_back, gathered, part_rows,
            )
            if flip:
                piece = lax.ppermute(piece, "head", [(i, i ^ flip) for i in range(head_count)])
            out = lax.dynamic_update_slice(
                out, piece, (0, other * kv_local * group_cols + head * group_cols)
            )
    return out


def solution(mesh):
    in_specs = (
        P("ctx", "head"),
        P("ctx", "head"),
        P("ctx", "head"),
        P("head", None),
        P("head", None),
    )
    out_specs = P(("ctx", "head"), None)
    return jax.shard_map(local, mesh=mesh, in_specs=in_specs, out_specs=out_specs, check_vma=False)
```

```python
import functools
import math

import jax
import jax.numpy as jnp
from jax import lax
from jax.experimental import pallas as pl
from jax.experimental.pallas import tpu as pltpu
from jax.sharding import PartitionSpec as P

HD = 128
BLK = 64
NV = 16
NS = 8
MOWN = 4
LOOK = 2
NEG = -1e30
STEP_BLOCKS = 2
CHUNKS = 2
BUFFERS = 4
TILE = 256


def slots_kernel(local_ref, keys_ref, values_ref, out_ref, sem):
    copies = []
    for head in range(out_ref.shape[0]):
        for slot in range(MOWN):
            rows = pl.ds(pl.multiple_of(local_ref[head, slot] * BLK, BLK), BLK)
            for side, source in enumerate((keys_ref, values_ref)):
                copies.append(
                    pltpu.make_async_copy(
                        source.at[rows, pl.ds(head * HD, HD)],
                        out_ref.at[head, pl.ds(slot * BLK, BLK), pl.ds(side * HD, HD)],
                        sem.at[len(copies)],
                    )
                )
    for copy in copies:
        copy.start()
    for copy in copies:
        copy.wait()


def owned_slots(local_block, keys, values):
    heads = local_block.shape[0]
    return pl.pallas_call(
        slots_kernel,
        out_shape=jax.ShapeDtypeStruct((heads, MOWN * BLK, 2 * HD), keys.dtype),
        in_specs=[
            pl.BlockSpec(memory_space=pltpu.SMEM),
            pl.BlockSpec(memory_space=pl.ANY),
            pl.BlockSpec(memory_space=pl.ANY),
        ],
        out_specs=pl.BlockSpec(memory_space=pl.ANY),
        scratch_shapes=[pltpu.SemaphoreType.DMA((heads * MOWN * 2,))],
        compiler_params=pltpu.CompilerParams(vmem_limit_bytes=1 << 20),
        cost_estimate=pl.CostEstimate(
            flops=0, bytes_accessed=4 * heads * MOWN * BLK * 2 * HD, transcendentals=0
        ),
    )(local_block, keys, values)


def attend_kernel(
    head,
    steps,
    group_heads,
    chunk_blocks,
    part_ref,
    parity_ref,
    slot_ref,
    slash_ref,
    query_ref,
    bias_ref,
    own_ref,
    *rest,
):
    two_back = rest[:CHUNKS]
    even_back = rest[CHUNKS : 2 * CHUNKS]
    (
        odd_back, gathered_ref, out_ref, vert, slash, scores_a, scores_b, weights_a, weights_b,
        max_a, max_b, diagonal_ref, vert_sem, slash_sem,
    ) = rest[2 * CHUNKS :]
    scores, weights, maxima = (scores_a, scores_b), (weights_a, weights_b), (max_a, max_b)
    blocks_dev = own_ref.shape[0] // BLK
    step = pl.program_id(0)
    part = part_ref[0]
    parity = parity_ref[0]
    part_blocks = steps * STEP_BLOCKS
    rate = math.log2(math.e) / math.sqrt(HD)
    contract = (((1,), (1,)), ((), ()))

    def fetch(pair):
        buffer = lax.rem(pair, BUFFERS)
        for at in range(STEP_BLOCKS):
            for entry in range(NS):
                source = part * part_blocks + pair * STEP_BLOCKS + at - slash_ref[head, entry]
                target = slash.at[buffer, at, pl.ds(entry * BLK, BLK)]
                sem = slash_sem.at[buffer]

                def rows(first):
                    return pl.ds(pl.multiple_of(first * BLK, BLK), BLK)

                @pl.when(source >= 0)
                def _():
                    pltpu.make_async_copy(own_ref.at[rows(source)], target, sem).start()

                @pl.when((source < 0) & (source >= -blocks_dev) & (parity == 1))
                def _():
                    pltpu.make_async_copy(
                        odd_back.at[rows(source + blocks_dev)], target, sem
                    ).start()

                for chunk in range(CHUNKS):
                    low = chunk * chunk_blocks
                    first = source + blocks_dev - low

                    @pl.when((first >= 0) & (first < chunk_blocks) & (source < 0) & (parity == 0))
                    def _():
                        pltpu.make_async_copy(
                            even_back[chunk].at[rows(first)], target, sem
                        ).start()

                    second = source + 2 * blocks_dev - low

                    @pl.when((second >= 0) & (second < chunk_blocks))
                    def _():
                        pltpu.make_async_copy(
                            two_back[chunk].at[rows(second)], target, sem
                        ).start()

    def arrived(pair):
        here = slash.at[lax.rem(pair, BUFFERS)]
        pltpu.make_async_copy(here, here, slash_sem.at[lax.rem(pair, BUFFERS)]).wait()

    def slash_of(pair, at):
        return slash.at[lax.rem(pair + BUFFERS, BUFFERS), at]

    def query_of(block):
        start = pl.multiple_of(jnp.minimum(block, part_blocks - 1) * BLK, BLK)
        return jnp.concatenate(
            [query_ref[pl.ds(start, BLK), h * HD : (h + 1) * HD] for h in range(group_heads)],
            axis=0,
        )

    def score_tile(query, bias, here, tile):
        low = tile * TILE
        if low < NV * BLK:
            keys = vert[low : low + TILE, :HD]
        else:
            keys = here[low - NV * BLK : low - NV * BLK + TILE, :HD]
        found = lax.dot_general(query, keys, contract, preferred_element_type=jnp.float32)
        found = found + bias[:, low : low + TILE]
        if low == NV * BLK:
            diagonal = jnp.concatenate([diagonal_ref[...]] * group_heads, axis=0)
            found = jnp.concatenate(
                [found[:, : 2 * BLK] + diagonal, found[:, 2 * BLK :]], axis=1
            )
        return found

    def weighted_values(here, at):
        ones = jnp.ones((TILE, HD), jnp.bfloat16)
        values = [
            jnp.concatenate([vert[low : low + TILE, HD:], ones], axis=1)
            for low in range(0, NV * BLK, TILE)
        ] + [
            jnp.concatenate([here[low : low + TILE, HD:], ones], axis=1)
            for low in range(0, NS * BLK, TILE)
        ]
        return jnp.dot(
            weights[at][...], jnp.concatenate(values, axis=0), preferred_element_type=jnp.float32
        )

    def store(total, block):
        result = (total[:, :HD] / total[:, HD:]).astype(jnp.bfloat16)
        start = pl.multiple_of(block * BLK, BLK)
        for h in range(group_heads):
            out_ref[pl.ds(start, BLK), h * HD : (h + 1) * HD] = result[h * BLK : (h + 1) * BLK]

    def stage(block, pair, at, before_pair, score, weigh, combine):
        other = 1 - at
        here = slash_of(pair, at)
        if score:
            query = query_of(block)
            row = part * part_blocks + jnp.minimum(block, part_blocks - 1)
            bias = bias_ref[pl.ds(row, 1), :]
        if combine:
            total = weighted_values(slash_of(before_pair, at), at)
        if weigh:
            row_max = maxima[other][...]
            row_max = jnp.concatenate([row_max] * (TILE // HD), axis=1)
        highest = None
        fresh = []
        for tile in range((NV + NS) * BLK // TILE):
            low = tile * TILE
            if score:
                found = score_tile(query, bias, here, tile)
                scores[at][:, low : low + TILE] = found
                for part_low in range(0, TILE, HD):
                    piece = found[:, part_low : part_low + HD]
                    highest = piece if highest is None else jnp.maximum(highest, piece)
            if weigh:
                fresh.append(
                    jnp.exp2((scores[other][:, low : low + TILE] - row_max) * rate).astype(
                        jnp.bfloat16
                    )
                )
                weights[other][:, low : low + TILE] = fresh[-1]
        if score:
            maxima[at][...] = jnp.broadcast_to(
                jnp.max(highest, axis=1, keepdims=True), highest.shape
            )
        if combine:
            store(total, jnp.maximum(block - 2, 0))

    @pl.when(step == 0)
    def _():
        fetch(0)
        for entry in range(NV):
            pltpu.make_async_copy(
                gathered_ref.at[
                    slot_ref[head, entry] // MOWN,
                    head,
                    pl.ds(pl.multiple_of(lax.rem(slot_ref[head, entry], MOWN) * BLK, BLK), BLK),
                ],
                vert.at[pl.ds(entry * BLK, BLK)],
                vert_sem,
            ).start()

        @pl.when(steps > 1)
        def _():
            fetch(1)

        column = lax.broadcasted_iota(jnp.int32, (BLK, 2 * BLK), 1)
        row = lax.broadcasted_iota(jnp.int32, (BLK, 2 * BLK), 0)
        diagonal_ref[...] = jnp.where((column < BLK) & (column > row), NEG, 0.0).astype(jnp.float32)
        weights_b[...] = jnp.zeros_like(weights_b)
        slash[BUFFERS - 1, 1] = jnp.zeros(slash.shape[2:], slash.dtype)
        pltpu.make_async_copy(vert, vert, vert_sem).wait()
        arrived(0)
        stage(0, 0, 0, 0, True, False, False)

    @pl.when(step + 1 < steps)
    def _():
        arrived(step + 1)

    @pl.when(step + 2 < steps)
    def _():
        fetch(step + 2)

    first = step * STEP_BLOCKS
    stage(first + 1, step, 1, step - 1, True, True, True)
    stage(first + 2, step + 1, 0, step, True, True, True)

    @pl.when(step + 1 == steps)
    def _():
        store(weighted_values(slash_of(step, 1), 1), first + 1)


def attend(head, part, parity, slot_index, slash, queries, bias, own, two_back, even_back, odd_back,
           gathered, part_rows):
    group_cols = queries.shape[1] // slash.shape[0]
    group_heads = group_cols // HD
    step_rows = STEP_BLOCKS * BLK
    steps = part_rows // step_rows
    any_spec = pl.BlockSpec(memory_space=pl.ANY)
    rows = group_heads * BLK
    keys_seen = (NV + NS) * BLK
    return pl.pallas_call(
        functools.partial(
            attend_kernel, head, steps, group_heads, two_back[0].shape[0] // BLK
        ),
        out_shape=jax.ShapeDtypeStruct((part_rows, group_cols), jnp.bfloat16),
        grid_spec=pltpu.PrefetchScalarGridSpec(
            num_scalar_prefetch=4,
            grid=(steps,),
            in_specs=[
                pl.BlockSpec((part_rows, group_cols), lambda s, part, *_: (part[0], head)),
                pl.BlockSpec(bias.shape, lambda s, *_: (0, 0)),
            ]
            + [any_spec] * (3 + 2 * CHUNKS),
            out_specs=pl.BlockSpec((part_rows, group_cols), lambda s, *_: (0, 0)),
            scratch_shapes=[
                pltpu.VMEM((NV * BLK, 2 * HD), jnp.bfloat16),
                pltpu.VMEM((BUFFERS, STEP_BLOCKS, NS * BLK, 2 * HD), jnp.bfloat16),
                pltpu.VMEM((rows, keys_seen), jnp.float32),
                pltpu.VMEM((rows, keys_seen), jnp.float32),
                pltpu.VMEM((rows, keys_seen), jnp.bfloat16),
                pltpu.VMEM((rows, keys_seen), jnp.bfloat16),
                pltpu.VMEM((rows, HD), jnp.float32),
                pltpu.VMEM((rows, HD), jnp.float32),
                pltpu.VMEM((BLK, 2 * BLK), jnp.float32),
                pltpu.SemaphoreType.DMA,
                pltpu.SemaphoreType.DMA((BUFFERS,)),
            ],
        ),
        compiler_params=pltpu.CompilerParams(
            dimension_semantics=("arbitrary",), vmem_limit_bytes=32 << 20
        ),
        cost_estimate=pl.CostEstimate(
            flops=4 * part_rows * group_heads * keys_seen * HD,
            bytes_accessed=4 * part_rows * group_cols + 16 * keys_seen * HD,
            transcendentals=part_rows * group_heads * keys_seen,
        ),
    )(part, parity, slot_index, slash, queries, bias, own, *two_back, *even_back, odd_back, gathered)


def local(queries, keys, values, vertical, slash):
    shard_count = lax.axis_size("ctx")
    shard_index = lax.axis_index("ctx")
    head_count = lax.axis_size("head")
    head_index = lax.axis_index("head")
    tok_rows = queries.shape[0]
    kv_local = keys.shape[1] // HD
    group_cols = queries.shape[1] // kv_local
    blocks_dev = tok_rows // BLK
    part_rows = tok_rows // head_count

    owners = vertical // blocks_dev
    order = jnp.arange(NV, dtype=jnp.int32)
    same_owner = owners[:, :, None] == owners[:, None, :]
    earlier = order[None, :] < order[:, None]
    slot_rank = jnp.sum((same_owner & earlier[None]).astype(jnp.int32), axis=2)
    slot_index = owners * MOWN + slot_rank
    in_slot = (owners == shard_index)[:, :, None] & (
        slot_rank[:, :, None] == jnp.arange(MOWN, dtype=jnp.int32)
    )
    local_block = jnp.sum(in_slot * (vertical % blocks_dev)[:, :, None], axis=1)
    gathered = lax.all_gather(owned_slots(local_block, keys, values), "ctx")

    slash_rank = jnp.sum((slash[:, None, :] < slash[:, :, None]).astype(jnp.int32), axis=2)
    place = slash_rank[:, :, None] == jnp.arange(NS, dtype=jnp.int32)
    slash = jnp.sum(place * slash[:, :, None], axis=1)

    global_blocks = shard_index * blocks_dev + jnp.arange(blocks_dev, dtype=jnp.int32)
    vert_valid = vertical[:, None, :] < global_blocks[None, :, None]
    slash_blocks = global_blocks[None, :, None] - slash[:, None, :]
    in_vertical = jnp.any(slash_blocks[:, :, :, None] == vertical[:, None, None, :], axis=3)
    slash_valid = (slash[:, None, :] == 0) | ((slash_blocks >= 0) & jnp.logical_not(in_vertical))
    valid = jnp.concatenate([vert_valid, slash_valid], axis=2)
    bias = jnp.repeat(jnp.where(valid, 0.0, NEG).astype(jnp.float32), BLK, axis=2)

    two_pairs = [(i, i + 2) for i in range(shard_count - 2)]
    even_to_odd = [(i, i + 1) for i in range(0, shard_count - 1, 2)]
    odd_to_even = [(i, i - 1) for i in range(1, shard_count, 2)]
    chunk_rows = tok_rows // CHUNKS
    windows = []
    before = gathered
    for head in range(kv_local):
        columns = slice(head * HD, (head + 1) * HD)
        own = jnp.concatenate([keys[:, columns], values[:, columns]], axis=1)
        own, before = lax.optimization_barrier((own, before))
        if head == 0:
            gathered = before
        two_back = [
            lax.ppermute(own[c * chunk_rows : (c + 1) * chunk_rows], "ctx", two_pairs)
            for c in range(CHUNKS)
        ]
        odd_back = lax.ppermute(own, "ctx", even_to_odd)
        even_back = [lax.ppermute(piece, "ctx", odd_to_even) for piece in two_back]
        two_back[-1], before = lax.optimization_barrier((two_back[-1], two_back[-1][:8]))
        windows.append((own, two_back, even_back, odd_back))

    parity = (shard_index % 2).reshape(1).astype(jnp.int32)
    out = jnp.zeros((part_rows, head_count * kv_local * group_cols), jnp.bfloat16)
    for head in range(kv_local):
        own, two_back, even_back, odd_back = windows[head]
        for flip in range(head_count - 1, -1, -1):
            other = head_index ^ flip
            piece = attend(
                head, other.reshape(1).astype(jnp.int32), parity, slot_index, slash, queries,
                bias[head], own, two_back, even_back, odd_back, gathered, part_rows,
            )
            if flip:
                piece = lax.ppermute(piece, "head", [(i, i ^ flip) for i in range(head_count)])
            out = lax.dynamic_update_slice(
                out, piece, (0, other * kv_local * group_cols + head * group_cols)
            )
    return out


def solution(mesh):
    in_specs = (
        P("ctx", "head"),
        P("ctx", "head"),
        P("ctx", "head"),
        P("head", None),
        P("head", None),
    )
    out_specs = P(("ctx", "head"), None)
    return jax.shard_map(local, mesh=mesh, in_specs=in_specs, out_specs=out_specs, check_vma=False)
```

```python
import functools
import math

import jax
import jax.numpy as jnp
from jax import lax
from jax.experimental import pallas as pl
from jax.experimental.pallas import tpu as pltpu
from jax.sharding import PartitionSpec as P

HD = 128
BLK = 64
NV = 16
NS = 8
MOWN = 4
LOOK = 2
NEG = -1e30
STEP_BLOCKS = 2
CHUNKS = 2
TILE = 256
ANY = pl.BlockSpec(memory_space=pl.ANY)
SMEM = pl.BlockSpec(memory_space=pltpu.SMEM)


def blocks_at(index, count=1):
    return pl.ds(pl.multiple_of(index * BLK, BLK), count * BLK)


def slots_kernel(local_ref, keys_ref, values_ref, out_ref, sem):
    copies = []
    for head in range(out_ref.shape[0]):
        for slot in range(MOWN):
            for side, source in enumerate((keys_ref, values_ref)):
                copies.append(
                    pltpu.make_async_copy(
                        source.at[blocks_at(local_ref[head, slot]), pl.ds(head * HD, HD)],
                        out_ref.at[head, pl.ds(slot * BLK, BLK), pl.ds(side * HD, HD)],
                        sem.at[len(copies)],
                    )
                )
    for copy in copies:
        copy.start()
    for copy in copies:
        copy.wait()


def owned_slots(local_block, keys, values):
    heads = local_block.shape[0]
    return pl.pallas_call(
        slots_kernel,
        out_shape=jax.ShapeDtypeStruct((heads, MOWN * BLK, 2 * HD), keys.dtype),
        in_specs=[SMEM, ANY, ANY],
        out_specs=ANY,
        scratch_shapes=[pltpu.SemaphoreType.DMA((heads * MOWN * 2,))],
        compiler_params=pltpu.CompilerParams(vmem_limit_bytes=1 << 20),
        cost_estimate=pl.CostEstimate(
            flops=0, bytes_accessed=4 * heads * MOWN * BLK * 2 * HD, transcendentals=0
        ),
    )(local_block, keys, values)


def pair_kernel(head, keys_ref, values_ref, *rest):
    out_ref, sem = rest[-2:]
    copies = [
        pltpu.make_async_copy(
            source.at[:, pl.ds(head * HD, HD)], out_ref.at[:, pl.ds(side * HD, HD)], sem.at[side]
        )
        for side, source in enumerate((keys_ref, values_ref))
    ]
    for copy in copies:
        copy.start()
    for copy in copies:
        copy.wait()


def pair_of(head, keys, values, after):
    return pl.pallas_call(
        functools.partial(pair_kernel, head),
        out_shape=jax.ShapeDtypeStruct((keys.shape[0], 2 * HD), keys.dtype),
        in_specs=[ANY] * (2 + len(after)),
        out_specs=ANY,
        scratch_shapes=[pltpu.SemaphoreType.DMA((2,))],
        compiler_params=pltpu.CompilerParams(vmem_limit_bytes=1 << 20),
        cost_estimate=pl.CostEstimate(
            flops=0, bytes_accessed=8 * keys.shape[0] * HD, transcendentals=0
        ),
    )(keys, values, *after)


def listed_kernel(place_ref, source_ref, *rest):
    arrays, out_ref, sem = rest[:-2], rest[-2], rest[-1]
    heads = out_ref.shape[0]
    for head in range(heads):
        for index, array in enumerate(arrays):
            for slot in range(MOWN):
                place = place_ref[index, head, slot]

                @pl.when(place >= 0)
                def _():
                    pltpu.make_async_copy(
                        array.at[head, pl.ds(slot * BLK, BLK)],
                        out_ref.at[head, blocks_at(place)],
                        sem,
                    ).start()

        for entry in range(NV):

            @pl.when(source_ref[head, entry] < 0)
            def _():
                pltpu.make_async_copy(
                    arrays[0].at[head, pl.ds(0, BLK)],
                    out_ref.at[head, pl.ds(entry * BLK, BLK)],
                    sem,
                ).start()

    pltpu.make_async_copy(out_ref, out_ref, sem).wait()


def listed_blocks(place, source, arrays):
    heads = source.shape[0]
    return pl.pallas_call(
        listed_kernel,
        out_shape=jax.ShapeDtypeStruct((heads, NV * BLK, 2 * HD), arrays[0].dtype),
        in_specs=[SMEM, SMEM] + [ANY] * len(arrays),
        out_specs=ANY,
        scratch_shapes=[pltpu.SemaphoreType.DMA],
        compiler_params=pltpu.CompilerParams(vmem_limit_bytes=1 << 20),
        cost_estimate=pl.CostEstimate(
            flops=0, bytes_accessed=8 * heads * NV * BLK * HD, transcendentals=0
        ),
    )(place, source, *arrays)


def attend_kernel(
    head, parts, part_blocks, group_heads, part_ref, parity_ref, slash_ref, bias_ref, query_ref,
    vert_ref, own_ref, *rest,
):
    two_back = rest[:CHUNKS]
    even_back = rest[CHUNKS : 2 * CHUNKS]
    odd_back = rest[2 * CHUNKS]
    rest = rest[2 * CHUNKS + 1 :]
    out_refs = rest[:parts]
    (
        queries, out, vert, vert_keys, window, scores_a, scores_b, weights_a, weights_b, max_a,
        max_b, diagonal_ref, query_sem, vert_sem, window_sem, out_sem,
    ) = rest[parts:]
    scores, weights, maxima = (scores_a, scores_b), (weights_a, weights_b), (max_a, max_b)
    tok_rows = own_ref.shape[0]
    blocks_dev = tok_rows // BLK
    part_rows = part_blocks * BLK
    group_cols = group_heads * HD
    chunk_rows = tok_rows // CHUNKS
    last = parts * part_blocks - 1
    step = pl.program_id(0)
    scale = 1.0 / math.sqrt(HD)
    contract = (((1,), (1,)), ((), ()))

    def shard_block(block):
        return part_ref[block // part_blocks] * part_blocks + lax.rem(block, part_blocks)

    def slash_rows(block):
        first = LOOK * blocks_dev + shard_block(block)
        return [blocks_at(first - slash_ref[head, entry]) for entry in range(NS)]

    def query_of(block):
        rows = blocks_at(block)
        return jnp.concatenate(
            [queries[rows, h * HD : (h + 1) * HD] for h in range(group_heads)], axis=0
        )

    def score_tile(query, bias, rows, tile):
        low = tile * TILE
        if low < NV * BLK:
            found = jnp.dot(
                query, vert_keys[:, low : low + TILE], preferred_element_type=jnp.float32
            )
        else:
            entry = (low - NV * BLK) // BLK
            keys = jnp.concatenate(
                [window[r, :HD] for r in rows[entry : entry + TILE // BLK]], axis=0
            )
            found = lax.dot_general(query, keys, contract, preferred_element_type=jnp.float32)
        found = found + bias[:, low : low + TILE]
        if low == NV * BLK:
            diagonal = jnp.concatenate([diagonal_ref[...]] * group_heads, axis=0)
            found = jnp.concatenate(
                [found[:, : 2 * BLK] + diagonal, found[:, 2 * BLK :]], axis=1
            )
        return found

    def weighted_values(block, at):
        ones = jnp.ones(((NV + NS) * BLK, HD), jnp.bfloat16)
        values = jnp.concatenate([vert[:, HD:]] + [window[r, HD:] for r in slash_rows(block)], axis=0)
        return jnp.dot(
            weights[at][...],
            jnp.concatenate([values, ones], axis=1),
            preferred_element_type=jnp.float32,
        )

    def store(total, block):
        result = (total[:, :HD] / total[:, HD:]).astype(jnp.bfloat16)
        rows = blocks_at(block)
        for h in range(group_heads):
            out[rows, h * HD : (h + 1) * HD] = result[h * BLK : (h + 1) * BLK]

    def stage(block, at, score, weigh, combine):
        other = 1 - at
        if score:
            fresh = jnp.minimum(block, last)
            query = query_of(fresh)
            rows = slash_rows(fresh)
            bias = bias_ref[pl.ds(shard_block(fresh), 1), :]
        if combine:
            done = jnp.maximum(block - 2, 0)
            total = weighted_values(done, at)
        if weigh:
            row_max = maxima[other][...]
            row_max = jnp.concatenate([row_max] * (TILE // HD), axis=1)
        highest = None
        for tile in range((NV + NS) * BLK // TILE):
            low = tile * TILE
            if score:
                found = score_tile(query, bias, rows, tile)
                scores[at][:, low : low + TILE] = found
                for piece_low in range(0, TILE, HD):
                    piece = found[:, piece_low : piece_low + HD]
                    highest = piece if highest is None else jnp.maximum(highest, piece)
            if weigh:
                weights[other][:, low : low + TILE] = jnp.exp(
                    (scores[other][:, low : low + TILE] - row_max) * scale
                ).astype(jnp.bfloat16)
        if score:
            maxima[at][...] = jnp.broadcast_to(
                jnp.max(highest, axis=1, keepdims=True), highest.shape
            )
        if combine:
            store(total, done)

    @pl.when(step == 0)
    def _():
        for k in range(parts):
            pltpu.make_async_copy(
                query_ref.at[
                    pl.ds(pl.multiple_of(part_ref[k] * part_rows, part_rows), part_rows),
                    pl.ds(head * group_cols, group_cols),
                ],
                queries.at[pl.ds(k * part_rows, part_rows)],
                query_sem,
            ).start()
        pltpu.make_async_copy(vert_ref.at[head], vert, vert_sem).start()
        for chunk in range(CHUNKS):
            pltpu.make_async_copy(
                two_back[chunk], window.at[pl.ds(chunk * chunk_rows, chunk_rows)], window_sem
            ).start()

        @pl.when(parity_ref[0] == 1)
        def _():
            pltpu.make_async_copy(
                odd_back, window.at[pl.ds(tok_rows, tok_rows)], window_sem
            ).start()

        @pl.when(parity_ref[0] == 0)
        def _():
            for chunk in range(CHUNKS):
                pltpu.make_async_copy(
                    even_back[chunk],
                    window.at[pl.ds(tok_rows + chunk * chunk_rows, chunk_rows)],
                    window_sem,
                ).start()

        pltpu.make_async_copy(
            own_ref, window.at[pl.ds(LOOK * tok_rows, tok_rows)], window_sem
        ).start()
        column = lax.broadcasted_iota(jnp.int32, (BLK, 2 * BLK), 1)
        row = lax.broadcasted_iota(jnp.int32, (BLK, 2 * BLK), 0)
        diagonal_ref[...] = jnp.where((column < BLK) & (column > row), NEG, 0.0).astype(jnp.float32)
        weights_b[...] = jnp.zeros_like(weights_b)
        pltpu.make_async_copy(vert, vert, vert_sem).wait()
        vert_keys[...] = vert[:, :HD].T
        pltpu.make_async_copy(queries, queries, query_sem).wait()
        pltpu.make_async_copy(window, window, window_sem).wait()
        stage(0, 0, True, False, False)

    first = step * STEP_BLOCKS
    stage(first + 1, 1, True, True, True)
    stage(first + 2, 0, True, True, True)

    @pl.when(first + STEP_BLOCKS > last)
    def _():
        store(weighted_values(last, 1), last)
        for k in range(parts):
            pltpu.make_async_copy(
                out.at[pl.ds(k * part_rows, part_rows)], out_refs[k], out_sem.at[k]
            ).start()
        for k in range(parts):
            pltpu.make_async_copy(
                out.at[pl.ds(k * part_rows, part_rows)], out_refs[k], out_sem.at[k]
            ).wait()


def attend(head, part, parity, slash, bias, queries, vert, own, two_back, even_back, odd_back,
           part_rows):
    parts = part.shape[0]
    group_cols = queries.shape[1] // slash.shape[0]
    group_heads = group_cols // HD
    part_blocks = part_rows // BLK
    tok_rows = own.shape[0]
    rows = group_heads * BLK
    keys_seen = (NV + NS) * BLK
    return pl.pallas_call(
        functools.partial(attend_kernel, head, parts, part_blocks, group_heads),
        out_shape=[jax.ShapeDtypeStruct((part_rows, group_cols), jnp.bfloat16)] * parts,
        grid_spec=pltpu.PrefetchScalarGridSpec(
            num_scalar_prefetch=3,
            grid=(parts * part_blocks // STEP_BLOCKS,),
            in_specs=[pl.BlockSpec(bias.shape, lambda s, *_: (0, 0))] + [ANY] * (4 + 2 * CHUNKS),
            out_specs=[ANY] * parts,
            scratch_shapes=[
                pltpu.VMEM((parts * part_rows, group_cols), jnp.bfloat16),
                pltpu.VMEM((parts * part_rows, group_cols), jnp.bfloat16),
                pltpu.VMEM((NV * BLK, 2 * HD), jnp.bfloat16),
                pltpu.VMEM((HD, NV * BLK), jnp.bfloat16),
                pltpu.VMEM(((LOOK + 1) * tok_rows, 2 * HD), jnp.bfloat16),
                pltpu.VMEM((rows, keys_seen), jnp.float32),
                pltpu.VMEM((rows, keys_seen), jnp.float32),
                pltpu.VMEM((rows, keys_seen), jnp.bfloat16),
                pltpu.VMEM((rows, keys_seen), jnp.bfloat16),
                pltpu.VMEM((rows, HD), jnp.float32),
                pltpu.VMEM((rows, HD), jnp.float32),
                pltpu.VMEM((BLK, 2 * BLK), jnp.float32),
                pltpu.SemaphoreType.DMA,
                pltpu.SemaphoreType.DMA,
                pltpu.SemaphoreType.DMA,
                pltpu.SemaphoreType.DMA((parts,)),
            ],
        ),
        compiler_params=pltpu.CompilerParams(
            dimension_semantics=("arbitrary",), vmem_limit_bytes=32 << 20
        ),
        cost_estimate=pl.CostEstimate(
            flops=4 * parts * part_rows * group_heads * keys_seen * HD,
            bytes_accessed=4 * parts * part_rows * group_cols + 12 * tok_rows * HD,
            transcendentals=parts * part_rows * group_heads * keys_seen,
        ),
    )(part, parity, slash, bias, queries, vert, own, *two_back, *even_back, odd_back)


def local(queries, keys, values, vertical, slash):
    shard_count = lax.axis_size("ctx")
    shard_index = lax.axis_index("ctx")
    head_count = lax.axis_size("head")
    head_index = lax.axis_index("head")
    tok_rows = queries.shape[0]
    kv_local = keys.shape[1] // HD
    group_cols = queries.shape[1] // kv_local
    blocks_dev = tok_rows // BLK
    part_rows = tok_rows // head_count
    partner = shard_index ^ 1
    two_pairs = [(i, i + 2) for i in range(shard_count - 2)]
    even_to_odd = [(i, i + 1) for i in range(0, shard_count - 1, 2)]
    odd_to_even = [(i, i - 1) for i in range(1, shard_count, 2)]
    chunk_rows = tok_rows // CHUNKS

    owners = vertical // blocks_dev
    order = jnp.arange(NV, dtype=jnp.int32)
    same_owner = owners[:, :, None] == owners[:, None, :]
    earlier = order[None, :] < order[:, None]
    slot_rank = jnp.sum((same_owner & earlier[None]).astype(jnp.int32), axis=2)
    slots = jnp.arange(MOWN, dtype=jnp.int32)
    in_slot = slot_rank[:, :, None] == slots
    local_block = jnp.sum(
        ((owners == shard_index)[:, :, None] & in_slot) * (vertical % blocks_dev)[:, :, None],
        axis=1,
    )
    behind = [owned_slots(local_block, keys, values)]
    for _ in range(1, shard_count // 2):
        behind.append(lax.ppermute(behind[-1], "ctx", two_pairs))
    across = [
        lax.ppermute(array, "ctx", even_to_odd + (odd_to_even if k else []))
        for k, array in enumerate(behind)
    ]
    steps = 2 * jnp.arange(shard_count // 2, dtype=jnp.int32)
    array_owner = jnp.concatenate([shard_index - steps, partner - steps])
    array_owner = jnp.where(array_owner <= shard_index, array_owner, -1)
    here = (array_owner[:, None, None] == owners)[:, :, :, None] & in_slot[None]
    place = jnp.sum(here * (order + 1)[None, None, :, None], axis=2) - 1
    source = jnp.where(owners <= shard_index, 0, -1).astype(jnp.int32)

    slash_rank = jnp.sum((slash[:, None, :] < slash[:, :, None]).astype(jnp.int32), axis=2)
    at_rank = slash_rank[:, :, None] == jnp.arange(NS, dtype=jnp.int32)
    slash = jnp.sum(at_rank * slash[:, :, None], axis=1)

    global_blocks = shard_index * blocks_dev + jnp.arange(blocks_dev, dtype=jnp.int32)
    vert_valid = vertical[:, None, :] < global_blocks[None, :, None]
    slash_blocks = global_blocks[None, :, None] - slash[:, None, :]
    in_vertical = jnp.any(slash_blocks[:, :, :, None] == vertical[:, None, None, :], axis=3)
    slash_valid = (slash[:, None, :] == 0) | ((slash_blocks >= 0) & jnp.logical_not(in_vertical))
    valid = jnp.concatenate([vert_valid, slash_valid], axis=2)
    bias = jnp.repeat(jnp.where(valid, 0.0, NEG).astype(jnp.float32), BLK, axis=2)

    windows = []
    after = []
    for head in range(kv_local):
        own = pair_of(head, keys, values, after)
        two_back = [
            lax.ppermute(own[c * chunk_rows : (c + 1) * chunk_rows], "ctx", two_pairs)
            for c in range(CHUNKS)
        ]
        odd_back = lax.ppermute(own, "ctx", even_to_odd)
        even_back = [lax.ppermute(piece, "ctx", odd_to_even) for piece in two_back]
        windows.append((own, two_back, even_back, odd_back))
        after = [two_back[0]]
    vert = listed_blocks(place, source, behind + across)

    parity = (shard_index % 2).reshape(1).astype(jnp.int32)
    out = jnp.zeros((part_rows, head_count * kv_local * group_cols), jnp.bfloat16)
    half = head_count // 2
    for head in range(kv_local):
        own, two_back, even_back, odd_back = windows[head]
        for flips in (range(head_count - 1, half - 1, -1), range(half - 1, -1, -1)):
            others = [head_index ^ flip for flip in flips]
            pieces = attend(
                head, jnp.stack(others).astype(jnp.int32), parity, slash, bias[head], queries,
                vert, own, two_back, even_back, odd_back, part_rows,
            )
            for flip, other, piece in zip(flips, others, pieces):
                if flip:
                    piece = lax.ppermute(piece, "head", [(i, i ^ flip) for i in range(head_count)])
                out = lax.dynamic_update_slice(
                    out, piece, (0, other * kv_local * group_cols + head * group_cols)
                )
    return out


def solution(mesh):
    in_specs = (
        P("ctx", "head"),
        P("ctx", "head"),
        P("ctx", "head"),
        P("head", None),
        P("head", None),
    )
    out_specs = P(("ctx", "head"), None)
    return jax.shard_map(local, mesh=mesh, in_specs=in_specs, out_specs=out_specs, check_vma=False)
```

```python
import functools
import math

import jax
import jax.numpy as jnp
from jax import lax
from jax.experimental import pallas as pl
from jax.experimental.pallas import tpu as pltpu
from jax.sharding import PartitionSpec as P

HD = 128
BLK = 64
NV = 16
NS = 8
MOWN = 4
LOOK = 2
NEG = -1e30
STEP_BLOCKS = 2
CHUNKS = 2
TILE = 256
ANY = pl.BlockSpec(memory_space=pl.ANY)
SMEM = pl.BlockSpec(memory_space=pltpu.SMEM)


def blocks_at(index, count=1):
    return pl.ds(pl.multiple_of(index * BLK, BLK), count * BLK)


def slots_kernel(head, local_ref, keys_ref, values_ref, *rest):
    out_ref, sem = rest[-2:]
    copies = []
    for slot in range(MOWN):
        for side, source in enumerate((keys_ref, values_ref)):
            copies.append(
                pltpu.make_async_copy(
                    source.at[blocks_at(local_ref[head, slot]), pl.ds(head * HD, HD)],
                    out_ref.at[pl.ds(slot * BLK, BLK), pl.ds(side * HD, HD)],
                    sem.at[len(copies)],
                )
            )
    for copy in copies:
        copy.start()
    for copy in copies:
        copy.wait()


def owned_slots(head, local_block, keys, values, after):
    return pl.pallas_call(
        functools.partial(slots_kernel, head),
        out_shape=jax.ShapeDtypeStruct((MOWN * BLK, 2 * HD), keys.dtype),
        in_specs=[SMEM] + [ANY] * (2 + len(after)),
        out_specs=ANY,
        scratch_shapes=[pltpu.SemaphoreType.DMA((MOWN * 2,))],
        compiler_params=pltpu.CompilerParams(vmem_limit_bytes=1 << 20),
        cost_estimate=pl.CostEstimate(
            flops=0, bytes_accessed=8 * MOWN * BLK * HD, transcendentals=0
        ),
    )(local_block, keys, values, *after)


def pair_kernel(head, keys_ref, values_ref, *rest):
    out_refs, sem = rest[-2 - CHUNKS : -1], rest[-1]
    whole, chunks = out_refs[0], out_refs[1:]
    copies = []
    for side, source in enumerate((keys_ref, values_ref)):
        columns, to = pl.ds(head * HD, HD), pl.ds(side * HD, HD)
        for index, chunk in enumerate(chunks):
            rows = pl.ds(index * chunk.shape[0], chunk.shape[0])
            copies.append((source.at[rows, columns], chunk.at[:, to]))
        copies.append((source.at[:, columns], whole.at[:, to]))
    copies = [pltpu.make_async_copy(*ends, sem.at[k]) for k, ends in enumerate(copies)]
    for copy in copies:
        copy.start()
    for copy in copies:
        copy.wait()


def pair_of(head, keys, values, after):
    rows = keys.shape[0]
    whole, *chunks = pl.pallas_call(
        functools.partial(pair_kernel, head),
        out_shape=[jax.ShapeDtypeStruct((rows, 2 * HD), keys.dtype)]
        + [jax.ShapeDtypeStruct((rows // CHUNKS, 2 * HD), keys.dtype)] * CHUNKS,
        in_specs=[ANY] * (2 + len(after)),
        out_specs=[ANY] * (1 + CHUNKS),
        scratch_shapes=[pltpu.SemaphoreType.DMA((2 + 2 * CHUNKS,))],
        compiler_params=pltpu.CompilerParams(vmem_limit_bytes=1 << 20),
        cost_estimate=pl.CostEstimate(flops=0, bytes_accessed=16 * rows * HD, transcendentals=0),
    )(keys, values, *after)
    return whole, chunks


def listed_kernel(head, place_ref, source_ref, behind_refs, across_ref, out_ref, sem):
    count = len(behind_refs)
    for index in range(2 * count):
        for slot in range(MOWN):
            place = place_ref[index, head, slot]
            if index < count:
                found = behind_refs[index].at[pl.ds(slot * BLK, BLK)]
            else:
                found = across_ref.at[pl.ds(((index - count) * MOWN + slot) * BLK, BLK)]

            @pl.when(place >= 0)
            def _():
                pltpu.make_async_copy(found, out_ref.at[blocks_at(place)], sem).start()

    for entry in range(NV):

        @pl.when(source_ref[head, entry] < 0)
        def _():
            pltpu.make_async_copy(
                behind_refs[0].at[pl.ds(0, BLK)], out_ref.at[pl.ds(entry * BLK, BLK)], sem
            ).start()

    pltpu.make_async_copy(out_ref, out_ref, sem).wait()


def listed_blocks(head, place, source, behind, across):
    return pl.pallas_call(
        functools.partial(listed_kernel, head),
        out_shape=jax.ShapeDtypeStruct((NV * BLK, 2 * HD), across.dtype),
        in_specs=[SMEM, SMEM, [ANY] * len(behind), ANY],
        out_specs=ANY,
        scratch_shapes=[pltpu.SemaphoreType.DMA],
        compiler_params=pltpu.CompilerParams(vmem_limit_bytes=1 << 20),
        cost_estimate=pl.CostEstimate(flops=0, bytes_accessed=8 * NV * BLK * HD, transcendentals=0),
    )(place, source, behind, across)


def attend_kernel(
    head, parts, waits, part_blocks, group_heads, part_ref, parity_ref, slash_ref, bias_ref, query_ref,
    vert_ref, own_ref, *rest,
):
    two_back = rest[:CHUNKS]
    even_back = rest[CHUNKS : 2 * CHUNKS]
    odd_back = rest[2 * CHUNKS]
    rest = rest[2 * CHUNKS + 1 + waits :]
    out_refs = rest[:parts]
    (
        queries, out, vert, vert_keys, window, scores_a, scores_b, weights_a, weights_b, max_a,
        max_b, diagonal_ref, query_sem, vert_sem, window_sem, out_sem,
    ) = rest[parts:]
    scores, weights, maxima = (scores_a, scores_b), (weights_a, weights_b), (max_a, max_b)
    tok_rows = own_ref.shape[0]
    blocks_dev = tok_rows // BLK
    part_rows = part_blocks * BLK
    group_cols = group_heads * HD
    chunk_rows = tok_rows // CHUNKS
    last = parts * part_blocks - 1
    step = pl.program_id(0)
    scale = 1.0 / math.sqrt(HD)
    contract = (((1,), (1,)), ((), ()))

    def shard_block(block):
        return part_ref[block // part_blocks] * part_blocks + lax.rem(block, part_blocks)

    def slash_rows(block):
        first = LOOK * blocks_dev + shard_block(block)
        return [blocks_at(first - slash_ref[head, entry]) for entry in range(NS)]

    def query_of(block):
        rows = blocks_at(block)
        return jnp.concatenate(
            [queries[rows, h * HD : (h + 1) * HD] for h in range(group_heads)], axis=0
        )

    def score_tile(query, bias, rows, tile):
        low = tile * TILE
        if low < NV * BLK:
            found = jnp.dot(
                query, vert_keys[:, low : low + TILE], preferred_element_type=jnp.float32
            )
        else:
            entry = (low - NV * BLK) // BLK
            keys = jnp.concatenate(
                [window[r, :HD] for r in rows[entry : entry + TILE // BLK]], axis=0
            )
            found = lax.dot_general(query, keys, contract, preferred_element_type=jnp.float32)
        found = found + bias[:, low : low + TILE]
        if low == NV * BLK:
            diagonal = jnp.concatenate([diagonal_ref[...]] * group_heads, axis=0)
            found = jnp.concatenate(
                [found[:, : 2 * BLK] + diagonal, found[:, 2 * BLK :]], axis=1
            )
        return found

    def weighted_values(block, at):
        ones = jnp.ones(((NV + NS) * BLK, HD), jnp.bfloat16)
        values = jnp.concatenate([vert[:, HD:]] + [window[r, HD:] for r in slash_rows(block)], axis=0)
        return jnp.dot(
            weights[at][...],
            jnp.concatenate([values, ones], axis=1),
            preferred_element_type=jnp.float32,
        )

    def store(total, block):
        result = (total[:, :HD] / total[:, HD:]).astype(jnp.bfloat16)
        rows = blocks_at(block)
        for h in range(group_heads):
            out[rows, h * HD : (h + 1) * HD] = result[h * BLK : (h + 1) * BLK]

    def stage(block, at, score, weigh, combine):
        other = 1 - at
        if score:
            fresh = jnp.minimum(block, last)
            query = query_of(fresh)
            rows = slash_rows(fresh)
            bias = bias_ref[pl.ds(shard_block(fresh), 1), :]
        if combine:
            done = jnp.maximum(block - 2, 0)
            total = weighted_values(done, at)
        if weigh:
            row_max = maxima[other][...]
            row_max = jnp.concatenate([row_max] * (TILE // HD), axis=1)
        highest = None
        for tile in range((NV + NS) * BLK // TILE):
            low = tile * TILE
            if score:
                found = score_tile(query, bias, rows, tile)
                scores[at][:, low : low + TILE] = found
                for piece_low in range(0, TILE, HD):
                    piece = found[:, piece_low : piece_low + HD]
                    highest = piece if highest is None else jnp.maximum(highest, piece)
            if weigh:
                weights[other][:, low : low + TILE] = jnp.exp(
                    (scores[other][:, low : low + TILE] - row_max) * scale
                ).astype(jnp.bfloat16)
        if score:
            maxima[at][...] = jnp.broadcast_to(
                jnp.max(highest, axis=1, keepdims=True), highest.shape
            )
        if combine:
            store(total, done)

    @pl.when(step == 0)
    def _():
        for k in range(parts):
            pltpu.make_async_copy(
                query_ref.at[
                    pl.ds(pl.multiple_of(part_ref[k] * part_rows, part_rows), part_rows),
                    pl.ds(head * group_cols, group_cols),
                ],
                queries.at[pl.ds(k * part_rows, part_rows)],
                query_sem,
            ).start()
        pltpu.make_async_copy(vert_ref, vert, vert_sem).start()
        for chunk in range(CHUNKS):
            pltpu.make_async_copy(
                two_back[chunk], window.at[pl.ds(chunk * chunk_rows, chunk_rows)], window_sem
            ).start()

        @pl.when(parity_ref[0] == 1)
        def _():
            pltpu.make_async_copy(
                odd_back, window.at[pl.ds(tok_rows, tok_rows)], window_sem
            ).start()

        @pl.when(parity_ref[0] == 0)
        def _():
            for chunk in range(CHUNKS):
                pltpu.make_async_copy(
                    even_back[chunk],
                    window.at[pl.ds(tok_rows + chunk * chunk_rows, chunk_rows)],
                    window_sem,
                ).start()

        pltpu.make_async_copy(
            own_ref, window.at[pl.ds(LOOK * tok_rows, tok_rows)], window_sem
        ).start()
        column = lax.broadcasted_iota(jnp.int32, (BLK, 2 * BLK), 1)
        row = lax.broadcasted_iota(jnp.int32, (BLK, 2 * BLK), 0)
        diagonal_ref[...] = jnp.where((column < BLK) & (column > row), NEG, 0.0).astype(jnp.float32)
        weights_b[...] = jnp.zeros_like(weights_b)
        pltpu.make_async_copy(vert, vert, vert_sem).wait()
        vert_keys[...] = vert[:, :HD].T
        pltpu.make_async_copy(queries, queries, query_sem).wait()
        pltpu.make_async_copy(window, window, window_sem).wait()
        stage(0, 0, True, False, False)

    first = step * STEP_BLOCKS
    stage(first + 1, 1, True, True, True)
    stage(first + 2, 0, True, True, True)

    @pl.when(first + STEP_BLOCKS > last)
    def _():
        store(weighted_values(last, 1), last)
        for k in range(parts):
            pltpu.make_async_copy(
                out.at[pl.ds(k * part_rows, part_rows)], out_refs[k], out_sem.at[k]
            ).start()
        for k in range(parts):
            pltpu.make_async_copy(
                out.at[pl.ds(k * part_rows, part_rows)], out_refs[k], out_sem.at[k]
            ).wait()


def attend(head, part, parity, slash, bias, queries, vert, own, two_back, even_back, odd_back,
           part_rows, after):
    parts = part.shape[0]
    group_cols = queries.shape[1] // slash.shape[0]
    group_heads = group_cols // HD
    part_blocks = part_rows // BLK
    tok_rows = own.shape[0]
    rows = group_heads * BLK
    keys_seen = (NV + NS) * BLK
    return pl.pallas_call(
        functools.partial(attend_kernel, head, parts, len(after), part_blocks, group_heads),
        out_shape=[jax.ShapeDtypeStruct((part_rows, group_cols), jnp.bfloat16)] * parts,
        grid_spec=pltpu.PrefetchScalarGridSpec(
            num_scalar_prefetch=3,
            grid=(parts * part_blocks // STEP_BLOCKS,),
            in_specs=[pl.BlockSpec(bias.shape, lambda s, *_: (0, 0))] + [ANY] * (4 + 2 * CHUNKS + len(after)),
            out_specs=[ANY] * parts,
            scratch_shapes=[
                pltpu.VMEM((parts * part_rows, group_cols), jnp.bfloat16),
                pltpu.VMEM((parts * part_rows, group_cols), jnp.bfloat16),
                pltpu.VMEM((NV * BLK, 2 * HD), jnp.bfloat16),
                pltpu.VMEM((HD, NV * BLK), jnp.bfloat16),
                pltpu.VMEM(((LOOK + 1) * tok_rows, 2 * HD), jnp.bfloat16),
                pltpu.VMEM((rows, keys_seen), jnp.float32),
                pltpu.VMEM((rows, keys_seen), jnp.float32),
                pltpu.VMEM((rows, keys_seen), jnp.bfloat16),
                pltpu.VMEM((rows, keys_seen), jnp.bfloat16),
                pltpu.VMEM((rows, HD), jnp.float32),
                pltpu.VMEM((rows, HD), jnp.float32),
                pltpu.VMEM((BLK, 2 * BLK), jnp.float32),
                pltpu.SemaphoreType.DMA,
                pltpu.SemaphoreType.DMA,
                pltpu.SemaphoreType.DMA,
                pltpu.SemaphoreType.DMA((parts,)),
            ],
        ),
        compiler_params=pltpu.CompilerParams(
            dimension_semantics=("arbitrary",), vmem_limit_bytes=32 << 20
        ),
        cost_estimate=pl.CostEstimate(
            flops=4 * parts * part_rows * group_heads * keys_seen * HD,
            bytes_accessed=4 * parts * part_rows * group_cols + 12 * tok_rows * HD,
            transcendentals=parts * part_rows * group_heads * keys_seen,
        ),
    )(part, parity, slash, bias, queries, vert, own, *two_back, *even_back, odd_back, *after)


def local(queries, keys, values, vertical, slash):
    shard_count = lax.axis_size("ctx")
    shard_index = lax.axis_index("ctx")
    head_count = lax.axis_size("head")
    head_index = lax.axis_index("head")
    tok_rows = queries.shape[0]
    kv_local = keys.shape[1] // HD
    group_cols = queries.shape[1] // kv_local
    blocks_dev = tok_rows // BLK
    part_rows = tok_rows // head_count
    partner = shard_index ^ 1
    two_pairs = [(i, i + 2) for i in range(shard_count - 2)]
    even_to_odd = [(i, i + 1) for i in range(0, shard_count - 1, 2)]
    odd_to_even = [(i, i - 1) for i in range(1, shard_count, 2)]

    owners = vertical // blocks_dev
    order = jnp.arange(NV, dtype=jnp.int32)
    same_owner = owners[:, :, None] == owners[:, None, :]
    earlier = order[None, :] < order[:, None]
    slot_rank = jnp.sum((same_owner & earlier[None]).astype(jnp.int32), axis=2)
    slots = jnp.arange(MOWN, dtype=jnp.int32)
    in_slot = slot_rank[:, :, None] == slots
    local_block = jnp.sum(
        ((owners == shard_index)[:, :, None] & in_slot) * (vertical % blocks_dev)[:, :, None],
        axis=1,
    )
    steps = 2 * jnp.arange(shard_count // 2, dtype=jnp.int32)
    array_owner = jnp.concatenate([shard_index - steps, partner - steps])
    array_owner = jnp.where(array_owner <= shard_index, array_owner, -1)
    here = (array_owner[:, None, None] == owners)[:, :, :, None] & in_slot[None]
    place = jnp.sum(here * (order + 1)[None, None, :, None], axis=2) - 1
    source = jnp.where(owners <= shard_index, 0, -1).astype(jnp.int32)

    slash_rank = jnp.sum((slash[:, None, :] < slash[:, :, None]).astype(jnp.int32), axis=2)
    at_rank = slash_rank[:, :, None] == jnp.arange(NS, dtype=jnp.int32)
    slash = jnp.sum(at_rank * slash[:, :, None], axis=1)

    global_blocks = shard_index * blocks_dev + jnp.arange(blocks_dev, dtype=jnp.int32)
    vert_valid = vertical[:, None, :] < global_blocks[None, :, None]
    slash_blocks = global_blocks[None, :, None] - slash[:, None, :]
    in_vertical = jnp.any(slash_blocks[:, :, :, None] == vertical[:, None, None, :], axis=3)
    slash_valid = (slash[:, None, :] == 0) | ((slash_blocks >= 0) & jnp.logical_not(in_vertical))
    valid = jnp.concatenate([vert_valid, slash_valid], axis=2)
    bias = jnp.repeat(jnp.where(valid, 0.0, NEG).astype(jnp.float32), BLK, axis=2)

    windows = []
    after = []
    for head in range(kv_local):
        behind = [owned_slots(head, local_block, keys, values, after)]
        own, chunks = pair_of(head, keys, values, behind)
        for distance in range(2, shard_count, 2):
            pairs = [(i, i + distance) for i in range(shard_count - distance)]
            behind.append(lax.ppermute(behind[0], "ctx", pairs))
        two_back = [lax.ppermute(chunk, "ctx", two_pairs) for chunk in chunks]
        odd_back = lax.ppermute(own, "ctx", even_to_odd)
        across = lax.ppermute(jnp.concatenate(behind), "ctx", even_to_odd + odd_to_even)
        even_back = [lax.ppermute(piece, "ctx", odd_to_even) for piece in two_back]
        vert = listed_blocks(head, place, source, behind, across)
        windows.append((vert, own, two_back, even_back, odd_back))
        after = two_back + even_back[:-1]

    parity = (shard_index % 2).reshape(1).astype(jnp.int32)
    out = jnp.zeros((part_rows, head_count * kv_local * group_cols), jnp.bfloat16)
    half = head_count // 2
    after = []
    for head in range(kv_local):
        vert, own, two_back, even_back, odd_back = windows[head]
        calls = [range(head_count - 1, half - 1, -1), range(half - 1, -1, -1)]
        if head + 1 == kv_local:
            calls = [range(f, f - 1, -1) for f in calls[0]] + calls[1:]
        for flips in calls:
            others = [head_index ^ flip for flip in flips]
            pieces = attend(
                head, jnp.stack(others).astype(jnp.int32), parity, slash, bias[head], queries,
                vert, own, two_back, even_back, odd_back, part_rows, after,
            )
            after = [pieces[-1]]
            for flip, other, piece in zip(flips, others, pieces):
                if flip:
                    piece = lax.ppermute(piece, "head", [(i, i ^ flip) for i in range(head_count)])
                out = lax.dynamic_update_slice(
                    out, piece, (0, other * kv_local * group_cols + head * group_cols)
                )
    return out


def solution(mesh):
    in_specs = (
        P("ctx", "head"),
        P("ctx", "head"),
        P("ctx", "head"),
        P("head", None),
        P("head", None),
    )
    out_specs = P(("ctx", "head"), None)
    return jax.shard_map(local, mesh=mesh, in_specs=in_specs, out_specs=out_specs, check_vma=False)
```

```python
import functools
import math

import jax
import jax.numpy as jnp
from jax import lax
from jax.experimental import pallas as pl
from jax.experimental.pallas import tpu as pltpu
from jax.sharding import PartitionSpec as P

HD = 128
BLK = 64
NV = 16
NS = 8
MOWN = 4
LOOK = 2
NEG = -1e30
STEP_BLOCKS = 2
CHUNKS = 2
TILE = 256
ANY = pl.BlockSpec(memory_space=pl.ANY)
SMEM = pl.BlockSpec(memory_space=pltpu.SMEM)


def blocks_at(index, count=1):
    return pl.ds(pl.multiple_of(index * BLK, BLK), count * BLK)


def slots_kernel(local_ref, keys_ref, values_ref, out_ref, sem):
    copies = []
    for head in range(local_ref.shape[0]):
        for slot in range(MOWN):
            for side, source in enumerate((keys_ref, values_ref)):
                copies.append(
                    pltpu.make_async_copy(
                        source.at[blocks_at(local_ref[head, slot]), pl.ds(head * HD, HD)],
                        out_ref.at[
                            pl.ds((head * MOWN + slot) * BLK, BLK), pl.ds(side * HD, HD)
                        ],
                        sem.at[len(copies)],
                    )
                )
    for copy in copies:
        copy.start()
    for copy in copies:
        copy.wait()


def owned_slots(local_block, keys, values):
    heads = local_block.shape[0]
    return pl.pallas_call(
        slots_kernel,
        out_shape=jax.ShapeDtypeStruct((heads * MOWN * BLK, 2 * HD), keys.dtype),
        in_specs=[SMEM, ANY, ANY],
        out_specs=ANY,
        scratch_shapes=[pltpu.SemaphoreType.DMA((heads * MOWN * 2,))],
        compiler_params=pltpu.CompilerParams(vmem_limit_bytes=1 << 20),
        cost_estimate=pl.CostEstimate(
            flops=0, bytes_accessed=8 * heads * MOWN * BLK * HD, transcendentals=0
        ),
    )(local_block, keys, values)


def pair_kernel(head, count, keys_ref, values_ref, *rest):
    out_refs, sem = rest[-2 - count : -1], rest[-1]
    whole, chunks = out_refs[0], out_refs[1:]
    copies = []
    for side, source in enumerate((keys_ref, values_ref)):
        columns, to = pl.ds(head * HD, HD), pl.ds(side * HD, HD)
        for index, chunk in enumerate(chunks):
            rows = pl.ds(index * chunk.shape[0], chunk.shape[0])
            copies.append((source.at[rows, columns], chunk.at[:, to]))
        copies.append((source.at[:, columns], whole.at[:, to]))
    copies = [pltpu.make_async_copy(*ends, sem.at[k]) for k, ends in enumerate(copies)]
    for copy in copies:
        copy.start()
    for copy in copies:
        copy.wait()


def pair_of(head, count, keys, values, after):
    rows = keys.shape[0]
    whole, *chunks = pl.pallas_call(
        functools.partial(pair_kernel, head, count),
        out_shape=[jax.ShapeDtypeStruct((rows, 2 * HD), keys.dtype)]
        + [jax.ShapeDtypeStruct((rows // count, 2 * HD), keys.dtype)] * count,
        in_specs=[ANY] * (2 + len(after)),
        out_specs=[ANY] * (1 + count),
        scratch_shapes=[pltpu.SemaphoreType.DMA((2 + 2 * count,))],
        compiler_params=pltpu.CompilerParams(vmem_limit_bytes=1 << 20),
        cost_estimate=pl.CostEstimate(flops=0, bytes_accessed=16 * rows * HD, transcendentals=0),
    )(keys, values, *after)
    return whole, chunks


def listed_kernel(head, place_ref, source_ref, behind_refs, across_ref, out_ref, sem):
    count = len(behind_refs)
    heads = place_ref.shape[1]
    for index in range(2 * count):
        for slot in range(MOWN):
            place = place_ref[index, head, slot]
            if index < count:
                found = behind_refs[index].at[pl.ds((head * MOWN + slot) * BLK, BLK)]
            else:
                first = ((index - count) * heads + head) * MOWN + slot
                found = across_ref.at[pl.ds(first * BLK, BLK)]

            @pl.when(place >= 0)
            def _():
                pltpu.make_async_copy(found, out_ref.at[blocks_at(place)], sem).start()

    for entry in range(NV):

        @pl.when(source_ref[head, entry] < 0)
        def _():
            pltpu.make_async_copy(
                behind_refs[0].at[pl.ds(0, BLK)], out_ref.at[pl.ds(entry * BLK, BLK)], sem
            ).start()

    pltpu.make_async_copy(out_ref, out_ref, sem).wait()


def listed_blocks(head, place, source, behind, across):
    return pl.pallas_call(
        functools.partial(listed_kernel, head),
        out_shape=jax.ShapeDtypeStruct((NV * BLK, 2 * HD), across.dtype),
        in_specs=[SMEM, SMEM, [ANY] * len(behind), ANY],
        out_specs=ANY,
        scratch_shapes=[pltpu.SemaphoreType.DMA],
        compiler_params=pltpu.CompilerParams(vmem_limit_bytes=1 << 20),
        cost_estimate=pl.CostEstimate(flops=0, bytes_accessed=8 * NV * BLK * HD, transcendentals=0),
    )(place, source, behind, across)


def attend_kernel(
    head, parts, chunks, waits, part_blocks, group_heads, part_ref, parity_ref, slash_ref, bias_ref, query_ref,
    vert_ref, own_ref, *rest,
):
    two_back = rest[:chunks]
    even_back = rest[chunks : 2 * chunks]
    odd_back = rest[2 * chunks]
    rest = rest[2 * chunks + 1 + waits :]
    out_refs = rest[:parts]
    (
        queries, out, vert, vert_keys, window, scores_a, scores_b, weights_a, weights_b, max_a,
        max_b, diagonal_ref, query_sem, vert_sem, window_sem, out_sem,
    ) = rest[parts:]
    scores, weights, maxima = (scores_a, scores_b), (weights_a, weights_b), (max_a, max_b)
    tok_rows = own_ref.shape[0]
    blocks_dev = tok_rows // BLK
    part_rows = part_blocks * BLK
    group_cols = group_heads * HD
    chunk_rows = tok_rows // chunks
    last = parts * part_blocks - 1
    step = pl.program_id(0)
    scale = 1.0 / math.sqrt(HD)
    contract = (((1,), (1,)), ((), ()))

    def shard_block(block):
        return part_ref[block // part_blocks] * part_blocks + lax.rem(block, part_blocks)

    def slash_rows(block):
        first = LOOK * blocks_dev + shard_block(block)
        return [blocks_at(first - slash_ref[head, entry]) for entry in range(NS)]

    def query_of(block):
        rows = blocks_at(block)
        return jnp.concatenate(
            [queries[rows, h * HD : (h + 1) * HD] for h in range(group_heads)], axis=0
        )

    def score_tile(query, bias, rows, tile):
        low = tile * TILE
        if low < NV * BLK:
            found = jnp.dot(
                query, vert_keys[:, low : low + TILE], preferred_element_type=jnp.float32
            )
        else:
            entry = (low - NV * BLK) // BLK
            keys = jnp.concatenate(
                [window[r, :HD] for r in rows[entry : entry + TILE // BLK]], axis=0
            )
            found = lax.dot_general(query, keys, contract, preferred_element_type=jnp.float32)
        found = found + bias[:, low : low + TILE]
        if low == NV * BLK:
            diagonal = jnp.concatenate([diagonal_ref[...]] * group_heads, axis=0)
            found = jnp.concatenate(
                [found[:, : 2 * BLK] + diagonal, found[:, 2 * BLK :]], axis=1
            )
        return found

    def weighted_values(block, at):
        ones = jnp.ones(((NV + NS) * BLK, HD), jnp.bfloat16)
        values = jnp.concatenate([vert[:, HD:]] + [window[r, HD:] for r in slash_rows(block)], axis=0)
        return jnp.dot(
            weights[at][...],
            jnp.concatenate([values, ones], axis=1),
            preferred_element_type=jnp.float32,
        )

    def store(total, block):
        result = (total[:, :HD] / total[:, HD:]).astype(jnp.bfloat16)
        rows = blocks_at(block)
        for h in range(group_heads):
            out[rows, h * HD : (h + 1) * HD] = result[h * BLK : (h + 1) * BLK]

    def stage(block, at, score, weigh, combine):
        other = 1 - at
        if score:
            fresh = jnp.minimum(block, last)
            query = query_of(fresh)
            rows = slash_rows(fresh)
            bias = bias_ref[pl.ds(shard_block(fresh), 1), :]
        if combine:
            done = jnp.maximum(block - 2, 0)
            total = weighted_values(done, at)
        if weigh:
            row_max = maxima[other][...]
            row_max = jnp.concatenate([row_max] * (TILE // HD), axis=1)
        highest = None
        for tile in range((NV + NS) * BLK // TILE):
            low = tile * TILE
            if score:
                found = score_tile(query, bias, rows, tile)
                scores[at][:, low : low + TILE] = found
                for piece_low in range(0, TILE, HD):
                    piece = found[:, piece_low : piece_low + HD]
                    highest = piece if highest is None else jnp.maximum(highest, piece)
            if weigh:
                weights[other][:, low : low + TILE] = jnp.exp(
                    (scores[other][:, low : low + TILE] - row_max) * scale
                ).astype(jnp.bfloat16)
        if score:
            maxima[at][...] = jnp.broadcast_to(
                jnp.max(highest, axis=1, keepdims=True), highest.shape
            )
        if combine:
            store(total, done)

    @pl.when(step == 0)
    def _():
        for k in range(parts):
            pltpu.make_async_copy(
                query_ref.at[
                    pl.ds(pl.multiple_of(part_ref[k] * part_rows, part_rows), part_rows),
                    pl.ds(head * group_cols, group_cols),
                ],
                queries.at[pl.ds(k * part_rows, part_rows)],
                query_sem,
            ).start()
        pltpu.make_async_copy(vert_ref, vert, vert_sem).start()
        for chunk in range(chunks):
            pltpu.make_async_copy(
                two_back[chunk], window.at[pl.ds(chunk * chunk_rows, chunk_rows)], window_sem
            ).start()

        @pl.when(parity_ref[0] == 1)
        def _():
            pltpu.make_async_copy(
                odd_back, window.at[pl.ds(tok_rows, tok_rows)], window_sem
            ).start()

        @pl.when(parity_ref[0] == 0)
        def _():
            for chunk in range(chunks):
                pltpu.make_async_copy(
                    even_back[chunk],
                    window.at[pl.ds(tok_rows + chunk * chunk_rows, chunk_rows)],
                    window_sem,
                ).start()

        pltpu.make_async_copy(
            own_ref, window.at[pl.ds(LOOK * tok_rows, tok_rows)], window_sem
        ).start()
        column = lax.broadcasted_iota(jnp.int32, (BLK, 2 * BLK), 1)
        row = lax.broadcasted_iota(jnp.int32, (BLK, 2 * BLK), 0)
        diagonal_ref[...] = jnp.where((column < BLK) & (column > row), NEG, 0.0).astype(jnp.float32)
        weights_b[...] = jnp.zeros_like(weights_b)
        pltpu.make_async_copy(vert, vert, vert_sem).wait()
        vert_keys[...] = vert[:, :HD].T
        pltpu.make_async_copy(queries, queries, query_sem).wait()
        pltpu.make_async_copy(window, window, window_sem).wait()
        stage(0, 0, True, False, False)

    first = step * STEP_BLOCKS
    stage(first + 1, 1, True, True, True)
    stage(first + 2, 0, True, True, True)

    @pl.when(first + STEP_BLOCKS > last)
    def _():
        store(weighted_values(last, 1), last)
        for k in range(parts):
            pltpu.make_async_copy(
                out.at[pl.ds(k * part_rows, part_rows)], out_refs[k], out_sem.at[k]
            ).start()
        for k in range(parts):
            pltpu.make_async_copy(
                out.at[pl.ds(k * part_rows, part_rows)], out_refs[k], out_sem.at[k]
            ).wait()


def attend(head, part, parity, slash, bias, queries, vert, own, two_back, even_back, odd_back,
           part_rows, after):
    parts = part.shape[0]
    group_cols = queries.shape[1] // slash.shape[0]
    group_heads = group_cols // HD
    part_blocks = part_rows // BLK
    tok_rows = own.shape[0]
    rows = group_heads * BLK
    keys_seen = (NV + NS) * BLK
    return pl.pallas_call(
        functools.partial(
            attend_kernel, head, parts, len(two_back), len(after), part_blocks, group_heads
        ),
        out_shape=[jax.ShapeDtypeStruct((part_rows, group_cols), jnp.bfloat16)] * parts,
        grid_spec=pltpu.PrefetchScalarGridSpec(
            num_scalar_prefetch=3,
            grid=(parts * part_blocks // STEP_BLOCKS,),
            in_specs=[pl.BlockSpec(bias.shape, lambda s, *_: (0, 0))] + [ANY] * (4 + 2 * len(two_back) + len(after)),
            out_specs=[ANY] * parts,
            scratch_shapes=[
                pltpu.VMEM((parts * part_rows, group_cols), jnp.bfloat16),
                pltpu.VMEM((parts * part_rows, group_cols), jnp.bfloat16),
                pltpu.VMEM((NV * BLK, 2 * HD), jnp.bfloat16),
                pltpu.VMEM((HD, NV * BLK), jnp.bfloat16),
                pltpu.VMEM(((LOOK + 1) * tok_rows, 2 * HD), jnp.bfloat16),
                pltpu.VMEM((rows, keys_seen), jnp.float32),
                pltpu.VMEM((rows, keys_seen), jnp.float32),
                pltpu.VMEM((rows, keys_seen), jnp.bfloat16),
                pltpu.VMEM((rows, keys_seen), jnp.bfloat16),
                pltpu.VMEM((rows, HD), jnp.float32),
                pltpu.VMEM((rows, HD), jnp.float32),
                pltpu.VMEM((BLK, 2 * BLK), jnp.float32),
                pltpu.SemaphoreType.DMA,
                pltpu.SemaphoreType.DMA,
                pltpu.SemaphoreType.DMA,
                pltpu.SemaphoreType.DMA((parts,)),
            ],
        ),
        compiler_params=pltpu.CompilerParams(
            dimension_semantics=("arbitrary",), vmem_limit_bytes=32 << 20
        ),
        cost_estimate=pl.CostEstimate(
            flops=4 * parts * part_rows * group_heads * keys_seen * HD,
            bytes_accessed=4 * parts * part_rows * group_cols + 12 * tok_rows * HD,
            transcendentals=parts * part_rows * group_heads * keys_seen,
        ),
    )(part, parity, slash, bias, queries, vert, own, *two_back, *even_back, odd_back, *after)


def local(queries, keys, values, vertical, slash):
    shard_count = lax.axis_size("ctx")
    shard_index = lax.axis_index("ctx")
    head_count = lax.axis_size("head")
    head_index = lax.axis_index("head")
    tok_rows = queries.shape[0]
    kv_local = keys.shape[1] // HD
    group_cols = queries.shape[1] // kv_local
    blocks_dev = tok_rows // BLK
    part_rows = tok_rows // head_count
    partner = shard_index ^ 1
    two_pairs = [(i, i + 2) for i in range(shard_count - 2)]
    even_to_odd = [(i, i + 1) for i in range(0, shard_count - 1, 2)]
    odd_to_even = [(i, i - 1) for i in range(1, shard_count, 2)]

    owners = vertical // blocks_dev
    order = jnp.arange(NV, dtype=jnp.int32)
    same_owner = owners[:, :, None] == owners[:, None, :]
    earlier = order[None, :] < order[:, None]
    slot_rank = jnp.sum((same_owner & earlier[None]).astype(jnp.int32), axis=2)
    slots = jnp.arange(MOWN, dtype=jnp.int32)
    in_slot = slot_rank[:, :, None] == slots
    local_block = jnp.sum(
        ((owners == shard_index)[:, :, None] & in_slot) * (vertical % blocks_dev)[:, :, None],
        axis=1,
    )
    steps = 2 * jnp.arange(shard_count // 2, dtype=jnp.int32)
    array_owner = jnp.concatenate([shard_index - steps, partner - steps])
    array_owner = jnp.where(array_owner <= shard_index, array_owner, -1)
    here = (array_owner[:, None, None] == owners)[:, :, :, None] & in_slot[None]
    place = jnp.sum(here * (order + 1)[None, None, :, None], axis=2) - 1
    source = jnp.where(owners <= shard_index, 0, -1).astype(jnp.int32)

    slash_rank = jnp.sum((slash[:, None, :] < slash[:, :, None]).astype(jnp.int32), axis=2)
    at_rank = slash_rank[:, :, None] == jnp.arange(NS, dtype=jnp.int32)
    slash = jnp.sum(at_rank * slash[:, :, None], axis=1)

    global_blocks = shard_index * blocks_dev + jnp.arange(blocks_dev, dtype=jnp.int32)
    vert_valid = vertical[:, None, :] < global_blocks[None, :, None]
    slash_blocks = global_blocks[None, :, None] - slash[:, None, :]
    in_vertical = jnp.any(slash_blocks[:, :, :, None] == vertical[:, None, None, :], axis=3)
    slash_valid = (slash[:, None, :] == 0) | ((slash_blocks >= 0) & jnp.logical_not(in_vertical))
    valid = jnp.concatenate([vert_valid, slash_valid], axis=2)
    bias = jnp.repeat(jnp.where(valid, 0.0, NEG).astype(jnp.float32), BLK, axis=2)

    behind = [owned_slots(local_block, keys, values)]
    for distance in range(2, shard_count, 2):
        pairs = [(i, i + distance) for i in range(shard_count - distance)]
        behind.append(lax.ppermute(behind[0], "ctx", pairs))
    across = lax.ppermute(jnp.concatenate(behind), "ctx", even_to_odd + odd_to_even)

    windows = []
    after = [behind[1]]
    for head in range(kv_local):
        own, chunks = pair_of(head, CHUNKS if head == 0 else 1, keys, values, after)
        two_back = [lax.ppermute(chunk, "ctx", two_pairs) for chunk in chunks]
        odd_back = lax.ppermute(own, "ctx", even_to_odd)
        even_back = [lax.ppermute(piece, "ctx", odd_to_even) for piece in two_back]
        vert = listed_blocks(head, place, source, behind, across)
        windows.append((vert, own, two_back, even_back, odd_back))
        after = two_back[-1:]

    parity = (shard_index % 2).reshape(1).astype(jnp.int32)
    out = jnp.zeros((part_rows, head_count * kv_local * group_cols), jnp.bfloat16)
    after = []
    for head in range(kv_local):
        vert, own, two_back, even_back, odd_back = windows[head]
        for flip in range(head_count - 1, -1, -1):
            flips = [flip]
            others = [head_index ^ flip for flip in flips]
            pieces = attend(
                head, jnp.stack(others).astype(jnp.int32), parity, slash, bias[head], queries,
                vert, own, two_back, even_back, odd_back, part_rows, after,
            )
            after = [pieces[-1]]
            for flip, other, piece in zip(flips, others, pieces):
                if flip:
                    piece = lax.ppermute(piece, "head", [(i, i ^ flip) for i in range(head_count)])
                out = lax.dynamic_update_slice(
                    out, piece, (0, other * kv_local * group_cols + head * group_cols)
                )
    return out


def solution(mesh):
    in_specs = (
        P("ctx", "head"),
        P("ctx", "head"),
        P("ctx", "head"),
        P("head", None),
        P("head", None),
    )
    out_specs = P(("ctx", "head"), None)
    return jax.shard_map(local, mesh=mesh, in_specs=in_specs, out_specs=out_specs, check_vma=False)
```

```python
import functools
import math

import jax
import jax.numpy as jnp
from jax import lax
from jax.experimental import pallas as pl
from jax.experimental.pallas import tpu as pltpu
from jax.sharding import PartitionSpec as P

HD = 128
BLK = 64
NV = 16
NS = 8
MOWN = 4
LOOK = 2
NEG = -1e30
STEP_BLOCKS = 2
TILE = 256
ANY = pl.BlockSpec(memory_space=pl.ANY)
SMEM = pl.BlockSpec(memory_space=pltpu.SMEM)


def blocks_at(index, count=1):
    return pl.ds(pl.multiple_of(index * BLK, BLK), count * BLK)


def run_all(copies, sem):
    copies = [pltpu.make_async_copy(*ends, sem.at[k]) for k, ends in enumerate(copies)]
    for copy in copies:
        copy.start()
    for copy in copies:
        copy.wait()


def first_kernel(local_ref, keys_ref, values_ref, own_ref, send_ref, slots_ref, sem):
    chunk_rows = send_ref.shape[0] - slots_ref.shape[0]
    copies = []
    for side, source in enumerate((keys_ref, values_ref)):
        to = pl.ds(side * HD, HD)
        for head in range(local_ref.shape[0]):
            for slot in range(MOWN):
                found = source.at[blocks_at(local_ref[head, slot]), pl.ds(head * HD, HD)]
                low = (head * MOWN + slot) * BLK
                copies.append((found, send_ref.at[pl.ds(chunk_rows + low, BLK), to]))
                copies.append((found, slots_ref.at[pl.ds(low, BLK), to]))
        rows = pl.ds(0, chunk_rows)
        copies.append((source.at[rows, pl.ds(0, HD)], send_ref.at[rows, to]))
        copies.append((source.at[:, pl.ds(0, HD)], own_ref.at[:, to]))
    run_all(copies, sem)


def first_of(chunk_rows, local_block, keys, values):
    heads = local_block.shape[0]
    rows = keys.shape[0]
    slot_rows = heads * MOWN * BLK
    return pl.pallas_call(
        first_kernel,
        out_shape=[
            jax.ShapeDtypeStruct((rows, 2 * HD), keys.dtype),
            jax.ShapeDtypeStruct((chunk_rows + slot_rows, 2 * HD), keys.dtype),
            jax.ShapeDtypeStruct((slot_rows, 2 * HD), keys.dtype),
        ],
        in_specs=[SMEM, ANY, ANY],
        out_specs=[ANY] * 3,
        scratch_shapes=[pltpu.SemaphoreType.DMA((4 * heads * MOWN + 4,))],
        compiler_params=pltpu.CompilerParams(vmem_limit_bytes=1 << 20),
        cost_estimate=pl.CostEstimate(flops=0, bytes_accessed=16 * rows * HD, transcendentals=0),
    )(local_block, keys, values)


def pair_kernel(head, keys_ref, values_ref, *rest):
    out_ref, sem = rest[-2:]
    run_all(
        [
            (source.at[:, pl.ds(head * HD, HD)], out_ref.at[:, pl.ds(side * HD, HD)])
            for side, source in enumerate((keys_ref, values_ref))
        ],
        sem,
    )


def pair_of(head, keys, values, after):
    rows = keys.shape[0]
    return pl.pallas_call(
        functools.partial(pair_kernel, head),
        out_shape=jax.ShapeDtypeStruct((rows, 2 * HD), keys.dtype),
        in_specs=[ANY] * (2 + len(after)),
        out_specs=ANY,
        scratch_shapes=[pltpu.SemaphoreType.DMA((2,))],
        compiler_params=pltpu.CompilerParams(vmem_limit_bytes=1 << 20),
        cost_estimate=pl.CostEstimate(flops=0, bytes_accessed=8 * rows * HD, transcendentals=0),
    )(keys, values, *after)


def joined_kernel(pieces, parity_ref, *rest):
    refs, out_ref, sem = rest[:-2], rest[-2], rest[-1]
    to = 0
    for rows, even, odd in pieces:
        for value, (index, low) in enumerate((even, odd)):

            @pl.when(parity_ref[0] == value)
            def _():
                pltpu.make_async_copy(
                    refs[index].at[pl.ds(low, rows)], out_ref.at[pl.ds(to, rows)], sem
                ).start()

        to += rows
    pltpu.make_async_copy(out_ref, out_ref, sem).wait()


def joined(parity, pieces, after=()):
    arrays = []
    plan = []
    for rows, *sources in pieces:
        found = []
        for array, low in sources:
            at = [k for k, known in enumerate(arrays) if known is array]
            if not at:
                at = [len(arrays)]
                arrays.append(array)
            found.append((at[0], low))
        plan.append((rows, *found))
    total = sum(rows for rows, *_ in plan)
    return pl.pallas_call(
        functools.partial(joined_kernel, plan),
        out_shape=jax.ShapeDtypeStruct((total, 2 * HD), jnp.bfloat16),
        in_specs=[SMEM] + [ANY] * (len(arrays) + len(after)),
        out_specs=ANY,
        scratch_shapes=[pltpu.SemaphoreType.DMA],
        compiler_params=pltpu.CompilerParams(vmem_limit_bytes=1 << 20),
        cost_estimate=pl.CostEstimate(flops=0, bytes_accessed=8 * total * HD, transcendentals=0),
    )(parity, *arrays, *after)


def listed_kernel(head, lows, place_ref, source_ref, *rest):
    refs, out_ref, sem = rest[:-2], rest[-2], rest[-1]

    def block(index, slot):
        return refs[index].at[pl.ds(lows[index] + (head * MOWN + slot) * BLK, BLK)]

    for index in range(len(refs)):
        for slot in range(MOWN):
            place = place_ref[index, head, slot]

            @pl.when(place >= 0)
            def _():
                pltpu.make_async_copy(block(index, slot), out_ref.at[blocks_at(place)], sem).start()

    for entry in range(NV):

        @pl.when(source_ref[head, entry] < 0)
        def _():
            pltpu.make_async_copy(
                block(0, 0), out_ref.at[pl.ds(entry * BLK, BLK)], sem
            ).start()

    pltpu.make_async_copy(out_ref, out_ref, sem).wait()


def listed_blocks(head, place, source, slots):
    return pl.pallas_call(
        functools.partial(listed_kernel, head, [low for _, low in slots]),
        out_shape=jax.ShapeDtypeStruct((NV * BLK, 2 * HD), jnp.bfloat16),
        in_specs=[SMEM, SMEM] + [ANY] * len(slots),
        out_specs=ANY,
        scratch_shapes=[pltpu.SemaphoreType.DMA],
        compiler_params=pltpu.CompilerParams(vmem_limit_bytes=1 << 20),
        cost_estimate=pl.CostEstimate(flops=0, bytes_accessed=8 * NV * BLK * HD, transcendentals=0),
    )(place, source, *[array for array, _ in slots])


def attend_kernel(
    head, parts, bounds, waits, part_blocks, group_heads, part_ref, slash_ref, bias_ref, query_ref,
    vert_ref, own_ref, *rest,
):
    chunks = len(bounds) - 1
    two_back = rest[:chunks]
    one_back = rest[chunks : 2 * chunks]
    rest = rest[2 * chunks + waits :]
    out_refs = rest[:parts]
    (
        queries, out, vert, vert_keys, window, scores_a, scores_b, weights_a, weights_b, max_a,
        max_b, diagonal_ref, query_sem, vert_sem, window_sem, out_sem,
    ) = rest[parts:]
    scores, weights, maxima = (scores_a, scores_b), (weights_a, weights_b), (max_a, max_b)
    tok_rows = own_ref.shape[0]
    blocks_dev = tok_rows // BLK
    part_rows = part_blocks * BLK
    group_cols = group_heads * HD
    last = parts * part_blocks - 1
    step = pl.program_id(0)
    scale = 1.0 / math.sqrt(HD)
    contract = (((1,), (1,)), ((), ()))

    def shard_block(block):
        return part_ref[block // part_blocks] * part_blocks + lax.rem(block, part_blocks)

    def slash_rows(block):
        first = LOOK * blocks_dev + shard_block(block)
        return [blocks_at(first - slash_ref[head, entry]) for entry in range(NS)]

    def query_of(block):
        rows = blocks_at(block)
        return jnp.concatenate(
            [queries[rows, h * HD : (h + 1) * HD] for h in range(group_heads)], axis=0
        )

    def score_tile(query, bias, rows, tile):
        low = tile * TILE
        if low < NV * BLK:
            found = jnp.dot(
                query, vert_keys[:, low : low + TILE], preferred_element_type=jnp.float32
            )
        else:
            entry = (low - NV * BLK) // BLK
            keys = jnp.concatenate(
                [window[r, :HD] for r in rows[entry : entry + TILE // BLK]], axis=0
            )
            found = lax.dot_general(query, keys, contract, preferred_element_type=jnp.float32)
        found = found + bias[:, low : low + TILE]
        if low == NV * BLK:
            diagonal = jnp.concatenate([diagonal_ref[...]] * group_heads, axis=0)
            found = jnp.concatenate(
                [found[:, : 2 * BLK] + diagonal, found[:, 2 * BLK :]], axis=1
            )
        return found

    def weighted_values(block, at):
        ones = jnp.ones(((NV + NS) * BLK, HD), jnp.bfloat16)
        values = jnp.concatenate([vert[:, HD:]] + [window[r, HD:] for r in slash_rows(block)], axis=0)
        return jnp.dot(
            weights[at][...],
            jnp.concatenate([values, ones], axis=1),
            preferred_element_type=jnp.float32,
        )

    def store(total, block):
        result = (total[:, :HD] / total[:, HD:]).astype(jnp.bfloat16)
        rows = blocks_at(block)
        for h in range(group_heads):
            out[rows, h * HD : (h + 1) * HD] = result[h * BLK : (h + 1) * BLK]

    def stage(block, at, score, weigh, combine):
        other = 1 - at
        if score:
            fresh = jnp.minimum(block, last)
            query = query_of(fresh)
            rows = slash_rows(fresh)
            bias = bias_ref[pl.ds(shard_block(fresh), 1), :]
        if combine:
            done = jnp.maximum(block - 2, 0)
            total = weighted_values(done, at)
        if weigh:
            row_max = maxima[other][...]
            row_max = jnp.concatenate([row_max] * (TILE // HD), axis=1)
        highest = None
        for tile in range((NV + NS) * BLK // TILE):
            low = tile * TILE
            if score:
                found = score_tile(query, bias, rows, tile)
                scores[at][:, low : low + TILE] = found
                for piece_low in range(0, TILE, HD):
                    piece = found[:, piece_low : piece_low + HD]
                    highest = piece if highest is None else jnp.maximum(highest, piece)
            if weigh:
                weights[other][:, low : low + TILE] = jnp.exp(
                    (scores[other][:, low : low + TILE] - row_max) * scale
                ).astype(jnp.bfloat16)
        if score:
            maxima[at][...] = jnp.broadcast_to(
                jnp.max(highest, axis=1, keepdims=True), highest.shape
            )
        if combine:
            store(total, done)

    @pl.when(step == 0)
    def _():
        for k in range(parts):
            pltpu.make_async_copy(
                query_ref.at[
                    pl.ds(pl.multiple_of(part_ref[k] * part_rows, part_rows), part_rows),
                    pl.ds(head * group_cols, group_cols),
                ],
                queries.at[pl.ds(k * part_rows, part_rows)],
                query_sem,
            ).start()
        pltpu.make_async_copy(vert_ref, vert, vert_sem).start()
        for back, sources in enumerate((two_back, one_back)):
            for chunk, source in enumerate(sources):
                rows = bounds[chunk + 1] - bounds[chunk]
                pltpu.make_async_copy(
                    source.at[pl.ds(0, rows)],
                    window.at[pl.ds(back * tok_rows + bounds[chunk], rows)],
                    window_sem,
                ).start()
        pltpu.make_async_copy(
            own_ref, window.at[pl.ds(LOOK * tok_rows, tok_rows)], window_sem
        ).start()
        column = lax.broadcasted_iota(jnp.int32, (BLK, 2 * BLK), 1)
        row = lax.broadcasted_iota(jnp.int32, (BLK, 2 * BLK), 0)
        diagonal_ref[...] = jnp.where((column < BLK) & (column > row), NEG, 0.0).astype(jnp.float32)
        weights_b[...] = jnp.zeros_like(weights_b)
        pltpu.make_async_copy(vert, vert, vert_sem).wait()
        vert_keys[...] = vert[:, :HD].T
        pltpu.make_async_copy(queries, queries, query_sem).wait()
        pltpu.make_async_copy(window, window, window_sem).wait()
        stage(0, 0, True, False, False)

    first = step * STEP_BLOCKS
    stage(first + 1, 1, True, True, True)
    stage(first + 2, 0, True, True, True)

    @pl.when(first + STEP_BLOCKS > last)
    def _():
        store(weighted_values(last, 1), last)
        for k in range(parts):
            pltpu.make_async_copy(
                out.at[pl.ds(k * part_rows, part_rows)], out_refs[k], out_sem.at[k]
            ).start()
        for k in range(parts):
            pltpu.make_async_copy(
                out.at[pl.ds(k * part_rows, part_rows)], out_refs[k], out_sem.at[k]
            ).wait()


def attend(head, part, bounds, slash, bias, queries, vert, own, two_back, one_back, part_rows, after):
    parts = part.shape[0]
    group_cols = queries.shape[1] // slash.shape[0]
    group_heads = group_cols // HD
    part_blocks = part_rows // BLK
    tok_rows = own.shape[0]
    rows = group_heads * BLK
    keys_seen = (NV + NS) * BLK
    return pl.pallas_call(
        functools.partial(
            attend_kernel, head, parts, bounds, len(after), part_blocks, group_heads
        ),
        out_shape=[jax.ShapeDtypeStruct((part_rows, group_cols), jnp.bfloat16)] * parts,
        grid_spec=pltpu.PrefetchScalarGridSpec(
            num_scalar_prefetch=2,
            grid=(parts * part_blocks // STEP_BLOCKS,),
            in_specs=[pl.BlockSpec(bias.shape, lambda s, *_: (0, 0))] + [ANY] * (3 + 2 * len(two_back) + len(after)),
            out_specs=[ANY] * parts,
            scratch_shapes=[
                pltpu.VMEM((parts * part_rows, group_cols), jnp.bfloat16),
                pltpu.VMEM((parts * part_rows, group_cols), jnp.bfloat16),
                pltpu.VMEM((NV * BLK, 2 * HD), jnp.bfloat16),
                pltpu.VMEM((HD, NV * BLK), jnp.bfloat16),
                pltpu.VMEM(((LOOK + 1) * tok_rows, 2 * HD), jnp.bfloat16),
                pltpu.VMEM((rows, keys_seen), jnp.float32),
                pltpu.VMEM((rows, keys_seen), jnp.float32),
                pltpu.VMEM((rows, keys_seen), jnp.bfloat16),
                pltpu.VMEM((rows, keys_seen), jnp.bfloat16),
                pltpu.VMEM((rows, HD), jnp.float32),
                pltpu.VMEM((rows, HD), jnp.float32),
                pltpu.VMEM((BLK, 2 * BLK), jnp.float32),
                pltpu.SemaphoreType.DMA,
                pltpu.SemaphoreType.DMA,
                pltpu.SemaphoreType.DMA,
                pltpu.SemaphoreType.DMA((parts,)),
            ],
        ),
        compiler_params=pltpu.CompilerParams(
            dimension_semantics=("arbitrary",), vmem_limit_bytes=24 << 20
        ),
        cost_estimate=pl.CostEstimate(
            flops=4 * parts * part_rows * group_heads * keys_seen * HD,
            bytes_accessed=4 * parts * part_rows * group_cols + 12 * tok_rows * HD,
            transcendentals=parts * part_rows * group_heads * keys_seen,
        ),
    )(part, slash, bias, queries, vert, own, *two_back, *one_back, *after)


def local(queries, keys, values, vertical, slash):
    shard_count = lax.axis_size("ctx")
    shard_index = lax.axis_index("ctx")
    head_count = lax.axis_size("head")
    head_index = lax.axis_index("head")
    tok_rows = queries.shape[0]
    kv_local = keys.shape[1] // HD
    group_cols = queries.shape[1] // kv_local
    blocks_dev = tok_rows // BLK
    part_rows = tok_rows // head_count
    partner = shard_index ^ 1
    two_pairs = [(i, i + 2) for i in range(shard_count - 2)]
    across_pairs = [(i, i ^ 1) for i in range(shard_count)]
    parity = (shard_index % 2).reshape(1).astype(jnp.int32)

    owners = vertical // blocks_dev
    order = jnp.arange(NV, dtype=jnp.int32)
    same_owner = owners[:, :, None] == owners[:, None, :]
    earlier = order[None, :] < order[:, None]
    slot_rank = jnp.sum((same_owner & earlier[None]).astype(jnp.int32), axis=2)
    slots = jnp.arange(MOWN, dtype=jnp.int32)
    in_slot = slot_rank[:, :, None] == slots
    local_block = jnp.sum(
        ((owners == shard_index)[:, :, None] & in_slot) * (vertical % blocks_dev)[:, :, None],
        axis=1,
    )
    distances = 2 * jnp.arange(shard_count // 2, dtype=jnp.int32)
    array_owner = jnp.concatenate([shard_index - distances, partner - distances])
    array_owner = jnp.where(array_owner <= shard_index, array_owner, -1)
    here = (array_owner[:, None, None] == owners)[:, :, :, None] & in_slot[None]
    place = jnp.sum(here * (order + 1)[None, None, :, None], axis=2) - 1
    source = jnp.where(owners <= shard_index, 0, -1).astype(jnp.int32)

    slash_rank = jnp.sum((slash[:, None, :] < slash[:, :, None]).astype(jnp.int32), axis=2)
    at_rank = slash_rank[:, :, None] == jnp.arange(NS, dtype=jnp.int32)
    slash = jnp.sum(at_rank * slash[:, :, None], axis=1)

    global_blocks = shard_index * blocks_dev + jnp.arange(blocks_dev, dtype=jnp.int32)
    vert_valid = vertical[:, None, :] < global_blocks[None, :, None]
    slash_blocks = global_blocks[None, :, None] - slash[:, None, :]
    in_vertical = jnp.any(slash_blocks[:, :, :, None] == vertical[:, None, None, :], axis=3)
    slash_valid = (slash[:, None, :] == 0) | ((slash_blocks >= 0) & jnp.logical_not(in_vertical))
    valid = jnp.concatenate([vert_valid, slash_valid], axis=2)
    bias = jnp.repeat(jnp.where(valid, 0.0, NEG).astype(jnp.float32), BLK, axis=2)

    steps = shard_count // 2 - 1
    bounds = [k * blocks_dev // steps * BLK for k in range(steps + 1)]
    slot_rows = kv_local * MOWN * BLK
    own, send, slots_own = first_of(bounds[1], local_block, keys, values)
    behind = [(slots_own, 0)]
    across = []
    two_back = []
    one_back = []
    for step in range(steps):
        rows = bounds[step + 1] - bounds[step]
        here = (own, bounds[step])
        if step:
            send = joined(
                parity, [(rows, here, here), (slot_rows, behind[-1], behind[-1])],
                [cross] + one_back[-2:-1],
            )
        come = lax.ppermute(send, "ctx", two_pairs)
        if step == 0:
            pairs = [(i, i + 1) for i in range(0, shard_count, 2)]
            across.append((lax.ppermute(slots_own, "ctx", pairs), 0))
        two_back.append(come)
        behind.append((come, rows))
        cross = joined(parity, [(rows, here, (come, 0)), (slot_rows, behind[-1], behind[-1])])
        one_back.append(lax.ppermute(cross, "ctx", across_pairs))
        across.append((one_back[-1], rows))
    slots = behind + across
    windows = [(bounds, own, two_back, one_back)]
    after = two_back[-1:] + one_back[-2:-1]
    for head in range(1, kv_local):
        own = pair_of(head, keys, values, after)
        come = lax.ppermute(own, "ctx", two_pairs)
        windows.append(([0, tok_rows], own, [come], None))
        after = [come]

    out = jnp.zeros((part_rows, head_count * kv_local * group_cols), jnp.bfloat16)
    after = []
    half = head_count // 2
    calls = [[flip] for flip in range(head_count - 1, half - 1, -1)]
    calls.append(list(range(half - 1, -1, -1)))
    for head in range(kv_local):
        bounds, own, two_back, one_back = windows[head]
        vert = listed_blocks(head, place, source, slots)
        for flips in calls:
            others = [head_index ^ flip for flip in flips]
            pieces = attend(
                head, jnp.stack(others).astype(jnp.int32), bounds, slash, bias[head], queries, vert, own,
                two_back, one_back, part_rows, after,
            )
            after = [pieces[-1]]
            if flips == calls[0] and head + 1 < kv_local:
                near, own_next, (come,), _ = windows[head + 1]
                cross = joined(parity, [(tok_rows, (own_next, 0), (come, 0))], after)
                crossed = lax.ppermute(cross, "ctx", across_pairs)
                windows[head + 1] = (near, own_next, [come], [crossed])
            for flip, other, piece in zip(flips, others, pieces):
                if flip:
                    piece = lax.ppermute(piece, "head", [(i, i ^ flip) for i in range(head_count)])
                out = lax.dynamic_update_slice(
                    out, piece, (0, other * kv_local * group_cols + head * group_cols)
                )
    return out


def solution(mesh):
    in_specs = (
        P("ctx", "head"),
        P("ctx", "head"),
        P("ctx", "head"),
        P("head", None),
        P("head", None),
    )
    out_specs = P(("ctx", "head"), None)
    return jax.shard_map(local, mesh=mesh, in_specs=in_specs, out_specs=out_specs, check_vma=False)
```

```python
import functools
import math

import jax
import jax.numpy as jnp
from jax import lax
from jax.experimental import pallas as pl
from jax.experimental.pallas import tpu as pltpu
from jax.sharding import PartitionSpec as P

HD = 128
BLK = 64
NV = 16
NS = 8
MOWN = 4
LOOK = 2
NEG = -1e30
STEP_BLOCKS = 2
TILE = 256
HBM = pl.BlockSpec(memory_space=pltpu.HBM)
VMEM = pl.BlockSpec(memory_space=pltpu.VMEM)
SMEM = pl.BlockSpec(memory_space=pltpu.SMEM)


def blocks_at(index, count=1):
    return pl.ds(pl.multiple_of(index * BLK, BLK), count * BLK)


def run_all(copies, sem):
    copies = [pltpu.make_async_copy(*ends, sem.at[k]) for k, ends in enumerate(copies)]
    for copy in copies:
        copy.start()
    for copy in copies:
        copy.wait()


def first_kernel(local_ref, keys_ref, values_ref, own_ref, send_ref, slots_ref, sem):
    chunk_rows = send_ref.shape[0] - slots_ref.shape[0]
    copies = []
    for side, source in enumerate((keys_ref, values_ref)):
        to = pl.ds(side * HD, HD)
        for head in range(local_ref.shape[0]):
            for slot in range(MOWN):
                found = source.at[blocks_at(local_ref[head, slot]), pl.ds(head * HD, HD)]
                low = (head * MOWN + slot) * BLK
                copies.append((found, send_ref.at[pl.ds(chunk_rows + low, BLK), to]))
                copies.append((found, slots_ref.at[pl.ds(low, BLK), to]))
        rows = pl.ds(0, chunk_rows)
        copies.append((source.at[rows, pl.ds(0, HD)], send_ref.at[rows, to]))
        copies.append((source.at[:, pl.ds(0, HD)], own_ref.at[:, to]))
    run_all(copies, sem)


def first_of(chunk_rows, local_block, keys, values):
    heads = local_block.shape[0]
    rows = keys.shape[0]
    slot_rows = heads * MOWN * BLK
    return pl.pallas_call(
        first_kernel,
        out_shape=[
            jax.ShapeDtypeStruct((rows, 2 * HD), keys.dtype),
            jax.ShapeDtypeStruct((chunk_rows + slot_rows, 2 * HD), keys.dtype),
            jax.ShapeDtypeStruct((slot_rows, 2 * HD), keys.dtype),
        ],
        in_specs=[SMEM, HBM, HBM],
        out_specs=[VMEM] * 3,
        scratch_shapes=[pltpu.SemaphoreType.DMA((4 * heads * MOWN + 4,))],
        compiler_params=pltpu.CompilerParams(vmem_limit_bytes=8 << 20),
        cost_estimate=pl.CostEstimate(flops=0, bytes_accessed=16 * rows * HD, transcendentals=0),
    )(local_block, keys, values)


def pair_kernel(head, keys_ref, values_ref, *rest):
    out_ref, sem = rest[-2:]
    run_all(
        [
            (source.at[:, pl.ds(head * HD, HD)], out_ref.at[:, pl.ds(side * HD, HD)])
            for side, source in enumerate((keys_ref, values_ref))
        ],
        sem,
    )


def pair_of(head, keys, values, after):
    rows = keys.shape[0]
    return pl.pallas_call(
        functools.partial(pair_kernel, head),
        out_shape=jax.ShapeDtypeStruct((rows, 2 * HD), keys.dtype),
        in_specs=[HBM] * (2 + len(after)),
        out_specs=VMEM,
        scratch_shapes=[pltpu.SemaphoreType.DMA((2,))],
        compiler_params=pltpu.CompilerParams(vmem_limit_bytes=8 << 20),
        cost_estimate=pl.CostEstimate(flops=0, bytes_accessed=8 * rows * HD, transcendentals=0),
    )(keys, values, *after)


def joined_kernel(pieces, parity_ref, *rest):
    refs, out_ref, sem = rest[:-2], rest[-2], rest[-1]
    to = 0
    for rows, even, odd in pieces:
        for value, (index, low) in enumerate((even, odd)):

            @pl.when(parity_ref[0] == value)
            def _():
                pltpu.make_async_copy(
                    refs[index].at[pl.ds(low, rows)], out_ref.at[pl.ds(to, rows)], sem
                ).start()

        to += rows
    pltpu.make_async_copy(out_ref, out_ref, sem).wait()


def joined(parity, pieces, after=()):
    arrays = []
    plan = []
    for rows, *sources in pieces:
        found = []
        for array, low in sources:
            at = [k for k, known in enumerate(arrays) if known is array]
            if not at:
                at = [len(arrays)]
                arrays.append(array)
            found.append((at[0], low))
        plan.append((rows, *found))
    total = sum(rows for rows, *_ in plan)
    return pl.pallas_call(
        functools.partial(joined_kernel, plan),
        out_shape=jax.ShapeDtypeStruct((total, 2 * HD), jnp.bfloat16),
        in_specs=[SMEM] + [HBM] * (len(arrays) + len(after)),
        out_specs=VMEM,
        scratch_shapes=[pltpu.SemaphoreType.DMA],
        compiler_params=pltpu.CompilerParams(vmem_limit_bytes=8 << 20),
        cost_estimate=pl.CostEstimate(flops=0, bytes_accessed=8 * total * HD, transcendentals=0),
    )(parity, *arrays, *after)


def listed_kernel(head, lows, place_ref, source_ref, *rest):
    refs, out_ref, sem = rest[:-2], rest[-2], rest[-1]

    def block(index, slot):
        return refs[index].at[pl.ds(lows[index] + (head * MOWN + slot) * BLK, BLK)]

    for index in range(len(refs)):
        for slot in range(MOWN):
            place = place_ref[index, head, slot]

            @pl.when(place >= 0)
            def _():
                pltpu.make_async_copy(block(index, slot), out_ref.at[blocks_at(place)], sem).start()

    for entry in range(NV):

        @pl.when(source_ref[head, entry] < 0)
        def _():
            pltpu.make_async_copy(
                block(0, 0), out_ref.at[pl.ds(entry * BLK, BLK)], sem
            ).start()

    pltpu.make_async_copy(out_ref, out_ref, sem).wait()


def listed_blocks(head, place, source, slots):
    return pl.pallas_call(
        functools.partial(listed_kernel, head, [low for _, low in slots]),
        out_shape=jax.ShapeDtypeStruct((NV * BLK, 2 * HD), jnp.bfloat16),
        in_specs=[SMEM, SMEM] + [HBM] * len(slots),
        out_specs=VMEM,
        scratch_shapes=[pltpu.SemaphoreType.DMA],
        compiler_params=pltpu.CompilerParams(vmem_limit_bytes=8 << 20),
        cost_estimate=pl.CostEstimate(flops=0, bytes_accessed=8 * NV * BLK * HD, transcendentals=0),
    )(place, source, *[array for array, _ in slots])


def attend_kernel(
    head, parts, bounds, waits, part_blocks, group_heads, part_ref, slash_ref, bias_ref, query_ref,
    vert_ref, own_ref, *rest,
):
    chunks = len(bounds) - 1
    two_back = rest[:chunks]
    one_back = rest[chunks : 2 * chunks]
    rest = rest[2 * chunks + waits :]
    out_refs = rest[:parts]
    (
        queries, out, vert, vert_keys, window, scores_a, scores_b, weights_a, weights_b, max_a,
        max_b, diagonal_ref, query_sem, vert_sem, window_sem, out_sem,
    ) = rest[parts:]
    scores, weights, maxima = (scores_a, scores_b), (weights_a, weights_b), (max_a, max_b)
    tok_rows = own_ref.shape[0]
    blocks_dev = tok_rows // BLK
    part_rows = part_blocks * BLK
    group_cols = group_heads * HD
    last = parts * part_blocks - 1
    step = pl.program_id(0)
    scale = 1.0 / math.sqrt(HD)
    contract = (((1,), (1,)), ((), ()))

    def shard_block(block):
        return part_ref[block // part_blocks] * part_blocks + lax.rem(block, part_blocks)

    def slash_rows(block):
        first = LOOK * blocks_dev + shard_block(block)
        return [blocks_at(first - slash_ref[head, entry]) for entry in range(NS)]

    def query_of(block):
        rows = blocks_at(block)
        return jnp.concatenate(
            [queries[rows, h * HD : (h + 1) * HD] for h in range(group_heads)], axis=0
        )

    def score_tile(query, bias, rows, tile):
        low = tile * TILE
        if low < NV * BLK:
            found = jnp.dot(
                query, vert_keys[:, low : low + TILE], preferred_element_type=jnp.float32
            )
        else:
            entry = (low - NV * BLK) // BLK
            keys = jnp.concatenate(
                [window[r, :HD] for r in rows[entry : entry + TILE // BLK]], axis=0
            )
            found = lax.dot_general(query, keys, contract, preferred_element_type=jnp.float32)
        found = found + bias[:, low : low + TILE]
        if low == NV * BLK:
            diagonal = jnp.concatenate([diagonal_ref[...]] * group_heads, axis=0)
            found = jnp.concatenate(
                [found[:, : 2 * BLK] + diagonal, found[:, 2 * BLK :]], axis=1
            )
        return found

    def weighted_values(block, at):
        ones = jnp.ones(((NV + NS) * BLK, HD), jnp.bfloat16)
        values = jnp.concatenate([vert[:, HD:]] + [window[r, HD:] for r in slash_rows(block)], axis=0)
        return jnp.dot(
            weights[at][...],
            jnp.concatenate([values, ones], axis=1),
            preferred_element_type=jnp.float32,
        )

    def store(total, block):
        result = (total[:, :HD] / total[:, HD:]).astype(jnp.bfloat16)
        rows = blocks_at(block)
        for h in range(group_heads):
            out[rows, h * HD : (h + 1) * HD] = result[h * BLK : (h + 1) * BLK]

    def stage(block, at, score, weigh, combine, arrives=False):
        other = 1 - at
        if score:
            fresh = jnp.minimum(block, last)
            query = query_of(fresh)
            rows = slash_rows(fresh)
            bias = bias_ref[pl.ds(head * blocks_dev + shard_block(fresh), 1), :]
        if combine:
            done = jnp.maximum(block - 2, 0)
            total = weighted_values(done, at)
        if weigh:
            row_max = maxima[other][...]
            row_max = jnp.concatenate([row_max] * (TILE // HD), axis=1)
        highest = None
        for tile in range((NV + NS) * BLK // TILE):
            low = tile * TILE
            if arrives and low == NV * BLK:
                pltpu.make_async_copy(window, window, window_sem).wait()
            if score:
                found = score_tile(query, bias, rows, tile)
                scores[at][:, low : low + TILE] = found
                for piece_low in range(0, TILE, HD):
                    piece = found[:, piece_low : piece_low + HD]
                    highest = piece if highest is None else jnp.maximum(highest, piece)
            if weigh:
                weights[other][:, low : low + TILE] = jnp.exp(
                    (scores[other][:, low : low + TILE] - row_max) * scale
                ).astype(jnp.bfloat16)
        if score:
            maxima[at][...] = jnp.broadcast_to(
                jnp.max(highest, axis=1, keepdims=True), highest.shape
            )
        if combine:
            store(total, done)

    @pl.when(step == 0)
    def _():
        for k in range(parts):
            pltpu.make_async_copy(
                query_ref.at[
                    pl.ds(pl.multiple_of(part_ref[k] * part_rows, part_rows), part_rows),
                    pl.ds(head * group_cols, group_cols),
                ],
                queries.at[pl.ds(k * part_rows, part_rows)],
                query_sem,
            ).start()
        pltpu.make_async_copy(vert_ref, vert, vert_sem).start()
        for back, sources in enumerate((two_back, one_back)):
            for chunk, source in enumerate(sources):
                rows = bounds[chunk + 1] - bounds[chunk]
                pltpu.make_async_copy(
                    source.at[pl.ds(0, rows)],
                    window.at[pl.ds(back * tok_rows + bounds[chunk], rows)],
                    window_sem,
                ).start()
        pltpu.make_async_copy(
            own_ref, window.at[pl.ds(LOOK * tok_rows, tok_rows)], window_sem
        ).start()
        column = lax.broadcasted_iota(jnp.int32, (BLK, 2 * BLK), 1)
        row = lax.broadcasted_iota(jnp.int32, (BLK, 2 * BLK), 0)
        diagonal_ref[...] = jnp.where((column < BLK) & (column > row), NEG, 0.0).astype(jnp.float32)
        weights_b[...] = jnp.zeros_like(weights_b)
        pltpu.make_async_copy(vert, vert, vert_sem).wait()
        vert_keys[...] = vert[:, :HD].T
        pltpu.make_async_copy(queries, queries, query_sem).wait()
        stage(0, 0, True, False, False, True)

    first = step * STEP_BLOCKS
    stage(first + 1, 1, True, True, True)
    stage(first + 2, 0, True, True, True)

    @pl.when(first + STEP_BLOCKS > last)
    def _():
        store(weighted_values(last, 1), last)
        for k in range(parts):
            pltpu.make_async_copy(
                out.at[pl.ds(k * part_rows, part_rows)], out_refs[k], out_sem.at[k]
            ).start()
        for k in range(parts):
            pltpu.make_async_copy(
                out.at[pl.ds(k * part_rows, part_rows)], out_refs[k], out_sem.at[k]
            ).wait()


def attend(head, part, bounds, slash, bias, queries, vert, own, two_back, one_back, part_rows, after):
    parts = part.shape[0]
    group_cols = queries.shape[1] // slash.shape[0]
    group_heads = group_cols // HD
    part_blocks = part_rows // BLK
    tok_rows = own.shape[0]
    rows = group_heads * BLK
    keys_seen = (NV + NS) * BLK
    return pl.pallas_call(
        functools.partial(
            attend_kernel, head, parts, bounds, len(after), part_blocks, group_heads
        ),
        out_shape=[jax.ShapeDtypeStruct((part_rows, group_cols), jnp.bfloat16)] * parts,
        grid_spec=pltpu.PrefetchScalarGridSpec(
            num_scalar_prefetch=2,
            grid=(parts * part_blocks // STEP_BLOCKS,),
            in_specs=[pl.BlockSpec(bias.shape, lambda s, *_: (0, 0))] + [HBM] * (3 + 2 * len(two_back) + len(after)),
            out_specs=[HBM] * parts,
            scratch_shapes=[
                pltpu.VMEM((parts * part_rows, group_cols), jnp.bfloat16),
                pltpu.VMEM((parts * part_rows, group_cols), jnp.bfloat16),
                pltpu.VMEM((NV * BLK, 2 * HD), jnp.bfloat16),
                pltpu.VMEM((HD, NV * BLK), jnp.bfloat16),
                pltpu.VMEM(((LOOK + 1) * tok_rows, 2 * HD), jnp.bfloat16),
                pltpu.VMEM((rows, keys_seen), jnp.float32),
                pltpu.VMEM((rows, keys_seen), jnp.float32),
                pltpu.VMEM((rows, keys_seen), jnp.bfloat16),
                pltpu.VMEM((rows, keys_seen), jnp.bfloat16),
                pltpu.VMEM((rows, HD), jnp.float32),
                pltpu.VMEM((rows, HD), jnp.float32),
                pltpu.VMEM((BLK, 2 * BLK), jnp.float32),
                pltpu.SemaphoreType.DMA,
                pltpu.SemaphoreType.DMA,
                pltpu.SemaphoreType.DMA,
                pltpu.SemaphoreType.DMA((parts,)),
            ],
        ),
        compiler_params=pltpu.CompilerParams(
            dimension_semantics=("arbitrary",), vmem_limit_bytes=24 << 20
        ),
        cost_estimate=pl.CostEstimate(
            flops=4 * parts * part_rows * group_heads * keys_seen * HD,
            bytes_accessed=4 * parts * part_rows * group_cols + 12 * tok_rows * HD,
            transcendentals=parts * part_rows * group_heads * keys_seen,
        ),
    )(part, slash, bias, queries, vert, own, *two_back, *one_back, *after)


def local(queries, keys, values, vertical, slash):
    shard_count = lax.axis_size("ctx")
    shard_index = lax.axis_index("ctx")
    head_count = lax.axis_size("head")
    head_index = lax.axis_index("head")
    tok_rows = queries.shape[0]
    kv_local = keys.shape[1] // HD
    group_cols = queries.shape[1] // kv_local
    blocks_dev = tok_rows // BLK
    part_rows = tok_rows // head_count
    partner = shard_index ^ 1
    two_pairs = [(i, i + 2) for i in range(shard_count - 2)]
    across_pairs = [(i, i ^ 1) for i in range(shard_count)]
    parity = (shard_index % 2).reshape(1).astype(jnp.int32)

    owners = vertical // blocks_dev
    order = jnp.arange(NV, dtype=jnp.int32)
    same_owner = owners[:, :, None] == owners[:, None, :]
    earlier = order[None, :] < order[:, None]
    slot_rank = jnp.sum((same_owner & earlier[None]).astype(jnp.int32), axis=2)
    slots = jnp.arange(MOWN, dtype=jnp.int32)
    in_slot = slot_rank[:, :, None] == slots
    local_block = jnp.sum(
        ((owners == shard_index)[:, :, None] & in_slot) * (vertical % blocks_dev)[:, :, None],
        axis=1,
    )
    distances = 2 * jnp.arange(shard_count // 2, dtype=jnp.int32)
    array_owner = jnp.concatenate([shard_index - distances, partner - distances])
    array_owner = jnp.where(array_owner <= shard_index, array_owner, -1)
    here = (array_owner[:, None, None] == owners)[:, :, :, None] & in_slot[None]
    place = jnp.sum(here * (order + 1)[None, None, :, None], axis=2) - 1
    source = jnp.where(owners <= shard_index, 0, -1).astype(jnp.int32)

    slash_rank = jnp.sum((slash[:, None, :] < slash[:, :, None]).astype(jnp.int32), axis=2)
    at_rank = slash_rank[:, :, None] == jnp.arange(NS, dtype=jnp.int32)
    slash = jnp.sum(at_rank * slash[:, :, None], axis=1)

    global_blocks = shard_index * blocks_dev + jnp.arange(blocks_dev, dtype=jnp.int32)
    vert_valid = vertical[:, None, :] < global_blocks[None, :, None]
    slash_blocks = global_blocks[None, :, None] - slash[:, None, :]
    in_vertical = jnp.any(slash_blocks[:, :, :, None] == vertical[:, None, None, :], axis=3)
    slash_valid = (slash[:, None, :] == 0) | ((slash_blocks >= 0) & jnp.logical_not(in_vertical))
    valid = jnp.concatenate([vert_valid, slash_valid], axis=2)
    listed = jnp.arange(NV + NS, dtype=jnp.int32)
    spread = (jnp.arange((NV + NS) * BLK, dtype=jnp.int32) // BLK == listed[:, None])
    barred = jnp.where(valid, 0.0, NEG).reshape(kv_local * blocks_dev, NV + NS)
    bias = jnp.dot(
        barred.astype(jnp.bfloat16), spread.astype(jnp.bfloat16), preferred_element_type=jnp.float32
    )

    steps = shard_count // 2 - 1
    bounds = [k * blocks_dev // steps * BLK for k in range(steps + 1)]
    slot_rows = kv_local * MOWN * BLK
    own, send, slots_own = first_of(bounds[1], local_block, keys, values)
    behind = [(slots_own, 0)]
    across = []
    two_back = []
    one_back = []
    for step in range(steps):
        rows = bounds[step + 1] - bounds[step]
        here = (own, bounds[step])
        if step:
            send = joined(
                parity, [(rows, here, here), (slot_rows, behind[-1], behind[-1])],
                [cross] + one_back[-2:-1],
            )
        come = lax.ppermute(send, "ctx", two_pairs)
        if step == 0:
            pairs = [(i, i + 1) for i in range(0, shard_count, 2)]
            across.append((lax.ppermute(slots_own, "ctx", pairs), 0))
        two_back.append(come)
        behind.append((come, rows))
        cross = joined(parity, [(rows, here, (come, 0)), (slot_rows, behind[-1], behind[-1])])
        one_back.append(lax.ppermute(cross, "ctx", across_pairs))
        across.append((one_back[-1], rows))
    slots = behind + across
    windows = [(bounds, own, two_back, one_back)]
    after = two_back[-1:] + one_back[-2:-1] + [cross]
    for head in range(1, kv_local):
        own = pair_of(head, keys, values, after)
        come = lax.ppermute(own, "ctx", two_pairs)
        windows.append(([0, tok_rows], own, [come], None))
        after = [come]

    out = jnp.zeros((part_rows, head_count * kv_local * group_cols), jnp.bfloat16)
    after = []
    half = head_count // 2
    calls = [[flip] for flip in range(head_count - 1, half - 1, -1)]
    calls.append(list(range(half - 1, -1, -1)))
    for head in range(kv_local):
        bounds, own, two_back, one_back = windows[head]
        vert = listed_blocks(head, place, source, slots)
        for flips in calls:
            others = [head_index ^ flip for flip in flips]
            pieces = attend(
                head, jnp.stack(others).astype(jnp.int32), bounds, slash, bias, queries, vert, own,
                two_back, one_back, part_rows, after,
            )
            after = [pieces[-1]]
            if flips == calls[0] and head + 1 < kv_local:
                near, own_next, (come,), _ = windows[head + 1]
                cross = joined(parity, [(tok_rows, (own_next, 0), (come, 0))], after)
                crossed = lax.ppermute(cross, "ctx", across_pairs)
                windows[head + 1] = (near, own_next, [come], [crossed])
            for flip, other, piece in zip(flips, others, pieces):
                if flip:
                    piece = lax.ppermute(piece, "head", [(i, i ^ flip) for i in range(head_count)])
                out = lax.dynamic_update_slice(
                    out, piece, (0, other * kv_local * group_cols + head * group_cols)
                )
    return out


def solution(mesh):
    in_specs = (
        P("ctx", "head"),
        P("ctx", "head"),
        P("ctx", "head"),
        P("head", None),
        P("head", None),
    )
    out_specs = P(("ctx", "head"), None)
    return jax.shard_map(local, mesh=mesh, in_specs=in_specs, out_specs=out_specs, check_vma=False)
```

```python
import functools
import math

import jax
import jax.numpy as jnp
from jax import lax
from jax.experimental import pallas as pl
from jax.experimental.pallas import tpu as pltpu
from jax.sharding import PartitionSpec as P

HD = 128
BLK = 64
NV = 16
NS = 8
MOWN = 4
LOOK = 2
NEG = -1e30
STEP_BLOCKS = 2
TILE = 256
HBM = pl.BlockSpec(memory_space=pltpu.HBM)
VMEM = pl.BlockSpec(memory_space=pltpu.VMEM)
SMEM = pl.BlockSpec(memory_space=pltpu.SMEM)


def blocks_at(index, count=1):
    return pl.ds(pl.multiple_of(index * BLK, BLK), count * BLK)


def run_all(copies, sem):
    copies = [pltpu.make_async_copy(*ends, sem.at[k]) for k, ends in enumerate(copies)]
    for copy in copies:
        copy.start()
    for copy in copies:
        copy.wait()


def first_kernel(local_ref, keys_ref, values_ref, own_ref, send_ref, slots_ref, sem):
    chunk_rows = send_ref.shape[0] - slots_ref.shape[0]
    copies = []
    for side, source in enumerate((keys_ref, values_ref)):
        to = pl.ds(side * HD, HD)
        for head in range(local_ref.shape[0]):
            for slot in range(MOWN):
                found = source.at[blocks_at(local_ref[head, slot]), pl.ds(head * HD, HD)]
                low = (head * MOWN + slot) * BLK
                copies.append((found, send_ref.at[pl.ds(chunk_rows + low, BLK), to]))
                copies.append((found, slots_ref.at[pl.ds(low, BLK), to]))
        rows = pl.ds(0, chunk_rows)
        copies.append((source.at[rows, pl.ds(0, HD)], send_ref.at[rows, to]))
        copies.append((source.at[:, pl.ds(0, HD)], own_ref.at[:, to]))
    run_all(copies, sem)


def first_of(chunk_rows, local_block, keys, values):
    heads = local_block.shape[0]
    rows = keys.shape[0]
    slot_rows = heads * MOWN * BLK
    return pl.pallas_call(
        first_kernel,
        out_shape=[
            jax.ShapeDtypeStruct((rows, 2 * HD), keys.dtype),
            jax.ShapeDtypeStruct((chunk_rows + slot_rows, 2 * HD), keys.dtype),
            jax.ShapeDtypeStruct((slot_rows, 2 * HD), keys.dtype),
        ],
        in_specs=[SMEM, HBM, HBM],
        out_specs=[VMEM] * 3,
        scratch_shapes=[pltpu.SemaphoreType.DMA((4 * heads * MOWN + 4,))],
        compiler_params=pltpu.CompilerParams(vmem_limit_bytes=8 << 20),
        cost_estimate=pl.CostEstimate(flops=0, bytes_accessed=16 * rows * HD, transcendentals=0),
    )(local_block, keys, values)


def pair_kernel(head, keys_ref, values_ref, *rest):
    out_ref, sem = rest[-2:]
    run_all(
        [
            (source.at[:, pl.ds(head * HD, HD)], out_ref.at[:, pl.ds(side * HD, HD)])
            for side, source in enumerate((keys_ref, values_ref))
        ],
        sem,
    )


def pair_of(head, keys, values, after):
    rows = keys.shape[0]
    return pl.pallas_call(
        functools.partial(pair_kernel, head),
        out_shape=jax.ShapeDtypeStruct((rows, 2 * HD), keys.dtype),
        in_specs=[HBM] * (2 + len(after)),
        out_specs=VMEM,
        scratch_shapes=[pltpu.SemaphoreType.DMA((2,))],
        compiler_params=pltpu.CompilerParams(vmem_limit_bytes=8 << 20),
        cost_estimate=pl.CostEstimate(flops=0, bytes_accessed=8 * rows * HD, transcendentals=0),
    )(keys, values, *after)


def joined_kernel(pieces, parity_ref, *rest):
    refs, out_ref, sem = rest[:-2], rest[-2], rest[-1]
    to = 0
    for rows, even, odd in pieces:
        for value, (index, low) in enumerate((even, odd)):

            @pl.when(parity_ref[0] == value)
            def _():
                pltpu.make_async_copy(
                    refs[index].at[pl.ds(low, rows)], out_ref.at[pl.ds(to, rows)], sem
                ).start()

        to += rows
    pltpu.make_async_copy(out_ref, out_ref, sem).wait()


def joined(parity, pieces, after=()):
    arrays = []
    plan = []
    for rows, *sources in pieces:
        found = []
        for array, low in sources:
            at = [k for k, known in enumerate(arrays) if known is array]
            if not at:
                at = [len(arrays)]
                arrays.append(array)
            found.append((at[0], low))
        plan.append((rows, *found))
    total = sum(rows for rows, *_ in plan)
    return pl.pallas_call(
        functools.partial(joined_kernel, plan),
        out_shape=jax.ShapeDtypeStruct((total, 2 * HD), jnp.bfloat16),
        in_specs=[SMEM] + [HBM] * (len(arrays) + len(after)),
        out_specs=VMEM,
        scratch_shapes=[pltpu.SemaphoreType.DMA],
        compiler_params=pltpu.CompilerParams(vmem_limit_bytes=8 << 20),
        cost_estimate=pl.CostEstimate(flops=0, bytes_accessed=8 * total * HD, transcendentals=0),
    )(parity, *arrays, *after)


def listed_kernel(lows, place_ref, source_ref, *rest):
    refs, out_ref, sem = rest[:-2], rest[-2], rest[-1]
    for head in range(out_ref.shape[0]):

        def block(index, slot):
            return refs[index].at[pl.ds(lows[index] + (head * MOWN + slot) * BLK, BLK)]

        def put(found, target):
            pltpu.make_async_copy(found, out_ref.at[head, target], sem).start()

        for index in range(len(refs)):
            for slot in range(MOWN):
                place = place_ref[index, head, slot]
                pl.when(place >= 0)(
                    functools.partial(put, block(index, slot), blocks_at(place))
                )
        for entry in range(NV):
            pl.when(source_ref[head, entry] < 0)(
                functools.partial(put, block(0, 0), pl.ds(entry * BLK, BLK))
            )
    pltpu.make_async_copy(out_ref, out_ref, sem).wait()


def listed_blocks(place, source, slots):
    heads = source.shape[0]
    return pl.pallas_call(
        functools.partial(listed_kernel, [low for _, low in slots]),
        out_shape=jax.ShapeDtypeStruct((heads, NV * BLK, 2 * HD), jnp.bfloat16),
        in_specs=[SMEM, SMEM] + [HBM] * len(slots),
        out_specs=VMEM,
        scratch_shapes=[pltpu.SemaphoreType.DMA],
        compiler_params=pltpu.CompilerParams(vmem_limit_bytes=8 << 20),
        cost_estimate=pl.CostEstimate(
            flops=0, bytes_accessed=8 * heads * NV * BLK * HD, transcendentals=0
        ),
    )(place, source, *[array for array, _ in slots])


def attend_kernel(
    head, parts, bounds, waits, part_blocks, group_heads, part_ref, slash_ref, bias_ref, query_ref,
    vert_ref, own_ref, *rest,
):
    chunks = len(bounds) - 1
    two_back = rest[:chunks]
    one_back = rest[chunks : 2 * chunks]
    rest = rest[2 * chunks + waits :]
    out_refs = rest[:parts]
    (
        queries, out, vert, vert_keys, window, scores_a, scores_b, weights_a, weights_b, max_a,
        max_b, diagonal_ref, query_sem, vert_sem, window_sem, out_sem,
    ) = rest[parts:]
    scores, weights, maxima = (scores_a, scores_b), (weights_a, weights_b), (max_a, max_b)
    tok_rows = own_ref.shape[0]
    blocks_dev = tok_rows // BLK
    part_rows = part_blocks * BLK
    group_cols = group_heads * HD
    last = parts * part_blocks - 1
    step = pl.program_id(0)
    scale = 1.0 / math.sqrt(HD)
    contract = (((1,), (1,)), ((), ()))

    def shard_block(block):
        return part_ref[block // part_blocks] * part_blocks + lax.rem(block, part_blocks)

    def slash_rows(block):
        first = LOOK * blocks_dev + shard_block(block)
        return [blocks_at(first - slash_ref[head, entry]) for entry in range(NS)]

    def query_of(block):
        rows = blocks_at(block)
        return jnp.concatenate(
            [queries[rows, h * HD : (h + 1) * HD] for h in range(group_heads)], axis=0
        )

    def score_tile(query, bias, rows, tile):
        low = tile * TILE
        if low < NV * BLK:
            found = jnp.dot(
                query, vert_keys[:, low : low + TILE], preferred_element_type=jnp.float32
            )
        else:
            entry = (low - NV * BLK) // BLK
            keys = jnp.concatenate(
                [window[r, :HD] for r in rows[entry : entry + TILE // BLK]], axis=0
            )
            found = lax.dot_general(query, keys, contract, preferred_element_type=jnp.float32)
        found = found + bias[:, low : low + TILE]
        if low == NV * BLK:
            diagonal = jnp.concatenate([diagonal_ref[...]] * group_heads, axis=0)
            found = jnp.concatenate(
                [found[:, : 2 * BLK] + diagonal, found[:, 2 * BLK :]], axis=1
            )
        return found

    def weighted_values(block, at):
        ones = jnp.ones(((NV + NS) * BLK, HD), jnp.bfloat16)
        values = jnp.concatenate([vert[:, HD:]] + [window[r, HD:] for r in slash_rows(block)], axis=0)
        return jnp.dot(
            weights[at][...],
            jnp.concatenate([values, ones], axis=1),
            preferred_element_type=jnp.float32,
        )

    def store(total, block):
        result = (total[:, :HD] / total[:, HD:]).astype(jnp.bfloat16)
        rows = blocks_at(block)
        for h in range(group_heads):
            out[rows, h * HD : (h + 1) * HD] = result[h * BLK : (h + 1) * BLK]

    def stage(block, at, score, weigh, combine, arrives=False):
        other = 1 - at
        if score:
            fresh = jnp.minimum(block, last)
            query = query_of(fresh)
            rows = slash_rows(fresh)
            bias = bias_ref[pl.ds(head * blocks_dev + shard_block(fresh), 1), :]
        if combine:
            done = jnp.maximum(block - 2, 0)
            total = weighted_values(done, at)
        if weigh:
            row_max = maxima[other][...]
            row_max = jnp.concatenate([row_max] * (TILE // HD), axis=1)
        highest = None
        for tile in range((NV + NS) * BLK // TILE):
            low = tile * TILE
            if arrives and low == NV * BLK:
                pltpu.make_async_copy(window, window, window_sem).wait()
            if score:
                found = score_tile(query, bias, rows, tile)
                scores[at][:, low : low + TILE] = found
                for piece_low in range(0, TILE, HD):
                    piece = found[:, piece_low : piece_low + HD]
                    highest = piece if highest is None else jnp.maximum(highest, piece)
            if weigh:
                weights[other][:, low : low + TILE] = jnp.exp(
                    (scores[other][:, low : low + TILE] - row_max) * scale
                ).astype(jnp.bfloat16)
        if score:
            maxima[at][...] = jnp.broadcast_to(
                jnp.max(highest, axis=1, keepdims=True), highest.shape
            )
        if combine:
            store(total, done)

    @pl.when(step == 0)
    def _():
        for k in range(parts):
            pltpu.make_async_copy(
                query_ref.at[
                    pl.ds(pl.multiple_of(part_ref[k] * part_rows, part_rows), part_rows),
                    pl.ds(head * group_cols, group_cols),
                ],
                queries.at[pl.ds(k * part_rows, part_rows)],
                query_sem,
            ).start()
        pltpu.make_async_copy(vert_ref.at[head], vert, vert_sem).start()
        for back, sources in enumerate((two_back, one_back)):
            for chunk, source in enumerate(sources):
                rows = bounds[chunk + 1] - bounds[chunk]
                pltpu.make_async_copy(
                    source.at[pl.ds(0, rows)],
                    window.at[pl.ds(back * tok_rows + bounds[chunk], rows)],
                    window_sem,
                ).start()
        pltpu.make_async_copy(
            own_ref, window.at[pl.ds(LOOK * tok_rows, tok_rows)], window_sem
        ).start()
        column = lax.broadcasted_iota(jnp.int32, (BLK, 2 * BLK), 1)
        row = lax.broadcasted_iota(jnp.int32, (BLK, 2 * BLK), 0)
        diagonal_ref[...] = jnp.where((column < BLK) & (column > row), NEG, 0.0).astype(jnp.float32)
        weights_b[...] = jnp.zeros_like(weights_b)
        pltpu.make_async_copy(vert, vert, vert_sem).wait()
        vert_keys[...] = vert[:, :HD].T
        pltpu.make_async_copy(queries, queries, query_sem).wait()
        stage(0, 0, True, False, False, True)

    first = step * STEP_BLOCKS
    stage(first + 1, 1, True, True, True)
    stage(first + 2, 0, True, True, True)

    @pl.when(first + STEP_BLOCKS > last)
    def _():
        store(weighted_values(last, 1), last)
        for k in range(parts):
            pltpu.make_async_copy(
                out.at[pl.ds(k * part_rows, part_rows)], out_refs[k], out_sem.at[k]
            ).start()
        for k in range(parts):
            pltpu.make_async_copy(
                out.at[pl.ds(k * part_rows, part_rows)], out_refs[k], out_sem.at[k]
            ).wait()


def attend(head, part, bounds, slash, bias, queries, vert, own, two_back, one_back, part_rows, after):
    parts = part.shape[0]
    group_cols = queries.shape[1] // slash.shape[0]
    group_heads = group_cols // HD
    part_blocks = part_rows // BLK
    tok_rows = own.shape[0]
    rows = group_heads * BLK
    keys_seen = (NV + NS) * BLK
    return pl.pallas_call(
        functools.partial(
            attend_kernel, head, parts, bounds, len(after), part_blocks, group_heads
        ),
        out_shape=[jax.ShapeDtypeStruct((part_rows, group_cols), jnp.bfloat16)] * parts,
        grid_spec=pltpu.PrefetchScalarGridSpec(
            num_scalar_prefetch=2,
            grid=(parts * part_blocks // STEP_BLOCKS,),
            in_specs=[pl.BlockSpec(bias.shape, lambda s, *_: (0, 0))] + [HBM] * (3 + 2 * len(two_back) + len(after)),
            out_specs=[HBM] * parts,
            scratch_shapes=[
                pltpu.VMEM((parts * part_rows, group_cols), jnp.bfloat16),
                pltpu.VMEM((parts * part_rows, group_cols), jnp.bfloat16),
                pltpu.VMEM((NV * BLK, 2 * HD), jnp.bfloat16),
                pltpu.VMEM((HD, NV * BLK), jnp.bfloat16),
                pltpu.VMEM(((LOOK + 1) * tok_rows, 2 * HD), jnp.bfloat16),
                pltpu.VMEM((rows, keys_seen), jnp.float32),
                pltpu.VMEM((rows, keys_seen), jnp.float32),
                pltpu.VMEM((rows, keys_seen), jnp.bfloat16),
                pltpu.VMEM((rows, keys_seen), jnp.bfloat16),
                pltpu.VMEM((rows, HD), jnp.float32),
                pltpu.VMEM((rows, HD), jnp.float32),
                pltpu.VMEM((BLK, 2 * BLK), jnp.float32),
                pltpu.SemaphoreType.DMA,
                pltpu.SemaphoreType.DMA,
                pltpu.SemaphoreType.DMA,
                pltpu.SemaphoreType.DMA((parts,)),
            ],
        ),
        compiler_params=pltpu.CompilerParams(
            dimension_semantics=("arbitrary",), vmem_limit_bytes=56 << 20
        ),
        cost_estimate=pl.CostEstimate(
            flops=4 * parts * part_rows * group_heads * keys_seen * HD,
            bytes_accessed=4 * parts * part_rows * group_cols + 12 * tok_rows * HD,
            transcendentals=parts * part_rows * group_heads * keys_seen,
        ),
    )(part, slash, bias, queries, vert, own, *two_back, *one_back, *after)


def local(queries, keys, values, vertical, slash):
    shard_count = lax.axis_size("ctx")
    shard_index = lax.axis_index("ctx")
    head_count = lax.axis_size("head")
    head_index = lax.axis_index("head")
    tok_rows = queries.shape[0]
    kv_local = keys.shape[1] // HD
    group_cols = queries.shape[1] // kv_local
    blocks_dev = tok_rows // BLK
    part_rows = tok_rows // head_count
    partner = shard_index ^ 1
    two_pairs = [(i, i + 2) for i in range(shard_count - 2)]
    across_pairs = [(i, i ^ 1) for i in range(shard_count)]
    parity = (shard_index % 2).reshape(1).astype(jnp.int32)

    owners = vertical // blocks_dev
    order = jnp.arange(NV, dtype=jnp.int32)
    same_owner = owners[:, :, None] == owners[:, None, :]
    earlier = order[None, :] < order[:, None]
    slot_rank = jnp.sum((same_owner & earlier[None]).astype(jnp.int32), axis=2)
    slots = jnp.arange(MOWN, dtype=jnp.int32)
    in_slot = slot_rank[:, :, None] == slots
    local_block = jnp.sum(
        ((owners == shard_index)[:, :, None] & in_slot) * (vertical % blocks_dev)[:, :, None],
        axis=1,
    )
    distances = 2 * jnp.arange(shard_count // 2, dtype=jnp.int32)
    array_owner = jnp.concatenate([shard_index - distances, partner - distances])
    array_owner = jnp.where(array_owner <= shard_index, array_owner, -1)
    here = (array_owner[:, None, None] == owners)[:, :, :, None] & in_slot[None]
    place = jnp.sum(here * (order + 1)[None, None, :, None], axis=2) - 1
    source = jnp.where(owners <= shard_index, 0, -1).astype(jnp.int32)

    slash_rank = jnp.sum((slash[:, None, :] < slash[:, :, None]).astype(jnp.int32), axis=2)
    at_rank = slash_rank[:, :, None] == jnp.arange(NS, dtype=jnp.int32)
    slash = jnp.sum(at_rank * slash[:, :, None], axis=1)

    global_blocks = shard_index * blocks_dev + jnp.arange(blocks_dev, dtype=jnp.int32)
    vert_valid = vertical[:, None, :] < global_blocks[None, :, None]
    slash_blocks = global_blocks[None, :, None] - slash[:, None, :]
    in_vertical = jnp.any(slash_blocks[:, :, :, None] == vertical[:, None, None, :], axis=3)
    slash_valid = (slash[:, None, :] == 0) | ((slash_blocks >= 0) & jnp.logical_not(in_vertical))
    valid = jnp.concatenate([vert_valid, slash_valid], axis=2)
    listed = jnp.arange(NV + NS, dtype=jnp.int32)
    spread = (jnp.arange((NV + NS) * BLK, dtype=jnp.int32) // BLK == listed[:, None])
    barred = jnp.where(valid, 0.0, NEG).reshape(kv_local * blocks_dev, NV + NS)
    bias = jnp.dot(
        barred.astype(jnp.bfloat16), spread.astype(jnp.bfloat16), preferred_element_type=jnp.float32
    )

    steps = shard_count // 2 - 1
    bounds = [k * blocks_dev // steps * BLK for k in range(steps + 1)]
    slot_rows = kv_local * MOWN * BLK
    own, send, slots_own = first_of(bounds[1], local_block, keys, values)
    behind = [(slots_own, 0)]
    across = []
    two_back = []
    one_back = []
    for step in range(steps):
        rows = bounds[step + 1] - bounds[step]
        here = (own, bounds[step])
        if step:
            send = joined(
                parity, [(rows, here, here), (slot_rows, behind[-1], behind[-1])],
                [cross] + one_back[-2:-1],
            )
        come = lax.ppermute(send, "ctx", two_pairs)
        if step == 0:
            pairs = [(i, i + 1) for i in range(0, shard_count, 2)]
            across.append((lax.ppermute(slots_own, "ctx", pairs), 0))
        two_back.append(come)
        behind.append((come, rows))
        cross = joined(parity, [(rows, here, (come, 0)), (slot_rows, behind[-1], behind[-1])])
        one_back.append(lax.ppermute(cross, "ctx", across_pairs))
        across.append((one_back[-1], rows))
    slots = behind + across
    windows = [(bounds, own, two_back, one_back)]
    after = two_back[-2:-1] + [send]
    for head in range(1, kv_local):
        own = pair_of(head, keys, values, after)
        come = lax.ppermute(own, "ctx", two_pairs)
        windows.append(([0, tok_rows], own, [come], None))
        after = [come]

    out = jnp.zeros((part_rows, head_count * kv_local * group_cols), jnp.bfloat16)
    after = []
    half = head_count // 2
    calls = [[[head_count - 1], list(range(head_count - 2, -1, -1))]] * (kv_local - 1)
    calls.append([[flip] for flip in range(head_count - 1, half - 1, -1)])
    calls[-1].append(list(range(half - 1, -1, -1)))
    vert = listed_blocks(place, source, slots)
    for head in range(kv_local):
        bounds, own, two_back, one_back = windows[head]
        for flips in calls[head]:
            others = [head_index ^ flip for flip in flips]
            pieces = attend(
                head, jnp.stack(others).astype(jnp.int32), bounds, slash, bias, queries, vert, own,
                two_back, one_back, part_rows, after,
            )
            after = [pieces[-1]]
            if flips == calls[head][0] and head + 1 < kv_local:
                near, own_next, (come,), _ = windows[head + 1]
                cross = joined(parity, [(tok_rows, (own_next, 0), (come, 0))], after)
                crossed = lax.ppermute(cross, "ctx", across_pairs)
                windows[head + 1] = (near, own_next, [come], [crossed])
            for flip, other, piece in zip(flips, others, pieces):
                if flip:
                    piece = lax.ppermute(piece, "head", [(i, i ^ flip) for i in range(head_count)])
                out = lax.dynamic_update_slice(
                    out, piece, (0, other * kv_local * group_cols + head * group_cols)
                )
    return out


def solution(mesh):
    in_specs = (
        P("ctx", "head"),
        P("ctx", "head"),
        P("ctx", "head"),
        P("head", None),
        P("head", None),
    )
    out_specs = P(("ctx", "head"), None)
    return jax.shard_map(local, mesh=mesh, in_specs=in_specs, out_specs=out_specs, check_vma=False)
```

```python
import functools
import math

import jax
import jax.numpy as jnp
from jax import lax
from jax.experimental import pallas as pl
from jax.experimental.pallas import tpu as pltpu
from jax.sharding import PartitionSpec as P

HD = 128
BLK = 64
NV = 16
NS = 8
MOWN = 4
LOOK = 2
NEG = -1e30
STEP_BLOCKS = 2
TILE = 256
HBM = pl.BlockSpec(memory_space=pltpu.HBM)
VMEM = pl.BlockSpec(memory_space=pltpu.VMEM)
SMEM = pl.BlockSpec(memory_space=pltpu.SMEM)


def blocks_at(index, count=1):
    return pl.ds(pl.multiple_of(index * BLK, BLK), count * BLK)


def run_all(copies, sem):
    copies = [pltpu.make_async_copy(*ends, sem.at[k]) for k, ends in enumerate(copies)]
    for copy in copies:
        copy.start()
    for copy in copies:
        copy.wait()


def first_kernel(local_ref, keys_ref, values_ref, own_ref, send_ref, slots_ref, sem):
    chunk_rows = send_ref.shape[0] - slots_ref.shape[0]
    copies = []
    for side, source in enumerate((keys_ref, values_ref)):
        to = pl.ds(side * HD, HD)
        for head in range(local_ref.shape[0]):
            for slot in range(MOWN):
                found = source.at[blocks_at(local_ref[head, slot]), pl.ds(head * HD, HD)]
                low = (head * MOWN + slot) * BLK
                copies.append((found, send_ref.at[pl.ds(chunk_rows + low, BLK), to]))
                copies.append((found, slots_ref.at[pl.ds(low, BLK), to]))
        rows = pl.ds(0, chunk_rows)
        copies.append((source.at[rows, pl.ds(0, HD)], send_ref.at[rows, to]))
        copies.append((source.at[:, pl.ds(0, HD)], own_ref.at[:, to]))
    run_all(copies, sem)


def first_of(chunk_rows, local_block, keys, values):
    heads = local_block.shape[0]
    rows = keys.shape[0]
    slot_rows = heads * MOWN * BLK
    return pl.pallas_call(
        first_kernel,
        out_shape=[
            jax.ShapeDtypeStruct((rows, 2 * HD), keys.dtype),
            jax.ShapeDtypeStruct((chunk_rows + slot_rows, 2 * HD), keys.dtype),
            jax.ShapeDtypeStruct((slot_rows, 2 * HD), keys.dtype),
        ],
        in_specs=[SMEM, HBM, HBM],
        out_specs=[VMEM] * 3,
        scratch_shapes=[pltpu.SemaphoreType.DMA((4 * heads * MOWN + 4,))],
        compiler_params=pltpu.CompilerParams(vmem_limit_bytes=8 << 20),
        cost_estimate=pl.CostEstimate(flops=0, bytes_accessed=16 * rows * HD, transcendentals=0),
    )(local_block, keys, values)


def pair_kernel(head, keys_ref, values_ref, *rest):
    out_ref, sem = rest[-2:]
    run_all(
        [
            (source.at[:, pl.ds(head * HD, HD)], out_ref.at[:, pl.ds(side * HD, HD)])
            for side, source in enumerate((keys_ref, values_ref))
        ],
        sem,
    )


def pair_of(head, keys, values, after):
    rows = keys.shape[0]
    return pl.pallas_call(
        functools.partial(pair_kernel, head),
        out_shape=jax.ShapeDtypeStruct((rows, 2 * HD), keys.dtype),
        in_specs=[HBM] * (2 + len(after)),
        out_specs=VMEM,
        scratch_shapes=[pltpu.SemaphoreType.DMA((2,))],
        compiler_params=pltpu.CompilerParams(vmem_limit_bytes=8 << 20),
        cost_estimate=pl.CostEstimate(flops=0, bytes_accessed=8 * rows * HD, transcendentals=0),
    )(keys, values, *after)


def joined_kernel(pieces, parity_ref, *rest):
    refs, out_ref, sem = rest[:-2], rest[-2], rest[-1]
    to = 0
    for rows, even, odd in pieces:
        for value, (index, low) in enumerate((even, odd)):

            @pl.when(parity_ref[0] == value)
            def _():
                pltpu.make_async_copy(
                    refs[index].at[pl.ds(low, rows)], out_ref.at[pl.ds(to, rows)], sem
                ).start()

        to += rows
    pltpu.make_async_copy(out_ref, out_ref, sem).wait()


def joined(parity, pieces, after=()):
    arrays = []
    plan = []
    for rows, *sources in pieces:
        found = []
        for array, low in sources:
            at = [k for k, known in enumerate(arrays) if known is array]
            if not at:
                at = [len(arrays)]
                arrays.append(array)
            found.append((at[0], low))
        plan.append((rows, *found))
    total = sum(rows for rows, *_ in plan)
    return pl.pallas_call(
        functools.partial(joined_kernel, plan),
        out_shape=jax.ShapeDtypeStruct((total, 2 * HD), jnp.bfloat16),
        in_specs=[SMEM] + [HBM] * (len(arrays) + len(after)),
        out_specs=VMEM,
        scratch_shapes=[pltpu.SemaphoreType.DMA],
        compiler_params=pltpu.CompilerParams(vmem_limit_bytes=8 << 20),
        cost_estimate=pl.CostEstimate(flops=0, bytes_accessed=8 * total * HD, transcendentals=0),
    )(parity, *arrays, *after)


def listed_kernel(lows, place_ref, source_ref, *rest):
    refs, out_ref, sem = rest[:-2], rest[-2], rest[-1]
    for head in range(out_ref.shape[0]):

        def block(index, slot):
            return refs[index].at[pl.ds(lows[index] + (head * MOWN + slot) * BLK, BLK)]

        def put(found, target):
            pltpu.make_async_copy(found, out_ref.at[head, target], sem).start()

        for index in range(len(refs)):
            for slot in range(MOWN):
                place = place_ref[index, head, slot]
                pl.when(place >= 0)(
                    functools.partial(put, block(index, slot), blocks_at(place))
                )
        for entry in range(NV):
            pl.when(source_ref[head, entry] < 0)(
                functools.partial(put, block(0, 0), pl.ds(entry * BLK, BLK))
            )
    pltpu.make_async_copy(out_ref, out_ref, sem).wait()


def listed_blocks(place, source, slots):
    heads = source.shape[0]
    return pl.pallas_call(
        functools.partial(listed_kernel, [low for _, low in slots]),
        out_shape=jax.ShapeDtypeStruct((heads, NV * BLK, 2 * HD), jnp.bfloat16),
        in_specs=[SMEM, SMEM] + [HBM] * len(slots),
        out_specs=VMEM,
        scratch_shapes=[pltpu.SemaphoreType.DMA],
        compiler_params=pltpu.CompilerParams(vmem_limit_bytes=8 << 20),
        cost_estimate=pl.CostEstimate(
            flops=0, bytes_accessed=8 * heads * NV * BLK * HD, transcendentals=0
        ),
    )(place, source, *[array for array, _ in slots])


def attend_kernel(
    head, parts, bounds, waits, part_blocks, group_heads, part_ref, slash_ref, bias_ref, query_ref,
    vert_ref, own_ref, *rest,
):
    chunks = len(bounds) - 1
    two_back = rest[:chunks]
    one_back = rest[chunks : 2 * chunks]
    rest = rest[2 * chunks + waits :]
    out_refs = rest[:parts]
    (
        queries, out, vert, vert_keys, window, scores_a, scores_b, weights_a, weights_b, max_a,
        max_b, diagonal_ref, query_sem, vert_sem, window_sem, out_sem,
    ) = rest[parts:]
    scores, weights, maxima = (scores_a, scores_b), (weights_a, weights_b), (max_a, max_b)
    tok_rows = own_ref.shape[0]
    blocks_dev = tok_rows // BLK
    part_rows = part_blocks * BLK
    group_cols = group_heads * HD
    last = parts * part_blocks - 1
    step = pl.program_id(0)
    scale = 1.0 / math.sqrt(HD)
    contract = (((1,), (1,)), ((), ()))

    def shard_block(block):
        return part_ref[block // part_blocks] * part_blocks + lax.rem(block, part_blocks)

    def slash_rows(block):
        first = LOOK * blocks_dev + shard_block(block)
        return [blocks_at(first - slash_ref[head, entry]) for entry in range(NS)]

    def query_of(block):
        rows = blocks_at(block)
        return jnp.concatenate(
            [queries[rows, h * HD : (h + 1) * HD] for h in range(group_heads)], axis=0
        )

    def score_tile(query, bias, rows, tile):
        low = tile * TILE
        if low < NV * BLK:
            found = jnp.dot(
                query, vert_keys[:, low : low + TILE], preferred_element_type=jnp.float32
            )
        else:
            entry = (low - NV * BLK) // BLK
            keys = jnp.concatenate(
                [window[r, :HD] for r in rows[entry : entry + TILE // BLK]], axis=0
            )
            found = lax.dot_general(query, keys, contract, preferred_element_type=jnp.float32)
        found = found + bias[:, low : low + TILE]
        if low == NV * BLK:
            diagonal = jnp.concatenate([diagonal_ref[...]] * group_heads, axis=0)
            found = jnp.concatenate(
                [found[:, : 2 * BLK] + diagonal, found[:, 2 * BLK :]], axis=1
            )
        return found

    def weighted_values(block, at):
        ones = jnp.ones(((NV + NS) * BLK, HD), jnp.bfloat16)
        values = jnp.concatenate([vert[:, HD:]] + [window[r, HD:] for r in slash_rows(block)], axis=0)
        return jnp.dot(
            weights[at][...],
            jnp.concatenate([values, ones], axis=1),
            preferred_element_type=jnp.float32,
        )

    def store(total, block):
        result = (total[:, :HD] / total[:, HD:]).astype(jnp.bfloat16)
        rows = blocks_at(block)
        for h in range(group_heads):
            out[rows, h * HD : (h + 1) * HD] = result[h * BLK : (h + 1) * BLK]

    def stage(block, at, score, weigh, combine, arrives=False):
        other = 1 - at
        if score:
            fresh = jnp.minimum(block, last)
            query = query_of(fresh)
            rows = slash_rows(fresh)
            bias = bias_ref[pl.ds(head * blocks_dev + shard_block(fresh), 1), :]
        if combine:
            done = jnp.maximum(block - 2, 0)
            total = weighted_values(done, at)
        if weigh:
            row_max = maxima[other][...]
            row_max = jnp.concatenate([row_max] * (TILE // HD), axis=1)
        highest = None
        for tile in range((NV + NS) * BLK // TILE):
            low = tile * TILE
            if arrives and low == NV * BLK:
                pltpu.make_async_copy(window, window, window_sem).wait()
            if score:
                found = score_tile(query, bias, rows, tile)
                scores[at][:, low : low + TILE] = found
                for piece_low in range(0, TILE, HD):
                    piece = found[:, piece_low : piece_low + HD]
                    highest = piece if highest is None else jnp.maximum(highest, piece)
            if weigh:
                weights[other][:, low : low + TILE] = jnp.exp(
                    (scores[other][:, low : low + TILE] - row_max) * scale
                ).astype(jnp.bfloat16)
        if score:
            maxima[at][...] = jnp.broadcast_to(
                jnp.max(highest, axis=1, keepdims=True), highest.shape
            )
        if combine:
            store(total, done)

    @pl.when(step == 0)
    def _():
        for k in range(parts):
            pltpu.make_async_copy(
                query_ref.at[
                    pl.ds(pl.multiple_of(part_ref[k] * part_rows, part_rows), part_rows),
                    pl.ds(head * group_cols, group_cols),
                ],
                queries.at[pl.ds(k * part_rows, part_rows)],
                query_sem,
            ).start()
        pltpu.make_async_copy(vert_ref.at[head], vert, vert_sem).start()
        for back, sources in enumerate((two_back, one_back)):
            for chunk, source in enumerate(sources):
                rows = bounds[chunk + 1] - bounds[chunk]
                pltpu.make_async_copy(
                    source.at[pl.ds(0, rows)],
                    window.at[pl.ds(back * tok_rows + bounds[chunk], rows)],
                    window_sem,
                ).start()
        pltpu.make_async_copy(
            own_ref, window.at[pl.ds(LOOK * tok_rows, tok_rows)], window_sem
        ).start()
        column = lax.broadcasted_iota(jnp.int32, (BLK, 2 * BLK), 1)
        row = lax.broadcasted_iota(jnp.int32, (BLK, 2 * BLK), 0)
        diagonal_ref[...] = jnp.where((column < BLK) & (column > row), NEG, 0.0).astype(jnp.float32)
        weights_b[...] = jnp.zeros_like(weights_b)
        pltpu.make_async_copy(vert, vert, vert_sem).wait()
        vert_keys[...] = vert[:, :HD].T
        pltpu.make_async_copy(queries, queries, query_sem).wait()
        stage(0, 0, True, False, False, True)

    first = step * STEP_BLOCKS
    stage(first + 1, 1, True, True, True)
    stage(first + 2, 0, True, True, True)

    @pl.when(first + STEP_BLOCKS > last)
    def _():
        store(weighted_values(last, 1), last)
        for k in range(parts):
            pltpu.make_async_copy(
                out.at[pl.ds(k * part_rows, part_rows)], out_refs[k], out_sem.at[k]
            ).start()
        for k in range(parts):
            pltpu.make_async_copy(
                out.at[pl.ds(k * part_rows, part_rows)], out_refs[k], out_sem.at[k]
            ).wait()


def attend(head, part, bounds, slash, bias, queries, vert, own, two_back, one_back, part_rows, after):
    parts = part.shape[0]
    group_cols = queries.shape[1] // slash.shape[0]
    group_heads = group_cols // HD
    part_blocks = part_rows // BLK
    tok_rows = own.shape[0]
    rows = group_heads * BLK
    keys_seen = (NV + NS) * BLK
    return pl.pallas_call(
        functools.partial(
            attend_kernel, head, parts, bounds, len(after), part_blocks, group_heads
        ),
        out_shape=[jax.ShapeDtypeStruct((part_rows, group_cols), jnp.bfloat16)] * parts,
        grid_spec=pltpu.PrefetchScalarGridSpec(
            num_scalar_prefetch=2,
            grid=(parts * part_blocks // STEP_BLOCKS,),
            in_specs=[pl.BlockSpec(bias.shape, lambda s, *_: (0, 0))] + [HBM] * (3 + 2 * len(two_back) + len(after)),
            out_specs=[HBM] * parts,
            scratch_shapes=[
                pltpu.VMEM((parts * part_rows, group_cols), jnp.bfloat16),
                pltpu.VMEM((parts * part_rows, group_cols), jnp.bfloat16),
                pltpu.VMEM((NV * BLK, 2 * HD), jnp.bfloat16),
                pltpu.VMEM((HD, NV * BLK), jnp.bfloat16),
                pltpu.VMEM(((LOOK + 1) * tok_rows, 2 * HD), jnp.bfloat16),
                pltpu.VMEM((rows, keys_seen), jnp.float32),
                pltpu.VMEM((rows, keys_seen), jnp.float32),
                pltpu.VMEM((rows, keys_seen), jnp.bfloat16),
                pltpu.VMEM((rows, keys_seen), jnp.bfloat16),
                pltpu.VMEM((rows, HD), jnp.float32),
                pltpu.VMEM((rows, HD), jnp.float32),
                pltpu.VMEM((BLK, 2 * BLK), jnp.float32),
                pltpu.SemaphoreType.DMA,
                pltpu.SemaphoreType.DMA,
                pltpu.SemaphoreType.DMA,
                pltpu.SemaphoreType.DMA((parts,)),
            ],
        ),
        compiler_params=pltpu.CompilerParams(
            dimension_semantics=("arbitrary",), vmem_limit_bytes=18 << 20
        ),
        cost_estimate=pl.CostEstimate(
            flops=4 * parts * part_rows * group_heads * keys_seen * HD,
            bytes_accessed=4 * parts * part_rows * group_cols + 12 * tok_rows * HD,
            transcendentals=parts * part_rows * group_heads * keys_seen,
        ),
    )(part, slash, bias, queries, vert, own, *two_back, *one_back, *after)


def local(queries, keys, values, vertical, slash):
    shard_count = lax.axis_size("ctx")
    shard_index = lax.axis_index("ctx")
    head_count = lax.axis_size("head")
    head_index = lax.axis_index("head")
    tok_rows = queries.shape[0]
    kv_local = keys.shape[1] // HD
    group_cols = queries.shape[1] // kv_local
    blocks_dev = tok_rows // BLK
    part_rows = tok_rows // head_count
    partner = shard_index ^ 1
    two_pairs = [(i, (i + 2) % shard_count) for i in range(shard_count)]
    across_pairs = [(i, i ^ 1) for i in range(shard_count)]
    parity = (shard_index % 2).reshape(1).astype(jnp.int32)

    owners = vertical // blocks_dev
    order = jnp.arange(NV, dtype=jnp.int32)
    same_owner = owners[:, :, None] == owners[:, None, :]
    earlier = order[None, :] < order[:, None]
    slot_rank = jnp.sum((same_owner & earlier[None]).astype(jnp.int32), axis=2)
    slots = jnp.arange(MOWN, dtype=jnp.int32)
    in_slot = slot_rank[:, :, None] == slots
    local_block = jnp.sum(
        ((owners == shard_index)[:, :, None] & in_slot) * (vertical % blocks_dev)[:, :, None],
        axis=1,
    )
    distances = 2 * jnp.arange(shard_count // 2, dtype=jnp.int32)
    array_owner = jnp.concatenate([shard_index - distances, partner - distances])
    array_owner = jnp.where(array_owner <= shard_index, array_owner, -1)
    here = (array_owner[:, None, None] == owners)[:, :, :, None] & in_slot[None]
    place = jnp.sum(here * (order + 1)[None, None, :, None], axis=2) - 1
    source = jnp.where(owners <= shard_index, 0, -1).astype(jnp.int32)

    slash_rank = jnp.sum((slash[:, None, :] < slash[:, :, None]).astype(jnp.int32), axis=2)
    at_rank = slash_rank[:, :, None] == jnp.arange(NS, dtype=jnp.int32)
    slash = jnp.sum(at_rank * slash[:, :, None], axis=1)

    global_blocks = shard_index * blocks_dev + jnp.arange(blocks_dev, dtype=jnp.int32)
    vert_valid = vertical[:, None, :] < global_blocks[None, :, None]
    slash_blocks = global_blocks[None, :, None] - slash[:, None, :]
    in_vertical = jnp.any(slash_blocks[:, :, :, None] == vertical[:, None, None, :], axis=3)
    slash_valid = (slash[:, None, :] == 0) | ((slash_blocks >= 0) & jnp.logical_not(in_vertical))
    valid = jnp.concatenate([vert_valid, slash_valid], axis=2)
    listed = jnp.arange(NV + NS, dtype=jnp.int32)
    spread = (jnp.arange((NV + NS) * BLK, dtype=jnp.int32) // BLK == listed[:, None])
    barred = jnp.where(valid, 0.0, NEG).reshape(kv_local * blocks_dev, NV + NS)
    bias = jnp.dot(
        barred.astype(jnp.bfloat16), spread.astype(jnp.bfloat16), preferred_element_type=jnp.float32
    )

    steps = shard_count // 2 - 1
    bounds = [k * blocks_dev // steps * BLK for k in range(steps + 1)]
    slot_rows = kv_local * MOWN * BLK
    own, send, slots_own = first_of(bounds[1], local_block, keys, values)
    behind = [(slots_own, 0)]
    across = []
    two_back = []
    one_back = []
    for step in range(steps):
        rows = bounds[step + 1] - bounds[step]
        here = (own, bounds[step])
        if step:
            send = joined(
                parity, [(rows, here, here), (slot_rows, behind[-1], behind[-1])],
                [cross] + one_back[-2:-1],
            )
        come = lax.ppermute(send, "ctx", two_pairs)
        if step == 0:
            across.append((lax.ppermute(slots_own, "ctx", across_pairs), 0))
        two_back.append(come)
        behind.append((come, rows))
        cross = joined(parity, [(rows, here, (come, 0)), (slot_rows, behind[-1], behind[-1])])
        one_back.append(lax.ppermute(cross, "ctx", across_pairs))
        across.append((one_back[-1], rows))
    slots = behind + across
    windows = [(bounds, own, two_back, one_back)]
    after = two_back[-2:-1] + [send]
    for head in range(1, kv_local):
        own = pair_of(head, keys, values, after)
        come = lax.ppermute(own, "ctx", two_pairs)
        windows.append(([0, tok_rows], own, [come], None))
        after = [come]

    out = jnp.zeros((part_rows, head_count * kv_local * group_cols), jnp.bfloat16)
    after = []
    half = head_count // 2
    calls = [[[head_count - 1], list(range(head_count - 2, -1, -1))]] * (kv_local - 1)
    calls.append([[flip] for flip in range(head_count - 1, half - 1, -1)])
    calls[-1].append(list(range(half - 1, -1, -1)))
    vert = listed_blocks(place, source, slots)
    for head in range(kv_local):
        bounds, own, two_back, one_back = windows[head]
        for flips in calls[head]:
            others = [head_index ^ flip for flip in flips]
            pieces = attend(
                head, jnp.stack(others).astype(jnp.int32), bounds, slash, bias, queries, vert, own,
                two_back, one_back, part_rows, after,
            )
            after = [pieces[-1]]
            if flips == calls[head][0] and head + 1 < kv_local:
                near, own_next, (come,), _ = windows[head + 1]
                cross = joined(parity, [(tok_rows, (own_next, 0), (come, 0))], after)
                crossed = lax.ppermute(cross, "ctx", across_pairs)
                windows[head + 1] = (near, own_next, [come], [crossed])
            for flip, other, piece in zip(flips, others, pieces):
                if flip:
                    piece = lax.ppermute(piece, "head", [(i, i ^ flip) for i in range(head_count)])
                out = lax.dynamic_update_slice(
                    out, piece, (0, other * kv_local * group_cols + head * group_cols)
                )
    return out


def solution(mesh):
    in_specs = (
        P("ctx", "head"),
        P("ctx", "head"),
        P("ctx", "head"),
        P("head", None),
        P("head", None),
    )
    out_specs = P(("ctx", "head"), None)
    return jax.shard_map(local, mesh=mesh, in_specs=in_specs, out_specs=out_specs, check_vma=False)
```

```python
import functools
import math

import jax
import jax.numpy as jnp
from jax import lax
from jax.experimental import pallas as pl
from jax.experimental.pallas import tpu as pltpu
from jax.sharding import PartitionSpec as P

HD = 128
BLK = 64
NV = 16
NS = 8
MOWN = 4
LOOK = 2
NEG = -1e30
STEP_BLOCKS = 2
TILE = 256
HBM = pl.BlockSpec(memory_space=pltpu.HBM)
ANY = pl.BlockSpec(memory_space=pl.ANY)
VMEM = pl.BlockSpec(memory_space=pltpu.VMEM)
SMEM = pl.BlockSpec(memory_space=pltpu.SMEM)


def blocks_at(index, count=1):
    return pl.ds(pl.multiple_of(index * BLK, BLK), count * BLK)


def run_all(copies, sem):
    copies = [pltpu.make_async_copy(*ends, sem.at[k]) for k, ends in enumerate(copies)]
    for copy in copies:
        copy.start()
    for copy in copies:
        copy.wait()


def first_kernel(local_ref, keys_ref, values_ref, own_ref, send_ref, slots_ref, sem):
    chunk_rows = send_ref.shape[0] - slots_ref.shape[0]
    copies = []
    for side, source in enumerate((keys_ref, values_ref)):
        to = pl.ds(side * HD, HD)
        for head in range(local_ref.shape[0]):
            for slot in range(MOWN):
                found = source.at[blocks_at(local_ref[head, slot]), pl.ds(head * HD, HD)]
                low = (head * MOWN + slot) * BLK
                copies.append((found, send_ref.at[pl.ds(chunk_rows + low, BLK), to]))
                copies.append((found, slots_ref.at[pl.ds(low, BLK), to]))
        rows = pl.ds(0, chunk_rows)
        copies.append((source.at[rows, pl.ds(0, HD)], send_ref.at[rows, to]))
        copies.append((source.at[:, pl.ds(0, HD)], own_ref.at[:, to]))
    run_all(copies, sem)


def first_of(chunk_rows, local_block, keys, values):
    heads = local_block.shape[0]
    rows = keys.shape[0]
    slot_rows = heads * MOWN * BLK
    return pl.pallas_call(
        first_kernel,
        out_shape=[
            jax.ShapeDtypeStruct((rows, 2 * HD), keys.dtype),
            jax.ShapeDtypeStruct((chunk_rows + slot_rows, 2 * HD), keys.dtype),
            jax.ShapeDtypeStruct((slot_rows, 2 * HD), keys.dtype),
        ],
        in_specs=[SMEM, HBM, HBM],
        out_specs=[VMEM] * 3,
        scratch_shapes=[pltpu.SemaphoreType.DMA((4 * heads * MOWN + 4,))],
        compiler_params=pltpu.CompilerParams(vmem_limit_bytes=8 << 20),
        cost_estimate=pl.CostEstimate(flops=0, bytes_accessed=16 * rows * HD, transcendentals=0),
    )(local_block, keys, values)


def pair_kernel(head, keys_ref, values_ref, *rest):
    out_ref, sem = rest[-2:]
    run_all(
        [
            (source.at[:, pl.ds(head * HD, HD)], out_ref.at[:, pl.ds(side * HD, HD)])
            for side, source in enumerate((keys_ref, values_ref))
        ],
        sem,
    )


def pair_of(head, keys, values, after):
    rows = keys.shape[0]
    return pl.pallas_call(
        functools.partial(pair_kernel, head),
        out_shape=jax.ShapeDtypeStruct((rows, 2 * HD), keys.dtype),
        in_specs=[HBM] * (2 + len(after)),
        out_specs=VMEM,
        scratch_shapes=[pltpu.SemaphoreType.DMA((2,))],
        compiler_params=pltpu.CompilerParams(vmem_limit_bytes=8 << 20),
        cost_estimate=pl.CostEstimate(flops=0, bytes_accessed=8 * rows * HD, transcendentals=0),
    )(keys, values, *after)


def joined_kernel(pieces, parity_ref, *rest):
    refs, out_ref, sem = rest[:-2], rest[-2], rest[-1]
    to = 0
    for rows, even, odd in pieces:
        for value, (index, low) in enumerate((even, odd)):

            @pl.when(parity_ref[0] == value)
            def _():
                pltpu.make_async_copy(
                    refs[index].at[pl.ds(low, rows)], out_ref.at[pl.ds(to, rows)], sem
                ).start()

        to += rows
    pltpu.make_async_copy(out_ref, out_ref, sem).wait()


def joined(parity, pieces, after=()):
    arrays = []
    plan = []
    for rows, *sources in pieces:
        found = []
        for array, low in sources:
            at = [k for k, known in enumerate(arrays) if known is array]
            if not at:
                at = [len(arrays)]
                arrays.append(array)
            found.append((at[0], low))
        plan.append((rows, *found))
    total = sum(rows for rows, *_ in plan)
    return pl.pallas_call(
        functools.partial(joined_kernel, plan),
        out_shape=jax.ShapeDtypeStruct((total, 2 * HD), jnp.bfloat16),
        in_specs=[SMEM] + [HBM] * (len(arrays) + len(after)),
        out_specs=VMEM,
        scratch_shapes=[pltpu.SemaphoreType.DMA],
        compiler_params=pltpu.CompilerParams(vmem_limit_bytes=8 << 20),
        cost_estimate=pl.CostEstimate(flops=0, bytes_accessed=8 * total * HD, transcendentals=0),
    )(parity, *arrays, *after)


def listed_kernel(lows, place_ref, source_ref, *rest):
    refs, out_ref, sem = rest[:-2], rest[-2], rest[-1]
    for head in range(out_ref.shape[0]):

        def block(index, slot):
            return refs[index].at[pl.ds(lows[index] + (head * MOWN + slot) * BLK, BLK)]

        def put(found, target):
            pltpu.make_async_copy(found, out_ref.at[head, target], sem).start()

        for index in range(len(refs)):
            for slot in range(MOWN):
                place = place_ref[index, head, slot]
                pl.when(place >= 0)(
                    functools.partial(put, block(index, slot), blocks_at(place))
                )
        for entry in range(NV):
            pl.when(source_ref[head, entry] < 0)(
                functools.partial(put, block(0, 0), pl.ds(entry * BLK, BLK))
            )
    pltpu.make_async_copy(out_ref, out_ref, sem).wait()


def listed_blocks(place, source, slots):
    heads = source.shape[0]
    return pl.pallas_call(
        functools.partial(listed_kernel, [low for _, low in slots]),
        out_shape=jax.ShapeDtypeStruct((heads, NV * BLK, 2 * HD), jnp.bfloat16),
        in_specs=[SMEM, SMEM] + [HBM] * len(slots),
        out_specs=VMEM,
        scratch_shapes=[pltpu.SemaphoreType.DMA],
        compiler_params=pltpu.CompilerParams(vmem_limit_bytes=8 << 20),
        cost_estimate=pl.CostEstimate(
            flops=0, bytes_accessed=8 * heads * NV * BLK * HD, transcendentals=0
        ),
    )(place, source, *[array for array, _ in slots])


def attend_kernel(
    head, parts, bounds, waits, part_blocks, group_heads, part_ref, slash_ref, bias_ref, query_ref,
    vert_ref, own_ref, *rest,
):
    chunks = len(bounds) - 1
    two_back = rest[:chunks]
    one_back = rest[chunks : 2 * chunks]
    rest = rest[2 * chunks + waits :]
    out_refs = rest[:parts]
    (
        queries, out, vert, vert_keys, window, scores_a, scores_b, weights_a, weights_b, max_a,
        max_b, diagonal_ref, query_sem, vert_sem, window_sem, out_sem,
    ) = rest[parts:]
    scores, weights, maxima = (scores_a, scores_b), (weights_a, weights_b), (max_a, max_b)
    tok_rows = own_ref.shape[0]
    blocks_dev = tok_rows // BLK
    part_rows = part_blocks * BLK
    group_cols = group_heads * HD
    last = parts * part_blocks - 1
    step = pl.program_id(0)
    scale = 1.0 / math.sqrt(HD)
    contract = (((1,), (1,)), ((), ()))

    def shard_block(block):
        return part_ref[block // part_blocks] * part_blocks + lax.rem(block, part_blocks)

    def slash_rows(block):
        first = LOOK * blocks_dev + shard_block(block)
        return [blocks_at(first - slash_ref[head, entry]) for entry in range(NS)]

    def query_of(block):
        rows = blocks_at(block)
        return jnp.concatenate(
            [queries[rows, h * HD : (h + 1) * HD] for h in range(group_heads)], axis=0
        )

    def score_tile(query, bias, rows, tile):
        low = tile * TILE
        if low < NV * BLK:
            found = jnp.dot(
                query, vert_keys[:, low : low + TILE], preferred_element_type=jnp.float32
            )
        else:
            entry = (low - NV * BLK) // BLK
            keys = jnp.concatenate(
                [window[r, :HD] for r in rows[entry : entry + TILE // BLK]], axis=0
            )
            found = lax.dot_general(query, keys, contract, preferred_element_type=jnp.float32)
        found = found + bias[:, low : low + TILE]
        if low == NV * BLK:
            diagonal = jnp.concatenate([diagonal_ref[...]] * group_heads, axis=0)
            found = jnp.concatenate(
                [found[:, : 2 * BLK] + diagonal, found[:, 2 * BLK :]], axis=1
            )
        return found

    def weighted_values(block, at):
        ones = jnp.ones(((NV + NS) * BLK, HD), jnp.bfloat16)
        values = jnp.concatenate([vert[:, HD:]] + [window[r, HD:] for r in slash_rows(block)], axis=0)
        return jnp.dot(
            weights[at][...],
            jnp.concatenate([values, ones], axis=1),
            preferred_element_type=jnp.float32,
        )

    def store(total, block):
        result = (total[:, :HD] / total[:, HD:]).astype(jnp.bfloat16)
        rows = blocks_at(block)
        for h in range(group_heads):
            out[rows, h * HD : (h + 1) * HD] = result[h * BLK : (h + 1) * BLK]

    def stage(block, at, score, weigh, combine, arrives=False):
        other = 1 - at
        if score:
            fresh = jnp.minimum(block, last)
            query = query_of(fresh)
            rows = slash_rows(fresh)
            bias = bias_ref[pl.ds(head * blocks_dev + shard_block(fresh), 1), :]
        if combine:
            done = jnp.maximum(block - 2, 0)
            total = weighted_values(done, at)
        if weigh:
            row_max = maxima[other][...]
            row_max = jnp.concatenate([row_max] * (TILE // HD), axis=1)
        highest = None
        for tile in range((NV + NS) * BLK // TILE):
            low = tile * TILE
            if arrives and low == NV * BLK:
                pltpu.make_async_copy(window, window, window_sem).wait()
            if score:
                found = score_tile(query, bias, rows, tile)
                scores[at][:, low : low + TILE] = found
                for piece_low in range(0, TILE, HD):
                    piece = found[:, piece_low : piece_low + HD]
                    highest = piece if highest is None else jnp.maximum(highest, piece)
            if weigh:
                weights[other][:, low : low + TILE] = jnp.exp(
                    (scores[other][:, low : low + TILE] - row_max) * scale
                ).astype(jnp.bfloat16)
        if score:
            maxima[at][...] = jnp.broadcast_to(
                jnp.max(highest, axis=1, keepdims=True), highest.shape
            )
        if combine:
            store(total, done)

    @pl.when(step == 0)
    def _():
        for k in range(parts):
            pltpu.make_async_copy(
                query_ref.at[
                    pl.ds(pl.multiple_of(part_ref[k] * part_rows, part_rows), part_rows),
                    pl.ds(head * group_cols, group_cols),
                ],
                queries.at[pl.ds(k * part_rows, part_rows)],
                query_sem,
            ).start()
        pltpu.make_async_copy(vert_ref.at[head], vert, vert_sem).start()
        for back, sources in enumerate((two_back, one_back)):
            for chunk, source in enumerate(sources):
                rows = bounds[chunk + 1] - bounds[chunk]
                pltpu.make_async_copy(
                    source.at[pl.ds(0, rows)],
                    window.at[pl.ds(back * tok_rows + bounds[chunk], rows)],
                    window_sem,
                ).start()
        pltpu.make_async_copy(
            own_ref, window.at[pl.ds(LOOK * tok_rows, tok_rows)], window_sem
        ).start()
        column = lax.broadcasted_iota(jnp.int32, (BLK, 2 * BLK), 1)
        row = lax.broadcasted_iota(jnp.int32, (BLK, 2 * BLK), 0)
        diagonal_ref[...] = jnp.where((column < BLK) & (column > row), NEG, 0.0).astype(jnp.float32)
        weights_b[...] = jnp.zeros_like(weights_b)
        pltpu.make_async_copy(vert, vert, vert_sem).wait()
        vert_keys[...] = vert[:, :HD].T
        pltpu.make_async_copy(queries, queries, query_sem).wait()
        stage(0, 0, True, False, False, True)

    first = step * STEP_BLOCKS
    stage(first + 1, 1, True, True, True)
    stage(first + 2, 0, True, True, True)

    @pl.when(first + STEP_BLOCKS > last)
    def _():
        store(weighted_values(last, 1), last)
        for k in range(parts):
            pltpu.make_async_copy(
                out.at[pl.ds(k * part_rows, part_rows)], out_refs[k], out_sem.at[k]
            ).start()
        for k in range(parts):
            pltpu.make_async_copy(
                out.at[pl.ds(k * part_rows, part_rows)], out_refs[k], out_sem.at[k]
            ).wait()


def attend(head, part, bounds, slash, bias, queries, vert, own, two_back, one_back, part_rows, after):
    parts = part.shape[0]
    group_cols = queries.shape[1] // slash.shape[0]
    group_heads = group_cols // HD
    part_blocks = part_rows // BLK
    tok_rows = own.shape[0]
    rows = group_heads * BLK
    keys_seen = (NV + NS) * BLK
    return pl.pallas_call(
        functools.partial(
            attend_kernel, head, parts, bounds, len(after), part_blocks, group_heads
        ),
        out_shape=[jax.ShapeDtypeStruct((part_rows, group_cols), jnp.bfloat16)] * parts,
        grid_spec=pltpu.PrefetchScalarGridSpec(
            num_scalar_prefetch=2,
            grid=(parts * part_blocks // STEP_BLOCKS,),
            in_specs=[pl.BlockSpec(bias.shape, lambda s, *_: (0, 0))] + [ANY] * (3 + 2 * len(two_back) + len(after)),
            out_specs=[ANY] * parts,
            scratch_shapes=[
                pltpu.VMEM((parts * part_rows, group_cols), jnp.bfloat16),
                pltpu.VMEM((parts * part_rows, group_cols), jnp.bfloat16),
                pltpu.VMEM((NV * BLK, 2 * HD), jnp.bfloat16),
                pltpu.VMEM((HD, NV * BLK), jnp.bfloat16),
                pltpu.VMEM(((LOOK + 1) * tok_rows, 2 * HD), jnp.bfloat16),
                pltpu.VMEM((rows, keys_seen), jnp.float32),
                pltpu.VMEM((rows, keys_seen), jnp.float32),
                pltpu.VMEM((rows, keys_seen), jnp.bfloat16),
                pltpu.VMEM((rows, keys_seen), jnp.bfloat16),
                pltpu.VMEM((rows, HD), jnp.float32),
                pltpu.VMEM((rows, HD), jnp.float32),
                pltpu.VMEM((BLK, 2 * BLK), jnp.float32),
                pltpu.SemaphoreType.DMA,
                pltpu.SemaphoreType.DMA,
                pltpu.SemaphoreType.DMA,
                pltpu.SemaphoreType.DMA((parts,)),
            ],
        ),
        compiler_params=pltpu.CompilerParams(
            dimension_semantics=("arbitrary",), vmem_limit_bytes=32 << 20
        ),
        cost_estimate=pl.CostEstimate(
            flops=4 * parts * part_rows * group_heads * keys_seen * HD,
            bytes_accessed=4 * parts * part_rows * group_cols + 12 * tok_rows * HD,
            transcendentals=parts * part_rows * group_heads * keys_seen,
        ),
    )(part, slash, bias, queries, vert, own, *two_back, *one_back, *after)


def local(queries, keys, values, vertical, slash):
    shard_count = lax.axis_size("ctx")
    shard_index = lax.axis_index("ctx")
    head_count = lax.axis_size("head")
    head_index = lax.axis_index("head")
    tok_rows = queries.shape[0]
    kv_local = keys.shape[1] // HD
    group_cols = queries.shape[1] // kv_local
    blocks_dev = tok_rows // BLK
    part_rows = tok_rows // head_count
    partner = shard_index ^ 1
    two_pairs = [(i, (i + 2) % shard_count) for i in range(shard_count)]
    across_pairs = [(i, i ^ 1) for i in range(shard_count)]
    parity = (shard_index % 2).reshape(1).astype(jnp.int32)

    owners = vertical // blocks_dev
    order = jnp.arange(NV, dtype=jnp.int32)
    same_owner = owners[:, :, None] == owners[:, None, :]
    earlier = order[None, :] < order[:, None]
    slot_rank = jnp.sum((same_owner & earlier[None]).astype(jnp.int32), axis=2)
    slots = jnp.arange(MOWN, dtype=jnp.int32)
    in_slot = slot_rank[:, :, None] == slots
    local_block = jnp.sum(
        ((owners == shard_index)[:, :, None] & in_slot) * (vertical % blocks_dev)[:, :, None],
        axis=1,
    )
    distances = 2 * jnp.arange(shard_count // 2, dtype=jnp.int32)
    array_owner = jnp.concatenate([shard_index - distances, partner - distances])
    array_owner = jnp.where(array_owner <= shard_index, array_owner, -1)
    here = (array_owner[:, None, None] == owners)[:, :, :, None] & in_slot[None]
    place = jnp.sum(here * (order + 1)[None, None, :, None], axis=2) - 1
    source = jnp.where(owners <= shard_index, 0, -1).astype(jnp.int32)

    slash_rank = jnp.sum((slash[:, None, :] < slash[:, :, None]).astype(jnp.int32), axis=2)
    at_rank = slash_rank[:, :, None] == jnp.arange(NS, dtype=jnp.int32)
    slash = jnp.sum(at_rank * slash[:, :, None], axis=1)

    global_blocks = shard_index * blocks_dev + jnp.arange(blocks_dev, dtype=jnp.int32)
    vert_valid = vertical[:, None, :] < global_blocks[None, :, None]
    slash_blocks = global_blocks[None, :, None] - slash[:, None, :]
    in_vertical = jnp.any(slash_blocks[:, :, :, None] == vertical[:, None, None, :], axis=3)
    slash_valid = (slash[:, None, :] == 0) | ((slash_blocks >= 0) & jnp.logical_not(in_vertical))
    valid = jnp.concatenate([vert_valid, slash_valid], axis=2)
    listed = jnp.arange(NV + NS, dtype=jnp.int32)
    spread = (jnp.arange((NV + NS) * BLK, dtype=jnp.int32) // BLK == listed[:, None])
    barred = jnp.where(valid, 0.0, NEG).reshape(kv_local * blocks_dev, NV + NS)
    bias = jnp.dot(
        barred.astype(jnp.bfloat16), spread.astype(jnp.bfloat16), preferred_element_type=jnp.float32
    )

    steps = shard_count // 2 - 1
    bounds = [k * blocks_dev // steps * BLK for k in range(steps + 1)]
    slot_rows = kv_local * MOWN * BLK
    own, send, slots_own = first_of(bounds[1], local_block, keys, values)
    behind = [(slots_own, 0)]
    across = []
    two_back = []
    one_back = []
    for step in range(steps):
        rows = bounds[step + 1] - bounds[step]
        here = (own, bounds[step])
        if step:
            send = joined(
                parity, [(rows, here, here), (slot_rows, behind[-1], behind[-1])],
                [cross] + one_back[-2:-1],
            )
        come = lax.ppermute(send, "ctx", two_pairs)
        if step == 0:
            across.append((lax.ppermute(slots_own, "ctx", across_pairs), 0))
        two_back.append(come)
        behind.append((come, rows))
        cross = joined(parity, [(rows, here, (come, 0)), (slot_rows, behind[-1], behind[-1])])
        one_back.append(lax.ppermute(cross, "ctx", across_pairs))
        across.append((one_back[-1], rows))
    slots = behind + across
    windows = [(bounds, own, two_back, one_back)]
    after = two_back[-2:-1] + [send]
    for head in range(1, kv_local):
        own = pair_of(head, keys, values, after)
        come = lax.ppermute(own, "ctx", two_pairs)
        windows.append(([0, tok_rows], own, [come], None))
        after = [come]

    out = jnp.zeros((part_rows, head_count * kv_local * group_cols), jnp.bfloat16)
    after = []
    half = head_count // 2
    calls = [[[head_count - 1], list(range(head_count - 2, -1, -1))]] * (kv_local - 1)
    calls.append([[flip] for flip in range(head_count - 1, half - 1, -1)])
    calls[-1].append(list(range(half - 1, -1, -1)))
    vert = listed_blocks(place, source, slots)
    for head in range(kv_local):
        bounds, own, two_back, one_back = windows[head]
        for flips in calls[head]:
            others = [head_index ^ flip for flip in flips]
            pieces = attend(
                head, jnp.stack(others).astype(jnp.int32), bounds, slash, bias, queries, vert, own,
                two_back, one_back, part_rows, after,
            )
            after = [pieces[-1]]
            if flips == calls[head][0] and head + 1 < kv_local:
                near, own_next, (come,), _ = windows[head + 1]
                cross = joined(parity, [(tok_rows, (own_next, 0), (come, 0))], after)
                crossed = lax.ppermute(cross, "ctx", across_pairs)
                windows[head + 1] = (near, own_next, [come], [crossed])
            for flip, other, piece in zip(flips, others, pieces):
                if flip:
                    piece = lax.ppermute(piece, "head", [(i, i ^ flip) for i in range(head_count)])
                out = lax.dynamic_update_slice(
                    out, piece, (0, other * kv_local * group_cols + head * group_cols)
                )
    return out


def solution(mesh):
    in_specs = (
        P("ctx", "head"),
        P("ctx", "head"),
        P("ctx", "head"),
        P("head", None),
        P("head", None),
    )
    out_specs = P(("ctx", "head"), None)
    return jax.shard_map(local, mesh=mesh, in_specs=in_specs, out_specs=out_specs, check_vma=False)
```

```python
import functools
import math

import jax
import jax.numpy as jnp
from jax import lax
from jax.experimental import pallas as pl
from jax.experimental.pallas import tpu as pltpu
from jax.sharding import PartitionSpec as P

HD = 128
BLK = 64
NV = 16
NS = 8
MOWN = 4
LOOK = 2
NEG = -1e30
STEP_BLOCKS = 2
TILE = 256
HBM = pl.BlockSpec(memory_space=pltpu.HBM)
ANY = pl.BlockSpec(memory_space=pl.ANY)
VMEM = pl.BlockSpec(memory_space=pltpu.VMEM)
SMEM = pl.BlockSpec(memory_space=pltpu.SMEM)


def blocks_at(index, count=1):
    return pl.ds(pl.multiple_of(index * BLK, BLK), count * BLK)


def run_all(copies, sem):
    copies = [pltpu.make_async_copy(*ends, sem.at[k]) for k, ends in enumerate(copies)]
    for copy in copies:
        copy.start()
    for copy in copies:
        copy.wait()


def first_kernel(local_ref, keys_ref, values_ref, own_ref, send_ref, slots_ref, sem):
    chunk_rows = send_ref.shape[0] - slots_ref.shape[0]
    copies = []
    for side, source in enumerate((keys_ref, values_ref)):
        to = pl.ds(side * HD, HD)
        for head in range(local_ref.shape[0]):
            for slot in range(MOWN):
                found = source.at[blocks_at(local_ref[head, slot]), pl.ds(head * HD, HD)]
                low = (head * MOWN + slot) * BLK
                copies.append((found, send_ref.at[pl.ds(chunk_rows + low, BLK), to]))
                copies.append((found, slots_ref.at[pl.ds(low, BLK), to]))
        rows = pl.ds(0, chunk_rows)
        copies.append((source.at[rows, pl.ds(0, HD)], send_ref.at[rows, to]))
        copies.append((source.at[:, pl.ds(0, HD)], own_ref.at[:, to]))
    run_all(copies, sem)


def first_of(chunk_rows, local_block, keys, values):
    heads = local_block.shape[0]
    rows = keys.shape[0]
    slot_rows = heads * MOWN * BLK
    return pl.pallas_call(
        first_kernel,
        out_shape=[
            jax.ShapeDtypeStruct((rows, 2 * HD), keys.dtype),
            jax.ShapeDtypeStruct((chunk_rows + slot_rows, 2 * HD), keys.dtype),
            jax.ShapeDtypeStruct((slot_rows, 2 * HD), keys.dtype),
        ],
        in_specs=[SMEM, HBM, HBM],
        out_specs=[VMEM] * 3,
        scratch_shapes=[pltpu.SemaphoreType.DMA((4 * heads * MOWN + 4,))],
        compiler_params=pltpu.CompilerParams(vmem_limit_bytes=8 << 20),
        cost_estimate=pl.CostEstimate(flops=0, bytes_accessed=16 * rows * HD, transcendentals=0),
    )(local_block, keys, values)


def pair_kernel(head, keys_ref, values_ref, *rest):
    out_ref, sem = rest[-2:]
    run_all(
        [
            (source.at[:, pl.ds(head * HD, HD)], out_ref.at[:, pl.ds(side * HD, HD)])
            for side, source in enumerate((keys_ref, values_ref))
        ],
        sem,
    )


def pair_of(head, keys, values, after):
    rows = keys.shape[0]
    return pl.pallas_call(
        functools.partial(pair_kernel, head),
        out_shape=jax.ShapeDtypeStruct((rows, 2 * HD), keys.dtype),
        in_specs=[HBM] * (2 + len(after)),
        out_specs=VMEM,
        scratch_shapes=[pltpu.SemaphoreType.DMA((2,))],
        compiler_params=pltpu.CompilerParams(vmem_limit_bytes=8 << 20),
        cost_estimate=pl.CostEstimate(flops=0, bytes_accessed=8 * rows * HD, transcendentals=0),
    )(keys, values, *after)


def joined_kernel(pieces, parity_ref, *rest):
    refs, out_ref, sem = rest[:-2], rest[-2], rest[-1]
    to = 0
    for rows, even, odd in pieces:
        for value, (index, low) in enumerate((even, odd)):
            copy = pltpu.make_async_copy(
                refs[index].at[pl.ds(low, rows)], out_ref.at[pl.ds(to, rows)], sem
            )
            if even != odd:
                pl.when(parity_ref[0] == value)(copy.start)
            elif value:
                copy.start()

        to += rows
    pltpu.make_async_copy(out_ref, out_ref, sem).wait()


def joined(parity, pieces, after=()):
    arrays = []
    plan = []
    for rows, *sources in pieces:
        found = []
        for array, low in sources:
            at = [k for k, known in enumerate(arrays) if known is array]
            if not at:
                at = [len(arrays)]
                arrays.append(array)
            found.append((at[0], low))
        plan.append((rows, *found))
    total = sum(rows for rows, *_ in plan)
    return pl.pallas_call(
        functools.partial(joined_kernel, plan),
        out_shape=jax.ShapeDtypeStruct((total, 2 * HD), jnp.bfloat16),
        in_specs=[SMEM] + [HBM] * (len(arrays) + len(after)),
        out_specs=VMEM,
        scratch_shapes=[pltpu.SemaphoreType.DMA],
        compiler_params=pltpu.CompilerParams(vmem_limit_bytes=8 << 20),
        cost_estimate=pl.CostEstimate(flops=0, bytes_accessed=8 * total * HD, transcendentals=0),
    )(parity, *arrays, *after)


def listed_kernel(lows, place_ref, source_ref, *rest):
    refs, out_ref, sem = rest[:-2], rest[-2], rest[-1]
    for head in range(out_ref.shape[0]):

        def block(index, slot):
            return refs[index].at[pl.ds(lows[index] + (head * MOWN + slot) * BLK, BLK)]

        def put(found, target):
            pltpu.make_async_copy(found, out_ref.at[head, target], sem).start()

        for index in range(len(refs)):
            for slot in range(MOWN):
                place = place_ref[index, head, slot]
                pl.when(place >= 0)(
                    functools.partial(put, block(index, slot), blocks_at(place))
                )
        for entry in range(NV):
            pl.when(source_ref[head, entry] < 0)(
                functools.partial(put, block(0, 0), pl.ds(entry * BLK, BLK))
            )
    pltpu.make_async_copy(out_ref, out_ref, sem).wait()


def listed_blocks(place, source, slots):
    heads = source.shape[0]
    return pl.pallas_call(
        functools.partial(listed_kernel, [low for _, low in slots]),
        out_shape=jax.ShapeDtypeStruct((heads, NV * BLK, 2 * HD), jnp.bfloat16),
        in_specs=[SMEM, SMEM] + [HBM] * len(slots),
        out_specs=VMEM,
        scratch_shapes=[pltpu.SemaphoreType.DMA],
        compiler_params=pltpu.CompilerParams(vmem_limit_bytes=8 << 20),
        cost_estimate=pl.CostEstimate(
            flops=0, bytes_accessed=8 * heads * NV * BLK * HD, transcendentals=0
        ),
    )(place, source, *[array for array, _ in slots])


def attend_kernel(
    head, parts, waits, part_blocks, group_heads, part_ref, slash_ref, bias_ref, query_ref,
    vert_ref, window, *rest,
):
    rest = rest[waits:]
    out_refs = rest[:parts]
    (
        queries, out, vert, vert_keys, scores_a, scores_b, weights_a, weights_b, max_a,
        max_b, diagonal_ref, query_sem, vert_sem, out_sem,
    ) = rest[parts:]
    scores, weights, maxima = (scores_a, scores_b), (weights_a, weights_b), (max_a, max_b)
    blocks_dev = window.shape[0] // ((LOOK + 1) * BLK)
    part_rows = part_blocks * BLK
    group_cols = group_heads * HD
    last = parts * part_blocks - 1
    step = pl.program_id(0)
    scale = 1.0 / math.sqrt(HD)
    contract = (((1,), (1,)), ((), ()))

    def shard_block(block):
        return part_ref[block // part_blocks] * part_blocks + lax.rem(block, part_blocks)

    def slash_rows(block):
        first = LOOK * blocks_dev + shard_block(block)
        return [blocks_at(first - slash_ref[head, entry]) for entry in range(NS)]

    def query_of(block):
        rows = blocks_at(block)
        return jnp.concatenate(
            [queries[rows, h * HD : (h + 1) * HD] for h in range(group_heads)], axis=0
        )

    def score_tile(query, bias, rows, tile):
        low = tile * TILE
        if low < NV * BLK:
            found = jnp.dot(
                query, vert_keys[:, low : low + TILE], preferred_element_type=jnp.float32
            )
        else:
            entry = (low - NV * BLK) // BLK
            keys = jnp.concatenate(
                [window[r, :HD] for r in rows[entry : entry + TILE // BLK]], axis=0
            )
            found = lax.dot_general(query, keys, contract, preferred_element_type=jnp.float32)
        found = found + bias[:, low : low + TILE]
        if low == NV * BLK:
            diagonal = jnp.concatenate([diagonal_ref[...]] * group_heads, axis=0)
            found = jnp.concatenate(
                [found[:, : 2 * BLK] + diagonal, found[:, 2 * BLK :]], axis=1
            )
        return found

    def weighted_values(block, at):
        ones = jnp.ones(((NV + NS) * BLK, HD), jnp.bfloat16)
        values = jnp.concatenate([vert[:, HD:]] + [window[r, HD:] for r in slash_rows(block)], axis=0)
        return jnp.dot(
            weights[at][...],
            jnp.concatenate([values, ones], axis=1),
            preferred_element_type=jnp.float32,
        )

    def store(total, block):
        result = (total[:, :HD] / total[:, HD:]).astype(jnp.bfloat16)
        rows = blocks_at(block)
        for h in range(group_heads):
            out[rows, h * HD : (h + 1) * HD] = result[h * BLK : (h + 1) * BLK]

    def stage(block, at, score, weigh, combine):
        other = 1 - at
        if score:
            fresh = jnp.minimum(block, last)
            query = query_of(fresh)
            rows = slash_rows(fresh)
            bias = bias_ref[pl.ds(head * blocks_dev + shard_block(fresh), 1), :]
        if combine:
            done = jnp.maximum(block - 2, 0)
            total = weighted_values(done, at)
        if weigh:
            row_max = maxima[other][...]
            row_max = jnp.concatenate([row_max] * (TILE // HD), axis=1)
        highest = None
        for tile in range((NV + NS) * BLK // TILE):
            low = tile * TILE
            if score:
                found = score_tile(query, bias, rows, tile)
                scores[at][:, low : low + TILE] = found
                for piece_low in range(0, TILE, HD):
                    piece = found[:, piece_low : piece_low + HD]
                    highest = piece if highest is None else jnp.maximum(highest, piece)
            if weigh:
                weights[other][:, low : low + TILE] = jnp.exp(
                    (scores[other][:, low : low + TILE] - row_max) * scale
                ).astype(jnp.bfloat16)
        if score:
            maxima[at][...] = jnp.broadcast_to(
                jnp.max(highest, axis=1, keepdims=True), highest.shape
            )
        if combine:
            store(total, done)

    @pl.when(step == 0)
    def _():
        for k in range(parts):
            pltpu.make_async_copy(
                query_ref.at[
                    pl.ds(pl.multiple_of(part_ref[k] * part_rows, part_rows), part_rows),
                    pl.ds(head * group_cols, group_cols),
                ],
                queries.at[pl.ds(k * part_rows, part_rows)],
                query_sem,
            ).start()
        pltpu.make_async_copy(vert_ref.at[head], vert, vert_sem).start()
        column = lax.broadcasted_iota(jnp.int32, (BLK, 2 * BLK), 1)
        row = lax.broadcasted_iota(jnp.int32, (BLK, 2 * BLK), 0)
        diagonal_ref[...] = jnp.where((column < BLK) & (column > row), NEG, 0.0).astype(jnp.float32)
        weights_b[...] = jnp.zeros_like(weights_b)
        pltpu.make_async_copy(vert, vert, vert_sem).wait()
        vert_keys[...] = vert[:, :HD].T
        pltpu.make_async_copy(queries, queries, query_sem).wait()
        stage(0, 0, True, False, False)

    first = step * STEP_BLOCKS
    stage(first + 1, 1, True, True, True)
    stage(first + 2, 0, True, True, True)

    @pl.when(first + STEP_BLOCKS > last)
    def _():
        store(weighted_values(last, 1), last)
        for k in range(parts):
            pltpu.make_async_copy(
                out.at[pl.ds(k * part_rows, part_rows)], out_refs[k], out_sem.at[k]
            ).start()
        for k in range(parts):
            pltpu.make_async_copy(
                out.at[pl.ds(k * part_rows, part_rows)], out_refs[k], out_sem.at[k]
            ).wait()


def attend(head, part, slash, bias, queries, vert, window, part_rows, after):
    parts = part.shape[0]
    group_cols = queries.shape[1] // slash.shape[0]
    group_heads = group_cols // HD
    part_blocks = part_rows // BLK
    rows = group_heads * BLK
    keys_seen = (NV + NS) * BLK
    return pl.pallas_call(
        functools.partial(attend_kernel, head, parts, len(after), part_blocks, group_heads),
        out_shape=[jax.ShapeDtypeStruct((part_rows, group_cols), jnp.bfloat16)] * parts,
        grid_spec=pltpu.PrefetchScalarGridSpec(
            num_scalar_prefetch=2,
            grid=(parts * part_blocks // STEP_BLOCKS,),
            in_specs=[pl.BlockSpec(bias.shape, lambda s, *_: (0, 0))] + [ANY, ANY, VMEM]
            + [ANY] * len(after),
            out_specs=[ANY] * parts,
            scratch_shapes=[
                pltpu.VMEM((parts * part_rows, group_cols), jnp.bfloat16),
                pltpu.VMEM((parts * part_rows, group_cols), jnp.bfloat16),
                pltpu.VMEM((NV * BLK, 2 * HD), jnp.bfloat16),
                pltpu.VMEM((HD, NV * BLK), jnp.bfloat16),
                pltpu.VMEM((rows, keys_seen), jnp.float32),
                pltpu.VMEM((rows, keys_seen), jnp.float32),
                pltpu.VMEM((rows, keys_seen), jnp.bfloat16),
                pltpu.VMEM((rows, keys_seen), jnp.bfloat16),
                pltpu.VMEM((rows, HD), jnp.float32),
                pltpu.VMEM((rows, HD), jnp.float32),
                pltpu.VMEM((BLK, 2 * BLK), jnp.float32),
                pltpu.SemaphoreType.DMA,
                pltpu.SemaphoreType.DMA,
                pltpu.SemaphoreType.DMA((parts,)),
            ],
        ),
        compiler_params=pltpu.CompilerParams(
            dimension_semantics=("arbitrary",), vmem_limit_bytes=32 << 20
        ),
        cost_estimate=pl.CostEstimate(
            flops=4 * parts * part_rows * group_heads * keys_seen * HD,
            bytes_accessed=4 * parts * part_rows * group_cols + 4 * window.shape[0] * HD,
            transcendentals=parts * part_rows * group_heads * keys_seen,
        ),
    )(part, slash, bias, queries, vert, window, *after)


def local(queries, keys, values, vertical, slash):
    shard_count = lax.axis_size("ctx")
    shard_index = lax.axis_index("ctx")
    head_count = lax.axis_size("head")
    head_index = lax.axis_index("head")
    tok_rows = queries.shape[0]
    kv_local = keys.shape[1] // HD
    group_cols = queries.shape[1] // kv_local
    blocks_dev = tok_rows // BLK
    part_rows = tok_rows // head_count
    partner = shard_index ^ 1
    two_pairs = [(i, (i + 2) % shard_count) for i in range(shard_count)]
    across_pairs = [(i, i ^ 1) for i in range(shard_count)]
    parity = (shard_index % 2).reshape(1).astype(jnp.int32)

    owners = vertical // blocks_dev
    order = jnp.arange(NV, dtype=jnp.int32)
    same_owner = owners[:, :, None] == owners[:, None, :]
    earlier = order[None, :] < order[:, None]
    slot_rank = jnp.sum((same_owner & earlier[None]).astype(jnp.int32), axis=2)
    slots = jnp.arange(MOWN, dtype=jnp.int32)
    in_slot = slot_rank[:, :, None] == slots
    local_block = jnp.sum(
        ((owners == shard_index)[:, :, None] & in_slot) * (vertical % blocks_dev)[:, :, None],
        axis=1,
    )
    distances = 2 * jnp.arange(shard_count // 2, dtype=jnp.int32)
    array_owner = jnp.concatenate([shard_index - distances, partner - distances])
    array_owner = jnp.where(array_owner <= shard_index, array_owner, -1)
    here = (array_owner[:, None, None] == owners)[:, :, :, None] & in_slot[None]
    place = jnp.sum(here * (order + 1)[None, None, :, None], axis=2) - 1
    source = jnp.where(owners <= shard_index, 0, -1).astype(jnp.int32)

    slash_rank = jnp.sum((slash[:, None, :] < slash[:, :, None]).astype(jnp.int32), axis=2)
    at_rank = slash_rank[:, :, None] == jnp.arange(NS, dtype=jnp.int32)
    slash = jnp.sum(at_rank * slash[:, :, None], axis=1)

    global_blocks = shard_index * blocks_dev + jnp.arange(blocks_dev, dtype=jnp.int32)
    vert_valid = vertical[:, None, :] < global_blocks[None, :, None]
    slash_blocks = global_blocks[None, :, None] - slash[:, None, :]
    in_vertical = jnp.any(slash_blocks[:, :, :, None] == vertical[:, None, None, :], axis=3)
    slash_valid = (slash[:, None, :] == 0) | ((slash_blocks >= 0) & jnp.logical_not(in_vertical))
    valid = jnp.concatenate([vert_valid, slash_valid], axis=2)
    listed = jnp.arange(NV + NS, dtype=jnp.int32)
    spread = (jnp.arange((NV + NS) * BLK, dtype=jnp.int32) // BLK == listed[:, None])
    barred = jnp.where(valid, 0.0, NEG).reshape(kv_local * blocks_dev, NV + NS)
    bias = jnp.dot(
        barred.astype(jnp.bfloat16), spread.astype(jnp.bfloat16), preferred_element_type=jnp.float32
    )

    steps = shard_count // 2 - 1
    bounds = [k * blocks_dev // steps * BLK for k in range(steps + 1)]
    slot_rows = kv_local * MOWN * BLK
    own, send, slots_own = first_of(bounds[1], local_block, keys, values)
    behind = [(slots_own, 0)]
    across = []
    two_back = []
    one_back = []
    for step in range(steps):
        rows = bounds[step + 1] - bounds[step]
        here = (own, bounds[step])
        if step:
            send = joined(
                parity, [(rows, here, here), (slot_rows, behind[-1], behind[-1])],
                [cross] + one_back[-2:-1],
            )
        come = lax.ppermute(send, "ctx", two_pairs)
        if step == 0:
            across.append((lax.ppermute(slots_own, "ctx", across_pairs), 0))
        two_back.append(come)
        behind.append((come, rows))
        cross = joined(parity, [(rows, here, (come, 0)), (slot_rows, behind[-1], behind[-1])])
        one_back.append(lax.ppermute(cross, "ctx", across_pairs))
        across.append((one_back[-1], rows))
    slots = behind + across
    windows = [(bounds, own, two_back, one_back)]
    after = two_back[-2:-1] + [send]
    for head in range(1, kv_local):
        own = pair_of(head, keys, values, after)
        come = lax.ppermute(own, "ctx", two_pairs)
        windows.append(([0, tok_rows], own, [come], None))
        after = [come]

    out = jnp.zeros((part_rows, head_count * kv_local * group_cols), jnp.bfloat16)
    after = []
    half = head_count // 2
    calls = [[[head_count - 1], list(range(head_count - 2, -1, -1))]] * (kv_local - 1)
    calls.append([[flip] for flip in range(head_count - 1, half - 1, -1)])
    calls[-1].append(list(range(half - 1, -1, -1)))
    vert = listed_blocks(place, source, slots)
    for head in range(kv_local):
        bounds, own, two_back, one_back = windows[head]
        pieces = []
        for arrays in (two_back, one_back):
            for low, high, array in zip(bounds[:-1], bounds[1:], arrays):
                pieces.append((high - low, (array, 0), (array, 0)))
        pieces.append((tok_rows, (own, 0), (own, 0)))
        window = joined(parity, pieces)
        for flips in calls[head]:
            others = [head_index ^ flip for flip in flips]
            pieces = attend(
                head, jnp.stack(others).astype(jnp.int32), slash, bias, queries, vert, window,
                part_rows, after,
            )
            after = [pieces[-1]]
            if flips == calls[head][0] and head + 1 < kv_local:
                near, own_next, (come,), _ = windows[head + 1]
                cross = joined(parity, [(tok_rows, (own_next, 0), (come, 0))], after)
                crossed = lax.ppermute(cross, "ctx", across_pairs)
                windows[head + 1] = (near, own_next, [come], [crossed])
            for flip, other, piece in zip(flips, others, pieces):
                if flip:
                    piece = lax.ppermute(piece, "head", [(i, i ^ flip) for i in range(head_count)])
                out = lax.dynamic_update_slice(
                    out, piece, (0, other * kv_local * group_cols + head * group_cols)
                )
    return out


def solution(mesh):
    in_specs = (
        P("ctx", "head"),
        P("ctx", "head"),
        P("ctx", "head"),
        P("head", None),
        P("head", None),
    )
    out_specs = P(("ctx", "head"), None)
    return jax.shard_map(local, mesh=mesh, in_specs=in_specs, out_specs=out_specs, check_vma=False)
```

```python
import functools
import math

import jax
import jax.numpy as jnp
from jax import lax
from jax.experimental import pallas as pl
from jax.experimental.pallas import tpu as pltpu
from jax.sharding import PartitionSpec as P

HD = 128
BLK = 64
NV = 16
NS = 8
MOWN = 4
LOOK = 2
NEG = -1e30
STEP_BLOCKS = 2
TILE = 256
HBM = pl.BlockSpec(memory_space=pltpu.HBM)
ANY = pl.BlockSpec(memory_space=pl.ANY)
VMEM = pl.BlockSpec(memory_space=pltpu.VMEM)
SMEM = pl.BlockSpec(memory_space=pltpu.SMEM)


def blocks_at(index, count=1):
    return pl.ds(pl.multiple_of(index * BLK, BLK), count * BLK)


def run_all(copies, sem):
    copies = [pltpu.make_async_copy(*ends, sem.at[k]) for k, ends in enumerate(copies)]
    for copy in copies:
        copy.start()
    for copy in copies:
        copy.wait()


def first_kernel(local_ref, keys_ref, values_ref, own_ref, send_ref, slots_ref, sem):
    chunk_rows = send_ref.shape[0] - slots_ref.shape[0]
    copies = []
    for side, source in enumerate((keys_ref, values_ref)):
        to = pl.ds(side * HD, HD)
        for head in range(local_ref.shape[0]):
            for slot in range(MOWN):
                found = source.at[blocks_at(local_ref[head, slot]), pl.ds(head * HD, HD)]
                low = (head * MOWN + slot) * BLK
                copies.append((found, send_ref.at[pl.ds(chunk_rows + low, BLK), to]))
                copies.append((found, slots_ref.at[pl.ds(low, BLK), to]))
        rows = pl.ds(0, chunk_rows)
        copies.append((source.at[rows, pl.ds(0, HD)], send_ref.at[rows, to]))
        copies.append((source.at[:, pl.ds(0, HD)], own_ref.at[:, to]))
    run_all(copies, sem)


def first_of(chunk_rows, local_block, keys, values):
    heads = local_block.shape[0]
    rows = keys.shape[0]
    slot_rows = heads * MOWN * BLK
    return pl.pallas_call(
        first_kernel,
        out_shape=[
            jax.ShapeDtypeStruct((rows, 2 * HD), keys.dtype),
            jax.ShapeDtypeStruct((chunk_rows + slot_rows, 2 * HD), keys.dtype),
            jax.ShapeDtypeStruct((slot_rows, 2 * HD), keys.dtype),
        ],
        in_specs=[SMEM, HBM, HBM],
        out_specs=[VMEM] * 3,
        scratch_shapes=[pltpu.SemaphoreType.DMA((4 * heads * MOWN + 4,))],
        compiler_params=pltpu.CompilerParams(vmem_limit_bytes=8 << 20),
        cost_estimate=pl.CostEstimate(flops=0, bytes_accessed=16 * rows * HD, transcendentals=0),
    )(local_block, keys, values)


def pair_kernel(head, keys_ref, values_ref, *rest):
    out_ref, sem = rest[-2:]
    run_all(
        [
            (source.at[:, pl.ds(head * HD, HD)], out_ref.at[:, pl.ds(side * HD, HD)])
            for side, source in enumerate((keys_ref, values_ref))
        ],
        sem,
    )


def pair_of(head, keys, values, after):
    rows = keys.shape[0]
    return pl.pallas_call(
        functools.partial(pair_kernel, head),
        out_shape=jax.ShapeDtypeStruct((rows, 2 * HD), keys.dtype),
        in_specs=[HBM] * (2 + len(after)),
        out_specs=VMEM,
        scratch_shapes=[pltpu.SemaphoreType.DMA((2,))],
        compiler_params=pltpu.CompilerParams(vmem_limit_bytes=8 << 20),
        cost_estimate=pl.CostEstimate(flops=0, bytes_accessed=8 * rows * HD, transcendentals=0),
    )(keys, values, *after)


def joined_kernel(pieces, parity_ref, *rest):
    refs, out_ref, sem = rest[:-2], rest[-2], rest[-1]
    to = 0
    for rows, even, odd in pieces:
        for value, (index, low) in enumerate((even, odd)):
            copy = pltpu.make_async_copy(
                refs[index].at[pl.ds(low, rows)], out_ref.at[pl.ds(to, rows)], sem
            )
            if even != odd:
                pl.when(parity_ref[0] == value)(copy.start)
            elif value:
                copy.start()

        to += rows
    pltpu.make_async_copy(out_ref, out_ref, sem).wait()


def joined(parity, pieces, after=()):
    arrays = []
    plan = []
    for rows, *sources in pieces:
        found = []
        for array, low in sources:
            at = [k for k, known in enumerate(arrays) if known is array]
            if not at:
                at = [len(arrays)]
                arrays.append(array)
            found.append((at[0], low))
        plan.append((rows, *found))
    total = sum(rows for rows, *_ in plan)
    return pl.pallas_call(
        functools.partial(joined_kernel, plan),
        out_shape=jax.ShapeDtypeStruct((total, 2 * HD), jnp.bfloat16),
        in_specs=[SMEM] + [HBM] * (len(arrays) + len(after)),
        out_specs=VMEM,
        scratch_shapes=[pltpu.SemaphoreType.DMA],
        compiler_params=pltpu.CompilerParams(vmem_limit_bytes=8 << 20),
        cost_estimate=pl.CostEstimate(flops=0, bytes_accessed=8 * total * HD, transcendentals=0),
    )(parity, *arrays, *after)


def listed_kernel(lows, place_ref, source_ref, *rest):
    refs, out_ref, sem = rest[:-2], rest[-2], rest[-1]
    for head in range(out_ref.shape[0]):

        def block(index, slot):
            return refs[index].at[pl.ds(lows[index] + (head * MOWN + slot) * BLK, BLK)]

        def put(found, target):
            pltpu.make_async_copy(found, out_ref.at[head, target], sem).start()

        for index in range(len(refs)):
            for slot in range(MOWN):
                place = place_ref[index, head, slot]
                pl.when(place >= 0)(
                    functools.partial(put, block(index, slot), blocks_at(place))
                )
        for entry in range(NV):
            pl.when(source_ref[head, entry] < 0)(
                functools.partial(put, block(0, 0), pl.ds(entry * BLK, BLK))
            )
    pltpu.make_async_copy(out_ref, out_ref, sem).wait()


def listed_blocks(place, source, slots):
    heads = source.shape[0]
    return pl.pallas_call(
        functools.partial(listed_kernel, [low for _, low in slots]),
        out_shape=jax.ShapeDtypeStruct((heads, NV * BLK, 2 * HD), jnp.bfloat16),
        in_specs=[SMEM, SMEM] + [HBM] * len(slots),
        out_specs=VMEM,
        scratch_shapes=[pltpu.SemaphoreType.DMA],
        compiler_params=pltpu.CompilerParams(vmem_limit_bytes=8 << 20),
        cost_estimate=pl.CostEstimate(
            flops=0, bytes_accessed=8 * heads * NV * BLK * HD, transcendentals=0
        ),
    )(place, source, *[array for array, _ in slots])


def attend_kernel(
    head, parts, waits, part_blocks, group_heads, part_ref, slash_ref, bias_ref, query_ref,
    vert_ref, window, *rest,
):
    rest = rest[waits:]
    out_refs = rest[:parts]
    (
        queries, out, vert, vert_keys, scores_a, scores_b, weights_a, weights_b, max_a,
        max_b, diagonal_ref, query_sem, vert_sem, out_sem,
    ) = rest[parts:]
    scores, weights, maxima = (scores_a, scores_b), (weights_a, weights_b), (max_a, max_b)
    blocks_dev = window.shape[0] // ((LOOK + 1) * BLK)
    part_rows = part_blocks * BLK
    group_cols = group_heads * HD
    last = parts * part_blocks - 1
    step = pl.program_id(0)
    scale = 1.0 / math.sqrt(HD)
    contract = (((1,), (1,)), ((), ()))

    def shard_block(block):
        return part_ref[block // part_blocks] * part_blocks + lax.rem(block, part_blocks)

    def slash_rows(block):
        first = LOOK * blocks_dev + shard_block(block)
        return [blocks_at(first - slash_ref[head, entry]) for entry in range(NS)]

    def query_of(block):
        rows = blocks_at(block)
        return jnp.concatenate(
            [queries[rows, h * HD : (h + 1) * HD] for h in range(group_heads)], axis=0
        )

    def score_tile(query, bias, rows, tile):
        low = tile * TILE
        if low < NV * BLK:
            found = jnp.dot(
                query, vert_keys[:, low : low + TILE], preferred_element_type=jnp.float32
            )
        else:
            entry = (low - NV * BLK) // BLK
            keys = jnp.concatenate(
                [window[r, :HD] for r in rows[entry : entry + TILE // BLK]], axis=0
            )
            found = lax.dot_general(query, keys, contract, preferred_element_type=jnp.float32)
        found = found + bias[:, low : low + TILE]
        if low == NV * BLK:
            diagonal = jnp.concatenate([diagonal_ref[...]] * group_heads, axis=0)
            found = jnp.concatenate(
                [found[:, : 2 * BLK] + diagonal, found[:, 2 * BLK :]], axis=1
            )
        return found

    def weighted_values(block, at):
        ones = jnp.ones(((NV + NS) * BLK, HD), jnp.bfloat16)
        values = jnp.concatenate([vert[:, HD:]] + [window[r, HD:] for r in slash_rows(block)], axis=0)
        return jnp.dot(
            weights[at][...],
            jnp.concatenate([values, ones], axis=1),
            preferred_element_type=jnp.float32,
        )

    def store(total, block):
        result = (total[:, :HD] / total[:, HD:]).astype(jnp.bfloat16)
        rows = blocks_at(block)
        for h in range(group_heads):
            out[rows, h * HD : (h + 1) * HD] = result[h * BLK : (h + 1) * BLK]

    def stage(block, at, score, weigh, combine):
        other = 1 - at
        if score:
            fresh = jnp.minimum(block, last)
            query = query_of(fresh)
            rows = slash_rows(fresh)
            bias = bias_ref[pl.ds(head * blocks_dev + shard_block(fresh), 1), :]
        if combine:
            done = jnp.maximum(block - 2, 0)
            total = weighted_values(done, at)
        if weigh:
            row_max = maxima[other][...]
            row_max = jnp.concatenate([row_max] * (TILE // HD), axis=1)
        highest = None
        for tile in range((NV + NS) * BLK // TILE):
            low = tile * TILE
            if score:
                found = score_tile(query, bias, rows, tile)
                scores[at][:, low : low + TILE] = found
                for piece_low in range(0, TILE, HD):
                    piece = found[:, piece_low : piece_low + HD]
                    highest = piece if highest is None else jnp.maximum(highest, piece)
            if weigh:
                weights[other][:, low : low + TILE] = jnp.exp(
                    (scores[other][:, low : low + TILE] - row_max) * scale
                ).astype(jnp.bfloat16)
        if score:
            maxima[at][...] = jnp.broadcast_to(
                jnp.max(highest, axis=1, keepdims=True), highest.shape
            )
        if combine:
            store(total, done)

    @pl.when(step == 0)
    def _():
        for k in range(parts):
            pltpu.make_async_copy(
                query_ref.at[
                    pl.ds(pl.multiple_of(part_ref[k] * part_rows, part_rows), part_rows),
                    pl.ds(head * group_cols, group_cols),
                ],
                queries.at[pl.ds(k * part_rows, part_rows)],
                query_sem,
            ).start()
        pltpu.make_async_copy(vert_ref.at[head], vert, vert_sem).start()
        column = lax.broadcasted_iota(jnp.int32, (BLK, 2 * BLK), 1)
        row = lax.broadcasted_iota(jnp.int32, (BLK, 2 * BLK), 0)
        diagonal_ref[...] = jnp.where((column < BLK) & (column > row), NEG, 0.0).astype(jnp.float32)
        weights_b[...] = jnp.zeros_like(weights_b)
        pltpu.make_async_copy(vert, vert, vert_sem).wait()
        vert_keys[...] = vert[:, :HD].T
        pltpu.make_async_copy(queries, queries, query_sem).wait()
        stage(0, 0, True, False, False)

    first = step * STEP_BLOCKS
    stage(first + 1, 1, True, True, True)
    stage(first + 2, 0, True, True, True)

    @pl.when(first + STEP_BLOCKS > last)
    def _():
        store(weighted_values(last, 1), last)
        for k in range(parts):
            pltpu.make_async_copy(
                out.at[pl.ds(k * part_rows, part_rows)], out_refs[k], out_sem.at[k]
            ).start()
        for k in range(parts):
            pltpu.make_async_copy(
                out.at[pl.ds(k * part_rows, part_rows)], out_refs[k], out_sem.at[k]
            ).wait()


def attend(head, part, slash, bias, queries, vert, window, part_rows, after):
    parts = part.shape[0]
    group_cols = queries.shape[1] // slash.shape[0]
    group_heads = group_cols // HD
    part_blocks = part_rows // BLK
    rows = group_heads * BLK
    keys_seen = (NV + NS) * BLK
    return pl.pallas_call(
        functools.partial(attend_kernel, head, parts, len(after), part_blocks, group_heads),
        out_shape=[jax.ShapeDtypeStruct((part_rows, group_cols), jnp.bfloat16)] * parts,
        grid_spec=pltpu.PrefetchScalarGridSpec(
            num_scalar_prefetch=2,
            grid=(parts * part_blocks // STEP_BLOCKS,),
            in_specs=[pl.BlockSpec(bias.shape, lambda s, *_: (0, 0))] + [ANY, ANY, VMEM]
            + [ANY] * len(after),
            out_specs=[ANY] * parts,
            scratch_shapes=[
                pltpu.VMEM((parts * part_rows, group_cols), jnp.bfloat16),
                pltpu.VMEM((parts * part_rows, group_cols), jnp.bfloat16),
                pltpu.VMEM((NV * BLK, 2 * HD), jnp.bfloat16),
                pltpu.VMEM((HD, NV * BLK), jnp.bfloat16),
                pltpu.VMEM((rows, keys_seen), jnp.float32),
                pltpu.VMEM((rows, keys_seen), jnp.float32),
                pltpu.VMEM((rows, keys_seen), jnp.bfloat16),
                pltpu.VMEM((rows, keys_seen), jnp.bfloat16),
                pltpu.VMEM((rows, HD), jnp.float32),
                pltpu.VMEM((rows, HD), jnp.float32),
                pltpu.VMEM((BLK, 2 * BLK), jnp.float32),
                pltpu.SemaphoreType.DMA,
                pltpu.SemaphoreType.DMA,
                pltpu.SemaphoreType.DMA((parts,)),
            ],
        ),
        compiler_params=pltpu.CompilerParams(
            dimension_semantics=("arbitrary",), vmem_limit_bytes=18 << 20
        ),
        cost_estimate=pl.CostEstimate(
            flops=4 * parts * part_rows * group_heads * keys_seen * HD,
            bytes_accessed=4 * parts * part_rows * group_cols + 4 * window.shape[0] * HD,
            transcendentals=parts * part_rows * group_heads * keys_seen,
        ),
    )(part, slash, bias, queries, vert, window, *after)


def local(queries, keys, values, vertical, slash):
    shard_count = lax.axis_size("ctx")
    shard_index = lax.axis_index("ctx")
    head_count = lax.axis_size("head")
    head_index = lax.axis_index("head")
    tok_rows = queries.shape[0]
    kv_local = keys.shape[1] // HD
    group_cols = queries.shape[1] // kv_local
    blocks_dev = tok_rows // BLK
    part_rows = tok_rows // head_count
    partner = shard_index ^ 1
    two_pairs = [(i, (i + 2) % shard_count) for i in range(shard_count)]
    across_pairs = [(i, i ^ 1) for i in range(shard_count)]
    parity = (shard_index % 2).reshape(1).astype(jnp.int32)

    owners = vertical // blocks_dev
    order = jnp.arange(NV, dtype=jnp.int32)
    same_owner = owners[:, :, None] == owners[:, None, :]
    earlier = order[None, :] < order[:, None]
    slot_rank = jnp.sum((same_owner & earlier[None]).astype(jnp.int32), axis=2)
    slots = jnp.arange(MOWN, dtype=jnp.int32)
    in_slot = slot_rank[:, :, None] == slots
    local_block = jnp.sum(
        ((owners == shard_index)[:, :, None] & in_slot) * (vertical % blocks_dev)[:, :, None],
        axis=1,
    )
    distances = 2 * jnp.arange(shard_count // 2, dtype=jnp.int32)
    array_owner = jnp.concatenate([shard_index - distances, partner - distances])
    array_owner = jnp.where(array_owner <= shard_index, array_owner, -1)
    here = (array_owner[:, None, None] == owners)[:, :, :, None] & in_slot[None]
    place = jnp.sum(here * (order + 1)[None, None, :, None], axis=2) - 1
    source = jnp.where(owners <= shard_index, 0, -1).astype(jnp.int32)

    slash_rank = jnp.sum((slash[:, None, :] < slash[:, :, None]).astype(jnp.int32), axis=2)
    at_rank = slash_rank[:, :, None] == jnp.arange(NS, dtype=jnp.int32)
    slash = jnp.sum(at_rank * slash[:, :, None], axis=1)

    global_blocks = shard_index * blocks_dev + jnp.arange(blocks_dev, dtype=jnp.int32)
    vert_valid = vertical[:, None, :] < global_blocks[None, :, None]
    slash_blocks = global_blocks[None, :, None] - slash[:, None, :]
    in_vertical = jnp.any(slash_blocks[:, :, :, None] == vertical[:, None, None, :], axis=3)
    slash_valid = (slash[:, None, :] == 0) | ((slash_blocks >= 0) & jnp.logical_not(in_vertical))
    valid = jnp.concatenate([vert_valid, slash_valid], axis=2)
    listed = jnp.arange(NV + NS, dtype=jnp.int32)
    spread = (jnp.arange((NV + NS) * BLK, dtype=jnp.int32) // BLK == listed[:, None])
    barred = jnp.where(valid, 0.0, NEG).reshape(kv_local * blocks_dev, NV + NS)
    bias = jnp.dot(
        barred.astype(jnp.bfloat16), spread.astype(jnp.bfloat16), preferred_element_type=jnp.float32
    )

    steps = shard_count // 2 - 1
    bounds = [k * blocks_dev // steps * BLK for k in range(steps + 1)]
    slot_rows = kv_local * MOWN * BLK
    own, send, slots_own = first_of(bounds[1], local_block, keys, values)
    behind = [(slots_own, 0)]
    across = []
    two_back = []
    one_back = []
    for step in range(steps):
        rows = bounds[step + 1] - bounds[step]
        here = (own, bounds[step])
        if step:
            send = joined(
                parity, [(rows, here, here), (slot_rows, behind[-1], behind[-1])],
                [cross] + one_back[-2:-1],
            )
        come = lax.ppermute(send, "ctx", two_pairs)
        if step == 0:
            across.append((lax.ppermute(slots_own, "ctx", across_pairs), 0))
        two_back.append(come)
        behind.append((come, rows))
        cross = joined(parity, [(rows, here, (come, 0)), (slot_rows, behind[-1], behind[-1])])
        one_back.append(lax.ppermute(cross, "ctx", across_pairs))
        across.append((one_back[-1], rows))
    slots = behind + across
    windows = [(bounds, own, two_back, one_back)]
    after = two_back[-2:-1] + [send]
    for head in range(1, kv_local):
        own = pair_of(head, keys, values, after)
        come = lax.ppermute(own, "ctx", two_pairs)
        windows.append(([0, tok_rows], own, [come], None))
        after = [come]

    out = jnp.zeros((part_rows, head_count * kv_local * group_cols), jnp.bfloat16)
    after = []
    half = head_count // 2
    calls = [[[head_count - 1], list(range(head_count - 2, -1, -1))]] * (kv_local - 1)
    calls.append([[flip] for flip in range(head_count - 1, half - 1, -1)])
    calls[-1].append(list(range(half - 1, -1, -1)))
    vert = listed_blocks(place, source, slots)
    for head in range(kv_local):
        bounds, own, two_back, one_back = windows[head]
        pieces = []
        for arrays in (two_back, one_back):
            for low, high, array in zip(bounds[:-1], bounds[1:], arrays):
                pieces.append((high - low, (array, 0), (array, 0)))
        pieces.append((tok_rows, (own, 0), (own, 0)))
        window = joined(parity, pieces)
        for flips in calls[head]:
            others = [head_index ^ flip for flip in flips]
            pieces = attend(
                head, jnp.stack(others).astype(jnp.int32), slash, bias, queries, vert, window,
                part_rows, after,
            )
            after = [pieces[-1]]
            if flips == calls[head][0] and head + 1 < kv_local:
                near, own_next, (come,), _ = windows[head + 1]
                cross = joined(parity, [(tok_rows, (own_next, 0), (come, 0))], after)
                crossed = lax.ppermute(cross, "ctx", across_pairs)
                windows[head + 1] = (near, own_next, [come], [crossed])
            for flip, other, piece in zip(flips, others, pieces):
                if flip:
                    piece = lax.ppermute(piece, "head", [(i, i ^ flip) for i in range(head_count)])
                out = lax.dynamic_update_slice(
                    out, piece, (0, other * kv_local * group_cols + head * group_cols)
                )
    return out


def solution(mesh):
    in_specs = (
        P("ctx", "head"),
        P("ctx", "head"),
        P("ctx", "head"),
        P("head", None),
        P("head", None),
    )
    out_specs = P(("ctx", "head"), None)
    return jax.shard_map(local, mesh=mesh, in_specs=in_specs, out_specs=out_specs, check_vma=False)
```

```python
import functools
import math

import jax
import jax.numpy as jnp
from jax import lax
from jax.experimental import pallas as pl
from jax.experimental.pallas import tpu as pltpu
from jax.sharding import PartitionSpec as P

HD = 128
BLK = 64
NV = 16
NS = 8
MOWN = 4
LOOK = 2
NEG = -1e30
STEP_BLOCKS = 2
TILE = 512
HBM = pl.BlockSpec(memory_space=pltpu.HBM)
ANY = pl.BlockSpec(memory_space=pl.ANY)
VMEM = pl.BlockSpec(memory_space=pltpu.VMEM)
SMEM = pl.BlockSpec(memory_space=pltpu.SMEM)


def blocks_at(index, count=1):
    return pl.ds(pl.multiple_of(index * BLK, BLK), count * BLK)


def run_all(copies, sem):
    copies = [pltpu.make_async_copy(*ends, sem.at[k]) for k, ends in enumerate(copies)]
    for copy in copies:
        copy.start()
    for copy in copies:
        copy.wait()


def first_kernel(local_ref, keys_ref, values_ref, own_ref, send_ref, slots_ref, sem):
    chunk_rows = send_ref.shape[0] - slots_ref.shape[0]
    copies = []
    for side, source in enumerate((keys_ref, values_ref)):
        to = pl.ds(side * HD, HD)
        for head in range(local_ref.shape[0]):
            for slot in range(MOWN):
                found = source.at[blocks_at(local_ref[head, slot]), pl.ds(head * HD, HD)]
                low = (head * MOWN + slot) * BLK
                copies.append((found, send_ref.at[pl.ds(chunk_rows + low, BLK), to]))
                copies.append((found, slots_ref.at[pl.ds(low, BLK), to]))
        rows = pl.ds(0, chunk_rows)
        copies.append((source.at[rows, pl.ds(0, HD)], send_ref.at[rows, to]))
        copies.append((source.at[:, pl.ds(0, HD)], own_ref.at[:, to]))
    run_all(copies, sem)


def first_of(chunk_rows, local_block, keys, values):
    heads = local_block.shape[0]
    rows = keys.shape[0]
    slot_rows = heads * MOWN * BLK
    return pl.pallas_call(
        first_kernel,
        out_shape=[
            jax.ShapeDtypeStruct((rows, 2 * HD), keys.dtype),
            jax.ShapeDtypeStruct((chunk_rows + slot_rows, 2 * HD), keys.dtype),
            jax.ShapeDtypeStruct((slot_rows, 2 * HD), keys.dtype),
        ],
        in_specs=[SMEM, HBM, HBM],
        out_specs=[VMEM] * 3,
        scratch_shapes=[pltpu.SemaphoreType.DMA((4 * heads * MOWN + 4,))],
        compiler_params=pltpu.CompilerParams(vmem_limit_bytes=8 << 20),
        cost_estimate=pl.CostEstimate(flops=0, bytes_accessed=16 * rows * HD, transcendentals=0),
    )(local_block, keys, values)


def pair_kernel(head, keys_ref, values_ref, *rest):
    out_ref, sem = rest[-2:]
    run_all(
        [
            (source.at[:, pl.ds(head * HD, HD)], out_ref.at[:, pl.ds(side * HD, HD)])
            for side, source in enumerate((keys_ref, values_ref))
        ],
        sem,
    )


def pair_of(head, keys, values, after):
    rows = keys.shape[0]
    return pl.pallas_call(
        functools.partial(pair_kernel, head),
        out_shape=jax.ShapeDtypeStruct((rows, 2 * HD), keys.dtype),
        in_specs=[HBM] * (2 + len(after)),
        out_specs=VMEM,
        scratch_shapes=[pltpu.SemaphoreType.DMA((2,))],
        compiler_params=pltpu.CompilerParams(vmem_limit_bytes=8 << 20),
        cost_estimate=pl.CostEstimate(flops=0, bytes_accessed=8 * rows * HD, transcendentals=0),
    )(keys, values, *after)


def joined_kernel(pieces, parity_ref, *rest):
    refs, out_ref, sem = rest[:-2], rest[-2], rest[-1]
    to = 0
    for rows, even, odd in pieces:
        for value, (index, low) in enumerate((even, odd)):
            copy = pltpu.make_async_copy(
                refs[index].at[pl.ds(low, rows)], out_ref.at[pl.ds(to, rows)], sem
            )
            if even != odd:
                pl.when(parity_ref[0] == value)(copy.start)
            elif value:
                copy.start()

        to += rows
    pltpu.make_async_copy(out_ref, out_ref, sem).wait()


def joined(parity, pieces, after=()):
    arrays = []
    plan = []
    for rows, *sources in pieces:
        found = []
        for array, low in sources:
            at = [k for k, known in enumerate(arrays) if known is array]
            if not at:
                at = [len(arrays)]
                arrays.append(array)
            found.append((at[0], low))
        plan.append((rows, *found))
    total = sum(rows for rows, *_ in plan)
    return pl.pallas_call(
        functools.partial(joined_kernel, plan),
        out_shape=jax.ShapeDtypeStruct((total, 2 * HD), jnp.bfloat16),
        in_specs=[SMEM] + [HBM] * (len(arrays) + len(after)),
        out_specs=VMEM,
        scratch_shapes=[pltpu.SemaphoreType.DMA],
        compiler_params=pltpu.CompilerParams(vmem_limit_bytes=8 << 20),
        cost_estimate=pl.CostEstimate(flops=0, bytes_accessed=8 * total * HD, transcendentals=0),
    )(parity, *arrays, *after)


def listed_kernel(lows, place_ref, source_ref, *rest):
    refs, out_ref, sem = rest[:-2], rest[-2], rest[-1]
    for head in range(out_ref.shape[0]):

        def block(index, slot):
            return refs[index].at[pl.ds(lows[index] + (head * MOWN + slot) * BLK, BLK)]

        def put(found, target):
            pltpu.make_async_copy(found, out_ref.at[head, target], sem).start()

        for index in range(len(refs)):
            for slot in range(MOWN):
                place = place_ref[index, head, slot]
                pl.when(place >= 0)(
                    functools.partial(put, block(index, slot), blocks_at(place))
                )
        for entry in range(NV):
            pl.when(source_ref[head, entry] < 0)(
                functools.partial(put, block(0, 0), pl.ds(entry * BLK, BLK))
            )
    pltpu.make_async_copy(out_ref, out_ref, sem).wait()


def listed_blocks(place, source, slots):
    heads = source.shape[0]
    return pl.pallas_call(
        functools.partial(listed_kernel, [low for _, low in slots]),
        out_shape=jax.ShapeDtypeStruct((heads, NV * BLK, 2 * HD), jnp.bfloat16),
        in_specs=[SMEM, SMEM] + [HBM] * len(slots),
        out_specs=VMEM,
        scratch_shapes=[pltpu.SemaphoreType.DMA],
        compiler_params=pltpu.CompilerParams(vmem_limit_bytes=8 << 20),
        cost_estimate=pl.CostEstimate(
            flops=0, bytes_accessed=8 * heads * NV * BLK * HD, transcendentals=0
        ),
    )(place, source, *[array for array, _ in slots])


def attend_kernel(
    head, parts, waits, part_blocks, group_heads, part_ref, slash_ref, bias_ref, query_ref,
    vert_ref, window, *rest,
):
    rest = rest[waits:]
    out_refs = rest[:parts]
    (
        queries, out, vert, vert_keys, scores_a, scores_b, weights_a, weights_b, max_a,
        max_b, diagonal_ref, query_sem, vert_sem, out_sem,
    ) = rest[parts:]
    scores, weights, maxima = (scores_a, scores_b), (weights_a, weights_b), (max_a, max_b)
    blocks_dev = window.shape[0] // ((LOOK + 1) * BLK)
    part_rows = part_blocks * BLK
    group_cols = group_heads * HD
    last = parts * part_blocks - 1
    step = pl.program_id(0)
    scale = 1.0 / math.sqrt(HD)
    contract = (((1,), (1,)), ((), ()))

    def shard_block(block):
        return part_ref[block // part_blocks] * part_blocks + lax.rem(block, part_blocks)

    def slash_rows(block):
        first = LOOK * blocks_dev + shard_block(block)
        return [blocks_at(first - slash_ref[head, entry]) for entry in range(NS)]

    def query_of(block):
        rows = blocks_at(block)
        return jnp.concatenate(
            [queries[rows, h * HD : (h + 1) * HD] for h in range(group_heads)], axis=0
        )

    def score_tile(query, bias, rows, tile):
        low = tile * TILE
        if low < NV * BLK:
            found = jnp.dot(
                query, vert_keys[:, low : low + TILE], preferred_element_type=jnp.float32
            )
        else:
            entry = (low - NV * BLK) // BLK
            keys = jnp.concatenate(
                [window[r, :HD] for r in rows[entry : entry + TILE // BLK]], axis=0
            )
            found = lax.dot_general(query, keys, contract, preferred_element_type=jnp.float32)
        found = found + bias[:, low : low + TILE]
        if low == NV * BLK:
            diagonal = jnp.concatenate([diagonal_ref[...]] * group_heads, axis=0)
            found = jnp.concatenate(
                [found[:, : 2 * BLK] + diagonal, found[:, 2 * BLK :]], axis=1
            )
        return found

    def weighted_values(block, at):
        ones = jnp.ones(((NV + NS) * BLK, HD), jnp.bfloat16)
        values = jnp.concatenate([vert[:, HD:]] + [window[r, HD:] for r in slash_rows(block)], axis=0)
        return jnp.dot(
            weights[at][...],
            jnp.concatenate([values, ones], axis=1),
            preferred_element_type=jnp.float32,
        )

    def store(total, block):
        result = (total[:, :HD] / total[:, HD:]).astype(jnp.bfloat16)
        rows = blocks_at(block)
        for h in range(group_heads):
            out[rows, h * HD : (h + 1) * HD] = result[h * BLK : (h + 1) * BLK]

    def stage(block, at, score, weigh, combine):
        other = 1 - at
        if score:
            fresh = jnp.minimum(block, last)
            query = query_of(fresh)
            rows = slash_rows(fresh)
            bias = bias_ref[pl.ds(head * blocks_dev + shard_block(fresh), 1), :]
        if combine:
            done = jnp.maximum(block - 2, 0)
            total = weighted_values(done, at)
        if weigh:
            row_max = maxima[other][...]
            row_max = jnp.concatenate([row_max] * (TILE // HD), axis=1)
        highest = None
        for tile in range((NV + NS) * BLK // TILE):
            low = tile * TILE
            if score:
                found = score_tile(query, bias, rows, tile)
                scores[at][:, low : low + TILE] = found
                for piece_low in range(0, TILE, HD):
                    piece = found[:, piece_low : piece_low + HD]
                    highest = piece if highest is None else jnp.maximum(highest, piece)
            if weigh:
                weights[other][:, low : low + TILE] = jnp.exp(
                    (scores[other][:, low : low + TILE] - row_max) * scale
                ).astype(jnp.bfloat16)
        if score:
            maxima[at][...] = jnp.broadcast_to(
                jnp.max(highest, axis=1, keepdims=True), highest.shape
            )
        if combine:
            store(total, done)

    @pl.when(step == 0)
    def _():
        for k in range(parts):
            pltpu.make_async_copy(
                query_ref.at[
                    pl.ds(pl.multiple_of(part_ref[k] * part_rows, part_rows), part_rows),
                    pl.ds(head * group_cols, group_cols),
                ],
                queries.at[pl.ds(k * part_rows, part_rows)],
                query_sem,
            ).start()
        pltpu.make_async_copy(vert_ref.at[head], vert, vert_sem).start()
        column = lax.broadcasted_iota(jnp.int32, (BLK, 2 * BLK), 1)
        row = lax.broadcasted_iota(jnp.int32, (BLK, 2 * BLK), 0)
        diagonal_ref[...] = jnp.where((column < BLK) & (column > row), NEG, 0.0).astype(jnp.float32)
        weights_b[...] = jnp.zeros_like(weights_b)
        pltpu.make_async_copy(vert, vert, vert_sem).wait()
        vert_keys[...] = vert[:, :HD].T
        pltpu.make_async_copy(queries, queries, query_sem).wait()
        stage(0, 0, True, False, False)

    first = step * STEP_BLOCKS
    stage(first + 1, 1, True, True, True)
    stage(first + 2, 0, True, True, True)

    @pl.when(first + STEP_BLOCKS > last)
    def _():
        store(weighted_values(last, 1), last)
        for k in range(parts):
            pltpu.make_async_copy(
                out.at[pl.ds(k * part_rows, part_rows)], out_refs[k], out_sem.at[k]
            ).start()
        for k in range(parts):
            pltpu.make_async_copy(
                out.at[pl.ds(k * part_rows, part_rows)], out_refs[k], out_sem.at[k]
            ).wait()


def attend(head, part, slash, bias, queries, vert, window, part_rows, after):
    parts = part.shape[0]
    group_cols = queries.shape[1] // slash.shape[0]
    group_heads = group_cols // HD
    part_blocks = part_rows // BLK
    rows = group_heads * BLK
    keys_seen = (NV + NS) * BLK
    return pl.pallas_call(
        functools.partial(attend_kernel, head, parts, len(after), part_blocks, group_heads),
        out_shape=[jax.ShapeDtypeStruct((part_rows, group_cols), jnp.bfloat16)] * parts,
        grid_spec=pltpu.PrefetchScalarGridSpec(
            num_scalar_prefetch=2,
            grid=(parts * part_blocks // STEP_BLOCKS,),
            in_specs=[pl.BlockSpec(bias.shape, lambda s, *_: (0, 0))] + [ANY, ANY, VMEM]
            + [ANY] * len(after),
            out_specs=[ANY] * parts,
            scratch_shapes=[
                pltpu.VMEM((parts * part_rows, group_cols), jnp.bfloat16),
                pltpu.VMEM((parts * part_rows, group_cols), jnp.bfloat16),
                pltpu.VMEM((NV * BLK, 2 * HD), jnp.bfloat16),
                pltpu.VMEM((HD, NV * BLK), jnp.bfloat16),
                pltpu.VMEM((rows, keys_seen), jnp.float32),
                pltpu.VMEM((rows, keys_seen), jnp.float32),
                pltpu.VMEM((rows, keys_seen), jnp.bfloat16),
                pltpu.VMEM((rows, keys_seen), jnp.bfloat16),
                pltpu.VMEM((rows, HD), jnp.float32),
                pltpu.VMEM((rows, HD), jnp.float32),
                pltpu.VMEM((BLK, 2 * BLK), jnp.float32),
                pltpu.SemaphoreType.DMA,
                pltpu.SemaphoreType.DMA,
                pltpu.SemaphoreType.DMA((parts,)),
            ],
        ),
        compiler_params=pltpu.CompilerParams(
            dimension_semantics=("arbitrary",), vmem_limit_bytes=18 << 20
        ),
        cost_estimate=pl.CostEstimate(
            flops=4 * parts * part_rows * group_heads * keys_seen * HD,
            bytes_accessed=4 * parts * part_rows * group_cols + 4 * window.shape[0] * HD,
            transcendentals=parts * part_rows * group_heads * keys_seen,
        ),
    )(part, slash, bias, queries, vert, window, *after)


def local(queries, keys, values, vertical, slash):
    shard_count = lax.axis_size("ctx")
    shard_index = lax.axis_index("ctx")
    head_count = lax.axis_size("head")
    head_index = lax.axis_index("head")
    tok_rows = queries.shape[0]
    kv_local = keys.shape[1] // HD
    group_cols = queries.shape[1] // kv_local
    blocks_dev = tok_rows // BLK
    part_rows = tok_rows // head_count
    partner = shard_index ^ 1
    two_pairs = [(i, (i + 2) % shard_count) for i in range(shard_count)]
    across_pairs = [(i, i ^ 1) for i in range(shard_count)]
    parity = (shard_index % 2).reshape(1).astype(jnp.int32)

    owners = vertical // blocks_dev
    order = jnp.arange(NV, dtype=jnp.int32)
    same_owner = owners[:, :, None] == owners[:, None, :]
    earlier = order[None, :] < order[:, None]
    slot_rank = jnp.sum((same_owner & earlier[None]).astype(jnp.int32), axis=2)
    slots = jnp.arange(MOWN, dtype=jnp.int32)
    in_slot = slot_rank[:, :, None] == slots
    local_block = jnp.sum(
        ((owners == shard_index)[:, :, None] & in_slot) * (vertical % blocks_dev)[:, :, None],
        axis=1,
    )
    distances = 2 * jnp.arange(shard_count // 2, dtype=jnp.int32)
    array_owner = jnp.concatenate([shard_index - distances, partner - distances])
    array_owner = jnp.where(array_owner <= shard_index, array_owner, -1)
    here = (array_owner[:, None, None] == owners)[:, :, :, None] & in_slot[None]
    place = jnp.sum(here * (order + 1)[None, None, :, None], axis=2) - 1
    source = jnp.where(owners <= shard_index, 0, -1).astype(jnp.int32)

    slash_rank = jnp.sum((slash[:, None, :] < slash[:, :, None]).astype(jnp.int32), axis=2)
    at_rank = slash_rank[:, :, None] == jnp.arange(NS, dtype=jnp.int32)
    slash = jnp.sum(at_rank * slash[:, :, None], axis=1)

    global_blocks = shard_index * blocks_dev + jnp.arange(blocks_dev, dtype=jnp.int32)
    vert_valid = vertical[:, None, :] < global_blocks[None, :, None]
    slash_blocks = global_blocks[None, :, None] - slash[:, None, :]
    in_vertical = jnp.any(slash_blocks[:, :, :, None] == vertical[:, None, None, :], axis=3)
    slash_valid = (slash[:, None, :] == 0) | ((slash_blocks >= 0) & jnp.logical_not(in_vertical))
    valid = jnp.concatenate([vert_valid, slash_valid], axis=2)
    listed = jnp.arange(NV + NS, dtype=jnp.int32)
    spread = (jnp.arange((NV + NS) * BLK, dtype=jnp.int32) // BLK == listed[:, None])
    barred = jnp.where(valid, 0.0, NEG).reshape(kv_local * blocks_dev, NV + NS)
    bias = jnp.dot(
        barred.astype(jnp.bfloat16), spread.astype(jnp.bfloat16), preferred_element_type=jnp.float32
    )

    steps = shard_count // 2 - 1
    bounds = [k * blocks_dev // steps * BLK for k in range(steps + 1)]
    slot_rows = kv_local * MOWN * BLK
    own, send, slots_own = first_of(bounds[1], local_block, keys, values)
    behind = [(slots_own, 0)]
    across = []
    two_back = []
    one_back = []
    for step in range(steps):
        rows = bounds[step + 1] - bounds[step]
        here = (own, bounds[step])
        if step:
            send = joined(
                parity, [(rows, here, here), (slot_rows, behind[-1], behind[-1])],
                [cross] + one_back[-2:-1],
            )
        come = lax.ppermute(send, "ctx", two_pairs)
        if step == 0:
            across.append((lax.ppermute(slots_own, "ctx", across_pairs), 0))
        two_back.append(come)
        behind.append((come, rows))
        cross = joined(parity, [(rows, here, (come, 0)), (slot_rows, behind[-1], behind[-1])])
        one_back.append(lax.ppermute(cross, "ctx", across_pairs))
        across.append((one_back[-1], rows))
    slots = behind + across
    windows = [(bounds, own, two_back, one_back)]
    after = two_back[-2:-1] + [send]
    for head in range(1, kv_local):
        own = pair_of(head, keys, values, after)
        come = lax.ppermute(own, "ctx", two_pairs)
        windows.append(([0, tok_rows], own, [come], None))
        after = [come]

    out = jnp.zeros((part_rows, head_count * kv_local * group_cols), jnp.bfloat16)
    after = []
    half = head_count // 2
    calls = [[[head_count - 1], list(range(head_count - 2, -1, -1))]] * (kv_local - 1)
    calls.append([[flip] for flip in range(head_count - 1, half - 1, -1)])
    calls[-1].append(list(range(half - 1, -1, -1)))
    vert = listed_blocks(place, source, slots)
    for head in range(kv_local):
        bounds, own, two_back, one_back = windows[head]
        pieces = []
        for arrays in (two_back, one_back):
            for low, high, array in zip(bounds[:-1], bounds[1:], arrays):
                pieces.append((high - low, (array, 0), (array, 0)))
        pieces.append((tok_rows, (own, 0), (own, 0)))
        window = joined(parity, pieces)
        for flips in calls[head]:
            others = [head_index ^ flip for flip in flips]
            pieces = attend(
                head, jnp.stack(others).astype(jnp.int32), slash, bias, queries, vert, window,
                part_rows, after,
            )
            after = [pieces[-1]]
            if flips == calls[head][0] and head + 1 < kv_local:
                near, own_next, (come,), _ = windows[head + 1]
                cross = joined(parity, [(tok_rows, (own_next, 0), (come, 0))], after)
                crossed = lax.ppermute(cross, "ctx", across_pairs)
                windows[head + 1] = (near, own_next, [come], [crossed])
            for flip, other, piece in zip(flips, others, pieces):
                if flip:
                    piece = lax.ppermute(piece, "head", [(i, i ^ flip) for i in range(head_count)])
                out = lax.dynamic_update_slice(
                    out, piece, (0, other * kv_local * group_cols + head * group_cols)
                )
    return out


def solution(mesh):
    in_specs = (
        P("ctx", "head"),
        P("ctx", "head"),
        P("ctx", "head"),
        P("head", None),
        P("head", None),
    )
    out_specs = P(("ctx", "head"), None)
    return jax.shard_map(local, mesh=mesh, in_specs=in_specs, out_specs=out_specs, check_vma=False)
```
